128 devices in a mesh: lon: 32 (over x, z, y_hi), lat: 4 (over y_lo, core).
Axes of the slice: x: 4, y: 4 (y_hi: 2, y_lo: 2; y = y_hi * 2 + y_lo), z: 4, core: 2. Of those that a mesh axis runs over, the one named last changes fastest.
Arguments:
- tokens: bfloat16 [2, 48, 384, 512], P(None, 'lat', 'lon'), may hold values from -6 to 6
- cotangent: bfloat16 [2, 48, 384, 512], P(None, 'lat', 'lon'), may hold values from -6 to 6
- gain_first: float32 [512], replicated, may hold values from 0.5 to 1.5
- gain_second: float32 [512], replicated, may hold values from 0.5 to 1.5
- qkv_first: bfloat16 [512, 1536], replicated, may hold values from -0.25 to 0.25
- qkv_second: bfloat16 [512, 1536], replicated, may hold values from -0.25 to 0.25
- proj_first: bfloat16 [512, 512], replicated, may hold values from -0.25 to 0.25
- proj_second: bfloat16 [512, 512], replicated, may hold values from -0.25 to 0.25
- table_first: float32 [16, 1587], replicated, may hold values from -6 to 250
- table_second: float32 [16, 1587], replicated, may hold values from -6 to 250
- rel_index: int32 [288, 288], replicated, may hold values from 0 to 1586
- regions: int32 [2, 48, 384], P(None, 'lat', 'lon'), may hold values from 0 to 3, as said below
Outputs:
- mixed: bfloat16 [2, 48, 384, 512], P(None, 'lat', 'lon')
- grad_tokens: bfloat16 [2, 48, 384, 512], P(None, 'lat', 'lon')
- grad_gain_first: float32 [512], replicated
- grad_gain_second: float32 [512], replicated
- grad_qkv_first: float32 [512, 1536], replicated
- grad_qkv_second: float32 [512, 1536], replicated
- grad_proj_first: float32 [512, 512], replicated
- grad_proj_second: float32 [512, 512], replicated
- grad_table_first: float32 [16, 1587], replicated
- grad_table_second: float32 [16, 1587], replicated
The draws below stay inside these ranges and needn't reach their ends.
Inputs may be any that keep to these rules, and one draw needn't show every extreme that they name: `regions`: within each window of 12 patch rows and 12 patch columns (all levels), either all patches carry one id, or the last 6 patch rows of the window carry one id and its other patches a different id; windows holding the grid's last 6 patch rows are always split this way. Which windows are split, and the ids, are drawn anew for every window.
All inputs are finite; a program needn't handle non-finite values.
Results may differ from the reference program's by a relative error of at most 0.019.
Values may be sent and summed in bfloat16 or wider, within the bound.
A program may use at most 192 MiB of HBM per device.

```python
import jax
import jax.numpy as jnp
from jax import lax

D = 512
HEADS = 16
WIN = 12
HALF = 6
LEVELS = 2
NLAT = 48
NLON = 384
WT = 288
NB = 1587


def draw_table_first(key, part):
    key = jax.random.fold_in(key, 11)
    return jnp.clip(jax.random.normal(key, (HEADS, NB), jnp.float32), -6.0, 6.0)


def draw_table_second(key, part):
    key = jax.random.fold_in(key, 23)
    return jnp.clip(jax.random.normal(key, (HEADS, NB), jnp.float32), -6.0, 6.0)


def draw_regions(key, part):
    key = jax.random.fold_in(key, 37)
    win_rows = NLAT // WIN
    win_cols = NLON // WIN
    keys = jax.random.split(key, 3)
    inner = jax.random.randint(keys[0], (win_rows, win_cols), 0, 4, jnp.int32)
    offset = jax.random.randint(keys[1], (win_rows, win_cols), 1, 4, jnp.int32)
    split = jax.random.randint(keys[2], (win_rows, win_cols), 0, 2, jnp.int32)
    band = (inner + offset) % 4
    last_inner = inner[win_rows - 1, 0]
    inner = inner.at[win_rows - 1, 0].set(jnp.where(last_inner == 3, 0, last_inner))
    band = band.at[win_rows - 1, 0].set(3)
    inner = inner.at[0, 0].set(0)
    split = split.at[win_rows - 1].set(1)
    inner_full = jnp.repeat(jnp.repeat(inner, WIN, axis=0, total_repeat_length=NLAT), WIN, axis=1, total_repeat_length=NLON)
    band_full = jnp.repeat(jnp.repeat(band, WIN, axis=0, total_repeat_length=NLAT), WIN, axis=1, total_repeat_length=NLON)
    split_full = jnp.repeat(jnp.repeat(split, WIN, axis=0, total_repeat_length=NLAT), WIN, axis=1, total_repeat_length=NLON)
    rows = lax.broadcasted_iota(jnp.int32, (NLAT, NLON), 0)
    lower = rows % WIN >= WIN - HALF
    plane = jnp.where(lower & (split_full == 1), band_full, inner_full).astype(jnp.int32)
    return jnp.broadcast_to(plane[None], (LEVELS, NLAT, NLON)).astype(jnp.int32)


def set_ends(values, key, low, largest):
    shape = values.shape
    index_at = [jax.random.randint(jax.random.fold_in(key, axis), (), 0, shape[axis]) for axis in range(len(shape))]
    values = values.at[tuple(index_at)].set(low)
    longest = shape.index(max(shape))
    index_at[longest] = (index_at[longest] + 1) % shape[longest]
    return values.at[tuple(index_at)].set(largest)


def level_of(rng, shape, pieces, smallest, high):
    factor_of = 1.0
    for position, blocks in pieces:
        draws = jax.random.uniform(jax.random.fold_in(jax.random.fold_in(rng, 6), position), (blocks,), jnp.float32, smallest / len(pieces), high / len(pieces))
        factor_of = factor_of * jnp.repeat(jnp.exp(draws), shape[position] // blocks).reshape((-1,) + (1,) * (len(shape) - 1 - position))
    return factor_of


def normal_values(key, extent, scale, reach, cuts=(), held_as=jnp.bfloat16):
    loudness = level_of(key, extent, cuts, -0.22, 0.18) if cuts else 1.0
    array = jax.random.normal(key, extent, jnp.float32) * scale * loudness
    return jnp.minimum(jnp.maximum(array, -reach), reach).astype(held_as)


def setup_inputs(seed: int = 0) -> dict:
    arg_keys = jax.random.split(jax.random.key(seed), 13)
    tokens = normal_values(arg_keys[0], (LEVELS, NLAT, NLON, D), 1.0, 6.0, ((1, 4), (2, 32)))
    cotangent = normal_values(arg_keys[1], (LEVELS, NLAT, NLON, D), 1.0, 6.0, ((1, 4), (2, 32)))
    gain_first = jnp.clip(1.0 + 0.1 * jax.random.normal(arg_keys[2], (D,), jnp.float32), 0.5, 1.5)
    gain_second = jnp.clip(1.0 + 0.1 * jax.random.normal(arg_keys[3], (D,), jnp.float32), 0.5, 1.5)
    qkv_first = normal_values(arg_keys[4], (D, 3 * D), D ** -0.5, 0.25)
    qkv_second = normal_values(arg_keys[5], (D, 3 * D), D ** -0.5, 0.25)
    proj_first = normal_values(arg_keys[6], (D, D), D ** -0.5, 0.25)
    proj_second = normal_values(arg_keys[7], (D, D), D ** -0.5, 0.25)
    table_first = draw_table_first(jax.random.fold_in(arg_keys[12], 71), 0)
    table_second = draw_table_second(jax.random.fold_in(arg_keys[12], 71), 0)
    rel_index = set_ends(jax.random.randint(arg_keys[10], (WT, WT), 0, NB), jax.random.fold_in(arg_keys[10], 1), 0, NB - 1).astype(jnp.int32)
    regions = draw_regions(jax.random.fold_in(arg_keys[12], 71), 0)
    return dict(tokens=tokens, cotangent=cotangent, gain_first=gain_first, gain_second=gain_second, qkv_first=qkv_first, qkv_second=qkv_second, proj_first=proj_first, proj_second=proj_second, table_first=table_first, table_second=table_second, rel_index=rel_index, regions=regions)


EPS = 1e-05

def norm_rows(values, gain):
    center = lax.optimization_barrier(jnp.mean(values, -1, keepdims=True))
    centred = values - center
    spread = lax.optimization_barrier(jnp.mean(centred * centred, -1, keepdims=True))
    return (centred * lax.rsqrt(spread + EPS) * gain).astype(jnp.bfloat16)

def to_windows(grid):
    levels, rows, cols, width = grid.shape
    parts = grid.reshape(levels, rows // WIN, WIN, cols // WIN, WIN, width)
    parts = parts.transpose(1, 3, 0, 2, 4, 5)
    return parts.reshape(-1, levels * WIN * WIN, width)

def from_windows(blocks, levels, rows, cols):
    width = blocks.shape[-1]
    parts = blocks.reshape(rows // WIN, cols // WIN, levels, WIN, WIN, width)
    return parts.transpose(2, 0, 3, 1, 4, 5).reshape(levels, rows, cols, width)

def window_attention(packed, labels, bias):
    heads = bias.shape[0]
    width = packed.shape[1] // 3
    depth = width // heads
    number = packed.shape[0]
    query = packed[:, :width].astype(jnp.float32).reshape(number, heads, depth)
    keyset = packed[:, width:2 * width].astype(jnp.float32).reshape(number, heads, depth)
    valueset = packed[:, 2 * width:].astype(jnp.float32).reshape(number, heads, depth)
    scores = jnp.einsum('qhd,khd->hqk', query, keyset) * depth ** (-0.5) + bias
    allowed = labels[:, None] == labels[None, :]
    scores = jnp.where(allowed[None], scores, -1e+30)
    highest = lax.optimization_barrier(jnp.max(scores, -1, keepdims=True))
    expo = jnp.exp(scores - highest)
    weights = (expo / lax.optimization_barrier(jnp.sum(expo, -1, keepdims=True))).astype(jnp.bfloat16)
    context = jnp.einsum('hqk,khd->qhd', weights.astype(jnp.float32), valueset)
    return context.reshape(number, width).astype(jnp.bfloat16)

def attend(projected, table, rel_index, labels):
    bias = table[:, rel_index]
    levels, rows, cols, _ = projected.shape
    blocks = to_windows(projected)
    marks = to_windows(labels[..., None])[..., 0]
    single = jax.checkpoint(lambda pair: window_attention(pair[0], pair[1], bias))
    result = lax.map(single, (blocks, marks))
    return from_windows(result, levels, rows, cols)

def block_forward(inputs, gain, qkv_weight, proj_weight, table, rel_index, labels):
    widened = inputs.astype(jnp.float32)
    normed = norm_rows(widened, gain)
    projected = jnp.dot(normed, qkv_weight, preferred_element_type=jnp.float32).astype(jnp.bfloat16)
    context = attend(projected, table, rel_index, labels)
    output = (widened + jnp.dot(context, proj_weight, preferred_element_type=jnp.float32)).astype(jnp.bfloat16)
    return (output, (normed, projected, context))

def block_backward(grad_out, inputs, saved, gain, qkv_weight, proj_weight, table, rel_index, labels):
    normed, projected, context = saved
    width = inputs.shape[-1]
    grad_proj = jnp.dot(context.reshape(-1, width).T, grad_out.reshape(-1, width), preferred_element_type=jnp.float32)
    grad_context = jnp.dot(grad_out, proj_weight.T, preferred_element_type=jnp.float32).astype(jnp.bfloat16)
    _, pull = jax.vjp(lambda p, t: attend(p, t, rel_index, labels), projected, table)
    grad_projected, grad_table = pull(grad_context)
    grad_qkv = jnp.dot(normed.reshape(-1, width).T, grad_projected.reshape(-1, 3 * width), preferred_element_type=jnp.float32)
    grad_normed = jnp.dot(grad_projected, qkv_weight.T, preferred_element_type=jnp.float32).astype(jnp.bfloat16)
    _, pull_norm = jax.vjp(norm_rows, inputs.astype(jnp.float32), gain)
    grad_widened, grad_gain = pull_norm(grad_normed)
    grad_inputs = (grad_widened + grad_out.astype(jnp.float32)).astype(jnp.bfloat16)
    return (grad_inputs, (grad_gain, grad_qkv, grad_proj, grad_table))

def reference(tokens, cotangent, gain_first, gain_second, qkv_first, qkv_second, proj_first, proj_second, table_first, table_second, rel_index, regions):
    plain = jnp.zeros(tokens.shape[:3], jnp.int32)
    first_out, first_saved = block_forward(tokens, gain_first, qkv_first, proj_first, table_first, rel_index, plain)
    shifted = jnp.roll(first_out, (-HALF, -HALF), (1, 2))
    mixed, second_saved = block_forward(shifted, gain_second, qkv_second, proj_second, table_second, rel_index, regions)
    grad_shifted, second_grads = block_backward(cotangent, shifted, second_saved, gain_second, qkv_second, proj_second, table_second, rel_index, regions)
    grad_first_out = jnp.roll(grad_shifted, (HALF, HALF), (1, 2))
    grad_tokens, first_grads = block_backward(grad_first_out, tokens, first_saved, gain_first, qkv_first, proj_first, table_first, rel_index, plain)
    return (mixed, grad_tokens, first_grads[0], second_grads[0], first_grads[1], second_grads[1], first_grads[2], second_grads[2], first_grads[3], second_grads[3])
```

```python
import jax
import jax.numpy as jnp
from jax import lax
from jax.experimental import pallas as pl
from jax.experimental.pallas import tpu as pltpu
from jax.sharding import PartitionSpec as P

F32, BF16, I32 = jnp.float32, jnp.bfloat16, jnp.int32
MESH = pl.DeviceIdType.MESH
D, HEADS, DEPTH, WT, NB = 512, 16, 32, 288, 1587
QUAD, QPAD = 72, 80
PADW, CHUNKS, HIGHS = 384, 13, 7
EPS = 1e-05
LOG2E = 1.4426950408889634
SCALE = DEPTH**-0.5
GROWS, SROWS = 8192, 512
VM = pl.BlockSpec(memory_space=pltpu.VMEM)
SM = pl.BlockSpec(memory_space=pltpu.SMEM)
PARAMS = pltpu.CompilerParams(vmem_limit_bytes=60 << 20)


def quad_row(row_half, col_half, level, row):
    return row_half * 144 + col_half * 72 + level * 36 + row * 6


def dot(a, b):
    return jnp.dot(a, b, preferred_element_type=F32)


def dot_nt(a, b):
    return lax.dot_general(a, b, (((1,), (1,)), ((), ())), preferred_element_type=F32)


def dot_tn(a, b):
    return lax.dot_general(a, b, (((0,), (0,)), ((), ())), preferred_element_type=F32)


def into_quads(src, dst):
    for lev in range(2):
        for r in range(12):
            v = src[lev, r].astype(F32)
            for ch in range(2):
                dst[pl.ds(quad_row(r // 6, ch, lev, r % 6), 6), :] = v[ch * 6 : ch * 6 + 6]


def out_of_quads(src, dst):
    for lev in range(2):
        for r in range(12):
            both = [src[pl.ds(quad_row(r // 6, ch, lev, r % 6), 6), :] for ch in range(2)]
            dst[lev, r] = jnp.concatenate(both, 0).astype(BF16)


def put_quads(value, dst):
    for q in range(4):
        dst[q, :QUAD, :] = value[q * QUAD : (q + 1) * QUAD]
        dst[q, QUAD:, :] = jnp.zeros((QPAD - QUAD, D), dst.dtype)


def get_quads(src):
    return jnp.concatenate([src[q, :QUAD, :].astype(F32) for q in range(4)], 0)


def norm(x):
    xc = x - jnp.mean(x, -1, keepdims=True)
    rstd = lax.rsqrt(jnp.mean(xc * xc, -1, keepdims=True) + EPS)
    return xc * rstd, rstd


def project(h, w_ref, p, pt):
    for n in range(3):
        cols = slice(n * D, n * D + D)
        v = dot(h, w_ref[:, cols])
        p[:, cols] = v.astype(BF16)
        pt[cols, :] = v.T.astype(BF16)


def index_in_quads(rel_ref, rows, highs, lows):
    at = lax.broadcasted_iota(I32, (WT, WT), 0)
    half = (at >= 144).astype(I32)
    rest = at - 144 * half
    col = (rest >= 72).astype(I32)
    rest = rest - 72 * col
    level = (rest >= 36).astype(I32)
    rest = rest - 36 * level
    row = sum((rest >= 6 * k).astype(I32) for k in range(1, 6))
    rest = rest - 6 * row
    natural = level * 144 + (half * 6 + row) * 12 + col * 6 + rest
    perm = (natural == lax.broadcasted_iota(I32, (WT, WT), 1)).astype(F32).astype(BF16)
    rel = rel_ref[...]
    high = (rel >> 8).astype(F32).astype(BF16)
    low = (rel & 255).astype(F32).astype(BF16)

    def moved(part):
        return dot_nt(dot(perm, part).astype(BF16), perm)

    high, low = moved(high), moved(low)
    highs[:, PADW - 128 :] = jnp.zeros((WT, 128), I32)
    lows[:, PADW - 128 :] = jnp.zeros((WT, 128), I32)
    highs[:, :WT] = high.astype(I32)
    lows[:, :WT] = low.astype(I32)


def pack_tables(first_ref, second_ref, packed, step_first, step_second):
    parts = []
    for ref, step_ref in ((first_ref, step_first), (second_ref, step_second)):
        t = ref[...]
        least = jnp.min(t, -1, keepdims=True)
        span = jnp.maximum(jnp.max(t, -1, keepdims=True) - least, 1e-20)
        parts.append(jnp.clip(jnp.floor((t - least) * (65535.0 / span) + 0.5), 0.0, 65535.0).astype(I32))
        step_ref[...] = jnp.broadcast_to(span * (LOG2E / 65535.0), (HEADS, 128))
    packed[:, (CHUNKS - 1) * 128 :] = jnp.zeros((HEADS, 128), I32)
    packed[:, :NB] = (parts[0] << 16) | parts[1]


def gather_bias(packed, highs, lows, bias, start, count):
    @pl.loop(start, start + count)
    def _(r):
        rows = pl.ds(pl.multiple_of(r * 8, 8), 8)
        for ct in range(3):
            lanes = pl.ds(ct * 128, 128)
            high, low = highs[rows, lanes], lows[rows, lanes]
            chunk = high * 2 + (low >> 7)
            lane = low & 127
            masks = [chunk == c for c in range(CHUNKS)]
            for h in range(HEADS):
                acc = None
                for c in range(CHUNKS):
                    row = jnp.broadcast_to(packed[h : h + 1, c * 128 : (c + 1) * 128], (8, 128))
                    found = jnp.take_along_axis(row, lane, axis=1)
                    acc = found if acc is None else jnp.where(masks[c], found, acc)
                bias[h, rows, lanes] = acc


def softmax_head(q, kt, packed, step, high, pen):
    s = dot(q, kt) * (SCALE * LOG2E)
    steps = lax.shift_right_logical(packed, 16) if high else packed & 0xFFFF
    s = s + steps.astype(F32) * step
    if pen is not None:
        s = s + pen
    e = jnp.exp2(s - jnp.max(s, -1, keepdims=True))
    return e * (1.0 / jnp.sum(e, -1, keepdims=True))


def over_heads(p, pt, forward=None, backward=None):
    lanes = lax.broadcasted_iota(I32, (WT, 128), 1) // DEPTH

    @pl.loop(0, 4)
    def _(g):
        g0 = pl.multiple_of(g * 128, 128)
        qg = p[:, pl.ds(g0, 128)]
        kg = p[:, pl.ds(D + g0, 128)]
        vg = p[:, pl.ds(2 * D + g0, 128)]
        ktg = pt[pl.ds(D + g0, 128), :]
        vtg = pt[pl.ds(2 * D + g0, 128), :]
        zero = jnp.zeros_like(qg)
        c_acc = q_acc = None
        if backward is not None:
            dc, dct, a_in, ds_out, dq, dkvt = backward
            dcg = dc[:, pl.ds(g0, 128)]
        for hh in range(4):
            h = g * 4 + hh
            mine = lanes == hh
            if forward is not None:
                bias, steps, high, pen, c, a_out = forward
                a32 = softmax_head(
                    jnp.where(mine, qg, zero),
                    ktg,
                    bias[h, :, :WT],
                    steps[pl.ds(h, 1), 0:1],
                    high,
                    None if pen is None else pen[...],
                )
                a = a32.astype(BF16)
                ch = dot(a, vg)
                c_acc = ch if c_acc is None else jnp.where(mine, ch, c_acc)
                if a_out is not None:
                    a_out[h] = a
            else:
                a = a_in[h]
                a32 = a.astype(F32)
            if backward is not None:
                r0 = pl.multiple_of(g0 + hh * DEPTH, DEPTH)
                da = dot(jnp.where(mine, dcg, zero), vtg)
                ds = a32 * (da - jnp.sum(a32 * da, -1, keepdims=True))
                ds_out[:, h, :WT] = ds
                dsb = ds.astype(BF16)
                dqh = dot(dsb, kg)
                q_acc = dqh if q_acc is None else jnp.where(mine, dqh, q_acc)
                dkvt[pl.ds(r0, DEPTH), :] = (dot(pt[pl.ds(r0, DEPTH), :], dsb) * SCALE).astype(BF16)
                dkvt[pl.ds(D + r0, DEPTH), :] = dot(dct[pl.ds(r0, DEPTH), :], a).astype(BF16)
        if forward is not None:
            c[:, pl.ds(g0, 128)] = c_acc.astype(BF16)
        if backward is not None:
            dq[:, pl.ds(g0, 128)] = (q_acc * SCALE).astype(BF16)


def table_grads(blocks, highs, lows, out):
    out[...] = jnp.zeros_like(out)
    low_of = lax.broadcasted_iota(I32, (256, PADW), 0).astype(F32).astype(BF16)
    one, nil = jnp.ones((256, PADW), BF16), jnp.zeros((256, PADW), BF16)

    @pl.loop(0, WT // 8)
    def _(r):
        rows = pl.ds(pl.multiple_of(r * 8, 8), 8)
        high8 = highs[rows, :].astype(F32).astype(BF16)
        low8 = lows[rows, :].astype(F32).astype(BF16)
        for part in range(2):
            left, right = [], []
            for i in range(part * 4, part * 4 + 4):
                high = jnp.broadcast_to(high8[i : i + 1], (HEADS, PADW))
                low = jnp.broadcast_to(low8[i : i + 1], (256, PADW))
                picked = []
                for block in blocks:
                    ds = block[r * 8 + i].astype(BF16)
                    picked += [jnp.where(high == jnp.array(k, BF16), ds, jnp.zeros_like(ds)) for k in range(HIGHS)]
                left.append(jnp.concatenate(picked, 0))
                right.append(jnp.where(low == low_of, one, nil))
            out[...] += dot_nt(jnp.concatenate(left, 1), jnp.concatenate(right, 1))


def put_columns(value, dst, first):
    for n in range(value.shape[1] // 128):
        at = (first + n) * D
        dst[at : at + D, :] = value[:, n * 128 : (n + 1) * 128].astype(BF16)


def backward_tail(h, xh, rstd, gain, ef, c, e, dq, dkvt, wqkv, grads, g_gain):
    put_columns(dot_tn(h, dq[...]), grads, 0)
    put_columns(dot_nt(h.T, dkvt[...]), grads, 4)
    put_columns(dot_tn(c, e), grads, 12)
    dh = dot_nt(dq[...], wqkv[:, :D]) + dot(wqkv[:, D:], dkvt[...]).T
    dh = dh.astype(BF16).astype(F32)
    g_gain[...] = jnp.sum(dh * xh, 0, keepdims=True)
    dxh = dh * gain
    return rstd * (dxh - jnp.mean(dxh, -1, keepdims=True) - xh * jnp.mean(dxh * xh, -1, keepdims=True)) + ef


def clear_pad(ds):
    ds[:, :, PADW - 128 :] = jnp.zeros((WT, HEADS, 128), F32)


def context_grad(e, wo, dc, dct):
    v = dot_nt(e, wo[...])
    dc[...] = v.astype(BF16)
    dct[...] = v.T.astype(BF16)


def first_forward_kernel(
    tok_ref, gain_ref, wqkv, wo, tab1, tab2, rel_ref,
    y_ref, bias, p, pt, c, a, highs, lows, step1, step2,
    quad, packed,
):
    pack_tables(tab1, tab2, packed, step1, step2)
    index_in_quads(rel_ref, None, highs, lows)
    gather_bias(packed, highs, lows, bias, 0, WT // 8)
    into_quads(tok_ref, quad)
    x = quad[...]
    xh, _ = norm(x)
    project((xh * gain_ref[...]).astype(BF16), wqkv, p, pt)
    over_heads(p, pt, forward=(bias, step1, True, None, c, a))
    put_quads((x + dot(c[...], wo[...])).astype(BF16), y_ref)


def second_kernel(
    z_ref, cot_ref, reg_ref, gain_ref, wqkv, wo, bias, steps,
    mixed_ref, dz_ref, g_gain, grads, ds_out,
    p, pt, c, dc, dct, dq, dkvt, pen, quad,
):
    x = get_quads(z_ref)
    xh, rstd = norm(x)
    h = (xh * gain_ref[...]).astype(BF16)
    project(h, wqkv, p, pt)
    into_quads(cot_ref, quad)
    e = quad[...].astype(BF16)
    context_grad(e, wo, dc, dct)
    split = reg_ref[0, 0, 0] != reg_ref[0, 11, 0]
    lower_row = lax.broadcasted_iota(I32, (WT, WT), 0) >= 144
    lower_col = lax.broadcasted_iota(I32, (WT, WT), 1) >= 144
    pen[...] = jnp.where((lower_row != lower_col) & split, -1e30, 0.0)
    clear_pad(ds_out)
    over_heads(p, pt, (bias, steps, False, pen, c, None), (dc, dct, None, ds_out, dq, dkvt))
    cv = c[...]
    quad[...] = x + dot(cv, wo[...])
    out_of_quads(quad, mixed_ref)
    dz = backward_tail(h, xh, rstd, gain_ref[...], e.astype(F32), cv, e, dq, dkvt, wqkv, grads, g_gain)
    put_quads(dz.astype(BF16), dz_ref)


def first_backward_kernel(
    tok_ref, dy_ref, gain_ref, wqkv, wo, p, pt, c, a, ds2, highs, lows, gain2,
    gt_ref, grads, small,
    dc, dct, dq, dkvt, ds1, quad, sums, g_gain,
):
    into_quads(tok_ref, quad)
    xh, rstd = norm(quad[...])
    h = (xh * gain_ref[...]).astype(BF16)
    ef = get_quads(dy_ref)
    e = ef.astype(BF16)
    context_grad(e, wo, dc, dct)
    clear_pad(ds1)
    over_heads(p, pt, None, (dc, dct, a, ds1, dq, dkvt))
    quad[...] = backward_tail(h, xh, rstd, gain_ref[...], ef, c[...], e, dq, dkvt, wqkv, grads, g_gain)
    out_of_quads(quad, gt_ref)
    table_grads((ds1, ds2), highs, lows, sums)
    small[:224, :] = sums[:, :128].astype(BF16)
    small[224:448, :] = sums[:, 128:].astype(BF16)
    gains = [g[:, n * 128 : (n + 1) * 128] for g in (g_gain, gain2) for n in range(4)]
    gains.append(jnp.zeros((SROWS - 456, 128), F32))
    small[448:, :] = jnp.concatenate(gains, 0).astype(BF16)


def place():
    lon, lat = lax.axis_index("lon"), lax.axis_index("lat")
    x, z, y = lon // 8, (lon // 2) % 4, (lon % 2) * 2 + lat // 2
    return x, y, z, lat % 2


def device(x, y, z, core):
    return {"lon": x * 8 + z * 2 + y // 2, "lat": (y % 2) * 2 + core}


def greet(to):
    barrier = pltpu.get_barrier_semaphore()
    for dev in to:
        pl.semaphore_signal(barrier, inc=1, device_id=dev, device_id_type=MESH)
    pl.semaphore_wait(barrier, len(to))


def shift_kernel(by, src, dst, send, recv, own):
    lon, lat = lax.axis_index("lon"), lax.axis_index("lat")

    def near(step, along_lon, along_lat):
        return {
            "lon": (lon + step * along_lon + 32) % 32,
            "lat": (lat + step * along_lat + 4) % 4,
        }

    moves = [(2, 1, 1, 0), (1, 2, 0, 1), (0, 3, 1, 1)]
    greet([near(-by, m[2], m[3]) for m in moves])
    copies = []
    for n, (here, there, along_lon, along_lat) in enumerate(moves):
        a, b = (here, there) if by < 0 else (there, here)
        copies.append(
            pltpu.make_async_remote_copy(
                src_ref=src.at[a], dst_ref=dst.at[b], send_sem=send.at[n], recv_sem=recv.at[n],
                device_id=near(by, along_lon, along_lat), device_id_type=MESH,
            )
        )
    a, b = (3, 0) if by < 0 else (0, 3)
    for copy in copies:
        copy.start()
    local = pltpu.make_async_copy(src.at[a], dst.at[b], own)
    local.start()
    local.wait()
    for copy in copies:
        copy.wait()


class Job:
    def __init__(self, units, refs, sems, where):
        self.src, self.out, self.r0, self.a, self.r1, self.b, self.r2, self.c4 = refs
        self.send, self.recv = sems
        self.half = self.src.shape[0] // 2
        self.where = where
        self.sets = []
        at = 0
        for n, count in enumerate(units):
            self.sets.append((at, count * 256, (n % 3, (n + 1) % 3, (n + 2) % 3)))
            at += count * 256
        self.live = []

    def peer(self, axis, d):
        to = list(self.where)
        to[axis] = (to[axis] + d) % 4
        return device(*to)

    def copy(self, src, dst, sem, to):
        made = pltpu.make_async_remote_copy(
            src_ref=src, dst_ref=dst, send_sem=self.send.at[sem], recv_sem=self.recv.at[sem],
            device_id=to, device_id_type=MESH,
        )
        made.start()
        self.live.append(made)

    def wait(self):
        for made in self.live:
            made.wait()
        self.live = []

    def other(self):
        x, y, z, core = self.where
        return device(x, y, z, 1 - core)

    def mine(self):
        return pl.multiple_of(self.where[3] * self.half, 128)

    def add(self, dst, dst_at, parts, rows):
        step = 256 if rows % 256 == 0 else rows

        @pl.loop(0, rows // step)
        def _(n):
            total = None
            for ref, lead, at in parts:
                where = pl.ds(pl.multiple_of(at + n * step, 16), step)
                v = (ref[where, :] if lead is None else ref[lead, where, :]).astype(F32)
                total = v if total is None else total + v
            dst[pl.ds(pl.multiple_of(dst_at + n * step, 16), step), :] = total.astype(BF16)

    def stage(self, n):
        if n == 0:
            theirs = pl.multiple_of((1 - self.where[3]) * self.half, 128)
            self.copy(self.src.at[pl.ds(theirs, self.half)], self.r0, 0, self.other())
        if n == 1:
            self.wait()
            self.add(self.a, 0, [(self.src, None, self.mine()), (self.r0, None, 0)], self.half)
            for k, (at, rows, axes) in enumerate(self.sets):
                me = self.where[axes[0]]
                for d in range(1, 4):
                    piece = pl.multiple_of(at + (me + d) % 4 * (rows // 4), 16)
                    self.copy(
                        self.a.at[pl.ds(piece, rows // 4)], self.r1.at[d - 1, pl.ds(at // 4, rows // 4)],
                        1 + k * 3 + d - 1, self.peer(axes[0], d),
                    )
        if n == 2:
            self.wait()
            for k, (at, rows, axes) in enumerate(self.sets):
                own = at + self.where[axes[0]] * (rows // 4)
                self.add(
                    self.b, at // 4, [(self.a, None, own)] + [(self.r1, d, at // 4) for d in range(3)], rows // 4
                )
                me = self.where[axes[1]]
                for d in range(1, 4):
                    piece = pl.multiple_of(at // 4 + (me + d) % 4 * (rows // 16), 16)
                    self.copy(
                        self.b.at[pl.ds(piece, rows // 16)], self.r2.at[d - 1, pl.ds(at // 16, rows // 16)],
                        10 + k * 3 + d - 1, self.peer(axes[1], d),
                    )
        if n == 3:
            self.wait()
            for k, (at, rows, axes) in enumerate(self.sets):
                own = at // 4 + self.where[axes[1]] * (rows // 16)
                me = self.where[axes[2]]
                small = pl.ds(at // 16, rows // 16)
                total = self.b[pl.ds(pl.multiple_of(own, 16), rows // 16), :].astype(F32)
                for d in range(3):
                    total = total + self.r2[d, small, :].astype(F32)
                self.c4[me, small, :] = total.astype(BF16)
                for d in range(1, 4):
                    self.copy(
                        self.c4.at[me, small], self.c4.at[me, small],
                        19 + k * 3 + d - 1, self.peer(axes[2], d),
                    )
        if n == 4:
            self.wait()
            for k, (at, rows, axes) in enumerate(self.sets):
                small = pl.ds(at // 16, rows // 16)
                total = self.c4[0, small, :].astype(F32)
                for d in range(1, 4):
                    total = total + self.c4[d, small, :].astype(F32)
                here = self.mine() + at + self.where[axes[0]] * (rows // 4) + self.where[axes[1]] * (rows // 16)
                spot = pl.ds(pl.multiple_of(here, 16), rows // 16)
                self.out[spot, :] = total.astype(BF16)
                for d in range(1, 4):
                    self.copy(self.out.at[spot], self.out.at[spot], 28 + k * 3 + d - 1, self.peer(axes[1], d))
        if n == 5:
            self.wait()
            for k, (at, rows, axes) in enumerate(self.sets):
                here = self.mine() + at + self.where[axes[0]] * (rows // 4)
                spot = pl.ds(pl.multiple_of(here, 16), rows // 4)
                for d in range(1, 4):
                    self.copy(self.out.at[spot], self.out.at[spot], 37 + k * 3 + d - 1, self.peer(axes[0], d))
        if n == 6:
            self.wait()
            spot = pl.ds(self.mine(), self.half)
            self.copy(self.out.at[spot], self.out.at[spot], 46, self.other())
        if n == 7:
            self.wait()


STAGES = 8
BIG, LITTLE = (6, 5, 5), (1,)


def job_scratch(rows):
    half = rows // 2
    return [
        pltpu.VMEM((half, 128), BF16),
        pltpu.VMEM((half, 128), BF16),
        pltpu.VMEM((3, half // 4, 128), BF16),
        pltpu.VMEM((half // 4, 128), BF16),
        pltpu.VMEM((3, half // 16, 128), BF16),
        pltpu.VMEM((4, half // 16, 128), BF16),
        pltpu.SemaphoreType.DMA((47,)),
        pltpu.SemaphoreType.DMA((47,)),
    ]


def all_peers(where):
    x, y, z, core = where
    to = [device(x, y, z, 1 - core)]
    for axis in range(3):
        for d in range(1, 4):
            at = list(where)
            at[axis] = (at[axis] + d) % 4
            to.append(device(*at))
    return to


def sum_kernel(g2, g1, s, o2, o1, os, *scratch):
    where = place()
    greet(all_peers(where))
    jobs = []
    for n, (units, src, out) in enumerate(((BIG, g2, o2), (BIG, g1, o1), (LITTLE, s, os))):
        mem = scratch[n * 8 : n * 8 + 8]
        jobs.append(Job(units, (src, out) + mem[:6], mem[6:], where))
    for stage in range(STAGES):
        for job in jobs:
            job.stage(stage)


def widen_kernel(s2, s1, small, gq1, gq2, gp1, gp2, gg1, gg2, gt1, gt2):
    for src, gq, gp in ((s1, gq1, gp1), (s2, gq2, gp2)):
        for n in range(12):
            gq[:, n * 128 : (n + 1) * 128] = src[n * D : (n + 1) * D, :].astype(F32)
        for n in range(4):
            gp[:, n * 128 : (n + 1) * 128] = src[(12 + n) * D : (13 + n) * D, :].astype(F32)
    tail = small[448:464, :].astype(F32)
    for b, (gg, gt) in enumerate(((gg1, gt1), (gg2, gt2))):
        for n in range(4):
            gg[:, n * 128 : (n + 1) * 128] = tail[b * 4 + n : b * 4 + n + 1]
        for k in range(2 * HIGHS):
            at = (b * HIGHS + k // 2) * 16 + (k % 2) * 224
            width = min(128, NB - k * 128)
            if width > 0:
                gt[:, k * 128 : k * 128 + width] = small[at : at + 16, :width].astype(F32)


def on_device(
    tokens, cotangent, gain_first, gain_second, qkv_first, qkv_second, proj_first, proj_second,
    table_first, table_second, rel_index, regions,
):
    def arr(shape, dtype=BF16):
        return jax.ShapeDtypeStruct(shape, dtype)

    def mem(*shape, dtype=BF16):
        return pltpu.VMEM(shape, dtype)

    gain_first, gain_second = gain_first.reshape(1, D), gain_second.reshape(1, D)
    grid = arr((2, 12, 12, D))
    quads = arr((4, QPAD, D))
    y, bias, p, pt, c, a, highs, lows, step1, step2 = pl.pallas_call(
        first_forward_kernel,
        out_shape=[
            quads, arr((HEADS, WT, PADW), I32), arr((WT, 3 * D)), arr((3 * D, WT)), arr((WT, D)),
            arr((HEADS, WT, WT)), arr((WT, PADW), I32), arr((WT, PADW), I32),
            arr((HEADS, 128), F32), arr((HEADS, 128), F32),
        ],
        in_specs=[VM] * 7, out_specs=[VM] * 10,
        scratch_shapes=[mem(WT, D, dtype=F32), mem(HEADS, CHUNKS * 128, dtype=I32)],
        compiler_params=PARAMS,
        name="first_forward",
    )(tokens, gain_first, qkv_first, proj_first, table_first, table_second, rel_index)

    def shifted(value, by):
        return pl.pallas_call(
            lambda *refs: shift_kernel(by, *refs),
            out_shape=quads, in_specs=[VM], out_specs=VM,
            scratch_shapes=[pltpu.SemaphoreType.DMA((3,)), pltpu.SemaphoreType.DMA((3,)), pltpu.SemaphoreType.DMA(())],
            compiler_params=pltpu.CompilerParams(collective_id=2 + by, has_side_effects=True),
            name="shift_on" if by < 0 else "shift_back",
        )(value)

    work = [mem(WT, D), mem(D, WT), mem(WT, D), mem(2 * D, WT)]
    mixed, dz, gain2, grads2, ds2 = pl.pallas_call(
        second_kernel,
        out_shape=[grid, quads, arr((1, D), F32), arr((GROWS, 128)), arr((WT, HEADS, PADW), F32)],
        in_specs=[VM, VM, SM] + [VM] * 5, out_specs=[VM] * 5,
        scratch_shapes=[mem(WT, 3 * D), mem(3 * D, WT), mem(WT, D)] + work
        + [mem(WT, WT, dtype=F32), mem(WT, D, dtype=F32)],
        compiler_params=PARAMS,
        name="second_block",
    )(shifted(y, -1), cotangent, regions, gain_second, qkv_second, proj_second, bias, step2)
    grad_tokens, grads1, small = pl.pallas_call(
        first_backward_kernel,
        out_shape=[grid, arr((GROWS, 128)), arr((SROWS, 128))],
        in_specs=[VM] * 13, out_specs=[VM] * 3,
        scratch_shapes=work + [
            mem(WT, HEADS, PADW, dtype=F32), mem(WT, D, dtype=F32), mem(224, 256, dtype=F32), mem(1, D, dtype=F32),
        ],
        compiler_params=PARAMS,
        name="first_backward",
    )(tokens, shifted(dz, 1), gain_first, qkv_first, proj_first, p, pt, c, a, ds2, highs, lows, gain2)
    s2, s1, ss = pl.pallas_call(
        sum_kernel,
        out_shape=[arr((GROWS, 128)), arr((GROWS, 128)), arr((SROWS, 128))],
        in_specs=[VM] * 3, out_specs=[VM] * 3,
        scratch_shapes=job_scratch(GROWS) + job_scratch(GROWS) + job_scratch(SROWS),
        compiler_params=pltpu.CompilerParams(vmem_limit_bytes=60 << 20, collective_id=5, has_side_effects=True),
        name="sum_grads",
    )(grads2, grads1, small)
    gq1, gq2, gp1, gp2, gg1, gg2, gt1, gt2 = pl.pallas_call(
        widen_kernel,
        out_shape=[
            arr((D, 3 * D), F32), arr((D, 3 * D), F32), arr((D, D), F32), arr((D, D), F32),
            arr((1, D), F32), arr((1, D), F32), arr((HEADS, NB), F32), arr((HEADS, NB), F32),
        ],
        in_specs=[VM] * 3, out_specs=[VM] * 8,
        compiler_params=PARAMS,
        name="widen_grads",
    )(s2, s1, ss)
    return mixed, grad_tokens, gg1.reshape(D), gg2.reshape(D), gq1, gq2, gp1, gp2, gt1, gt2


def solution(mesh):
    grid = P(None, "lat", "lon", None)
    return jax.shard_map(
        on_device,
        mesh=mesh,
        in_specs=(grid, grid) + (P(),) * 9 + (P(None, "lat", "lon"),),
        out_specs=(grid, grid) + (P(),) * 8,
        check_vma=False,
    )
```

```python
import jax
import jax.numpy as jnp
from jax import lax
from jax.experimental import pallas as pl
from jax.experimental.pallas import tpu as pltpu
from jax.sharding import PartitionSpec as P

F32, BF16, I32 = jnp.float32, jnp.bfloat16, jnp.int32
MESH = pl.DeviceIdType.MESH
D, HEADS, DEPTH, WT, NB = 512, 16, 32, 288, 1587
QUAD, QPAD = 72, 80
PADW, CHUNKS, HIGHS = 384, 13, 7
EPS = 1e-05
LOG2E = 1.4426950408889634
SCALE = DEPTH**-0.5
GROWS, SROWS = 8192, 512
VM = pl.BlockSpec(memory_space=pltpu.VMEM)
SM = pl.BlockSpec(memory_space=pltpu.SMEM)
PARAMS = pltpu.CompilerParams(vmem_limit_bytes=60 << 20)


def quad_row(row_half, col_half, level, row):
    return row_half * 144 + col_half * 72 + level * 36 + row * 6


def dot(a, b):
    return jnp.dot(a, b, preferred_element_type=F32)


def dot_nt(a, b):
    return lax.dot_general(a, b, (((1,), (1,)), ((), ())), preferred_element_type=F32)


def dot_tn(a, b):
    return lax.dot_general(a, b, (((0,), (0,)), ((), ())), preferred_element_type=F32)


def into_quads(src, dst):
    for lev in range(2):
        for r in range(12):
            v = src[lev, r].astype(F32)
            for ch in range(2):
                dst[pl.ds(quad_row(r // 6, ch, lev, r % 6), 6), :] = v[ch * 6 : ch * 6 + 6]


def out_of_quads(src, dst):
    for lev in range(2):
        for r in range(12):
            both = [src[pl.ds(quad_row(r // 6, ch, lev, r % 6), 6), :] for ch in range(2)]
            dst[lev, r] = jnp.concatenate(both, 0).astype(BF16)


def put_quads(value, dst):
    for q in range(4):
        dst[q, :QUAD, :] = value[q * QUAD : (q + 1) * QUAD]
        dst[q, QUAD:, :] = jnp.zeros((QPAD - QUAD, D), dst.dtype)


def get_quads(src):
    return jnp.concatenate([src[q, :QUAD, :].astype(F32) for q in range(4)], 0)


def norm(x):
    xc = x - jnp.mean(x, -1, keepdims=True)
    rstd = lax.rsqrt(jnp.mean(xc * xc, -1, keepdims=True) + EPS)
    return xc * rstd, rstd


def project(h, w_ref, p, pt):
    for n in range(3):
        cols = slice(n * D, n * D + D)
        v = dot(h, w_ref[:, cols])
        p[:, cols] = v.astype(BF16)
        pt[cols, :] = v.T.astype(BF16)


def index_in_quads(rel_ref, highs, lows):
    at = lax.broadcasted_iota(I32, (WT, WT), 0)
    half = (at >= 144).astype(I32)
    rest = at - 144 * half
    col = (rest >= 72).astype(I32)
    rest = rest - 72 * col
    level = (rest >= 36).astype(I32)
    rest = rest - 36 * level
    row = sum((rest >= 6 * k).astype(I32) for k in range(1, 6))
    rest = rest - 6 * row
    natural = level * 144 + (half * 6 + row) * 12 + col * 6 + rest
    perm = (natural == lax.broadcasted_iota(I32, (WT, WT), 1)).astype(F32).astype(BF16)
    rel = rel_ref[...]
    high = (rel >> 8).astype(F32).astype(BF16)
    low = (rel & 255).astype(F32).astype(BF16)

    def moved(part):
        return dot_nt(dot(perm, part).astype(BF16), perm)

    high, low = moved(high), moved(low)
    highs[:, PADW - 128 :] = jnp.zeros((WT, 128), I32)
    lows[:, PADW - 128 :] = jnp.zeros((WT, 128), I32)
    highs[:, :WT] = high.astype(I32)
    lows[:, :WT] = low.astype(I32)


def pack_tables(first_ref, second_ref, packed, step_first, step_second):
    parts = []
    for ref, step_ref in ((first_ref, step_first), (second_ref, step_second)):
        t = ref[...]
        least = jnp.min(t, -1, keepdims=True)
        span = jnp.maximum(jnp.max(t, -1, keepdims=True) - least, 1e-20)
        parts.append(jnp.clip(jnp.floor((t - least) * (65535.0 / span) + 0.5), 0.0, 65535.0).astype(I32))
        step_ref[...] = jnp.broadcast_to(span * (LOG2E / 65535.0), (HEADS, 128))
    packed[:, (CHUNKS - 1) * 128 :] = jnp.zeros((HEADS, 128), I32)
    packed[:, :NB] = (parts[0] << 16) | parts[1]


def gather_bias(packed, highs, lows, bias, start, count):
    @pl.loop(start, start + count)
    def _(r):
        rows = pl.ds(pl.multiple_of(r * 8, 8), 8)
        for ct in range(3):
            lanes = pl.ds(ct * 128, 128)
            high, low = highs[rows, lanes], lows[rows, lanes]
            chunk = high * 2 + (low >> 7)
            lane = low & 127
            masks = [chunk == c for c in range(CHUNKS)]
            for h in range(HEADS):
                acc = None
                for c in range(CHUNKS):
                    row = jnp.broadcast_to(packed[h : h + 1, c * 128 : (c + 1) * 128], (8, 128))
                    found = jnp.take_along_axis(row, lane, axis=1)
                    acc = found if acc is None else jnp.where(masks[c], found, acc)
                bias[h, rows, lanes] = acc


def softmax_head(q, kt, packed, step, high, pen):
    s = dot(q, kt) * (SCALE * LOG2E)
    steps = lax.shift_right_logical(packed, 16) if high else packed & 0xFFFF
    s = s + steps.astype(F32) * step
    if pen is not None:
        s = s + pen
    e = jnp.exp2(s - jnp.max(s, -1, keepdims=True))
    return e * (1.0 / jnp.sum(e, -1, keepdims=True))


def over_heads(p, pt, forward=None, backward=None, groups=(0, 4)):
    lanes = lax.broadcasted_iota(I32, (WT, 128), 1) // DEPTH

    @pl.loop(*groups)
    def _(g):
        g0 = pl.multiple_of(g * 128, 128)
        qg = p[:, pl.ds(g0, 128)]
        kg = p[:, pl.ds(D + g0, 128)]
        vg = p[:, pl.ds(2 * D + g0, 128)]
        ktg = pt[pl.ds(D + g0, 128), :]
        vtg = pt[pl.ds(2 * D + g0, 128), :]
        zero = jnp.zeros_like(qg)
        c_acc = q_acc = None
        if backward is not None:
            dc, dct, a_in, ds_out, dq, dkvt = backward
            dcg = dc[:, pl.ds(g0, 128)]
        for hh in range(4):
            h = g * 4 + hh
            mine = lanes == hh
            if forward is not None:
                bias, steps, high, pen, c, a_out = forward
                a32 = softmax_head(
                    jnp.where(mine, qg, zero),
                    ktg,
                    bias[h, :, :WT],
                    steps[pl.ds(h, 1), 0:1],
                    high,
                    None if pen is None else pen[...],
                )
                a = a32.astype(BF16)
                ch = dot(a, vg)
                c_acc = ch if c_acc is None else jnp.where(mine, ch, c_acc)
                if a_out is not None:
                    a_out[h] = a
            else:
                a = a_in[h]
                a32 = a.astype(F32)
            if backward is not None:
                r0 = pl.multiple_of(g0 + hh * DEPTH, DEPTH)
                da = dot(jnp.where(mine, dcg, zero), vtg)
                ds = a32 * (da - jnp.sum(a32 * da, -1, keepdims=True))
                ds_out[:, h, :WT] = ds
                dsb = ds.astype(BF16)
                dqh = dot(dsb, kg)
                q_acc = dqh if q_acc is None else jnp.where(mine, dqh, q_acc)
                dkvt[pl.ds(r0, DEPTH), :] = (dot(pt[pl.ds(r0, DEPTH), :], dsb) * SCALE).astype(BF16)
                dkvt[pl.ds(D + r0, DEPTH), :] = dot(dct[pl.ds(r0, DEPTH), :], a).astype(BF16)
        if forward is not None:
            c[:, pl.ds(g0, 128)] = c_acc.astype(BF16)
        if backward is not None:
            dq[:, pl.ds(g0, 128)] = (q_acc * SCALE).astype(BF16)


def table_grads(blocks, highs, lows, out, start, stop):
    low_of = lax.broadcasted_iota(I32, (256, PADW), 0).astype(F32).astype(BF16)
    one, nil = jnp.ones((256, PADW), BF16), jnp.zeros((256, PADW), BF16)

    @pl.loop(start, stop)
    def _(r):
        rows = pl.ds(pl.multiple_of(r * 8, 8), 8)
        high8 = highs[rows, :].astype(F32).astype(BF16)
        low8 = lows[rows, :].astype(F32).astype(BF16)
        for part in range(2):
            left, right = [], []
            for i in range(part * 4, part * 4 + 4):
                high = jnp.broadcast_to(high8[i : i + 1], (HEADS, PADW))
                low = jnp.broadcast_to(low8[i : i + 1], (256, PADW))
                picked = []
                for block in blocks:
                    ds = block[r * 8 + i].astype(BF16)
                    picked += [jnp.where(high == jnp.array(k, BF16), ds, jnp.zeros_like(ds)) for k in range(HIGHS)]
                left.append(jnp.concatenate(picked, 0))
                right.append(jnp.where(low == low_of, one, nil))
            out[...] += dot_nt(jnp.concatenate(left, 1), jnp.concatenate(right, 1))


def put_columns(value, dst, first):
    for n in range(value.shape[1] // 128):
        at = (first + n) * D
        dst[at : at + D, :] = value[:, n * 128 : (n + 1) * 128].astype(BF16)


def weight_grads(h, c, e, dq, dkvt, grads):
    put_columns(dot_tn(h, dq[...]), grads, 0)
    put_columns(dot_nt(h.T, dkvt[...]), grads, 4)
    put_columns(dot_tn(c[...], e), grads, 12)


def input_grad(xh, rstd, gain, ef, dq, dkvt, wqkv, g_gain):
    dh = dot_nt(dq[...], wqkv[:, :D]) + dot(wqkv[:, D:], dkvt[...]).T
    dh = dh.astype(BF16).astype(F32)
    g_gain[...] = jnp.sum(dh * xh, 0, keepdims=True)
    dxh = dh * gain
    return rstd * (dxh - jnp.mean(dxh, -1, keepdims=True) - xh * jnp.mean(dxh * xh, -1, keepdims=True)) + ef


def clear_pad(ds):
    ds[:, :, PADW - 128 :] = jnp.zeros((WT, HEADS, 128), F32)


def context_grad(e, wo, dc, dct):
    v = dot_nt(e, wo[...])
    dc[...] = v.astype(BF16)
    dct[...] = v.T.astype(BF16)


def place():
    lon, lat = lax.axis_index("lon"), lax.axis_index("lat")
    x, z, y = lon // 8, (lon // 2) % 4, (lon % 2) * 2 + lat // 2
    return x, y, z, lat % 2


def device(x, y, z, core):
    return {"lon": x * 8 + z * 2 + y // 2, "lat": (y % 2) * 2 + core}


def near(step, along_lon, along_lat):
    return {
        "lon": (lax.axis_index("lon") + step * along_lon + 32) % 32,
        "lat": (lax.axis_index("lat") + step * along_lat + 4) % 4,
    }


MOVES = ((2, 1, 1, 0), (1, 2, 0, 1), (0, 3, 1, 1))


def shift(by, src, dst, send, recv):
    copies = []
    for n, (here, there, along_lon, along_lat) in enumerate(MOVES):
        a, b = (here, there) if by < 0 else (there, here)
        copies.append(
            pltpu.make_async_remote_copy(
                src_ref=src.at[a], dst_ref=dst.at[b], send_sem=send.at[n], recv_sem=recv.at[n],
                device_id=near(by, along_lon, along_lat), device_id_type=MESH,
            )
        )
        copies[-1].start()
    a, b = (3, 0) if by < 0 else (0, 3)
    dst[b] = src[a]
    return copies


class Job:
    def __init__(self, units, refs, sems, where):
        self.src, self.out, self.r0, self.a, self.r1, self.b, self.r2, self.c4 = refs
        self.send, self.recv = sems
        self.half = self.src.shape[0] // 2
        self.where = where
        self.sets = []
        at = 0
        for n, count in enumerate(units):
            self.sets.append((at, count * 256, (n % 3, (n + 1) % 3, (n + 2) % 3)))
            at += count * 256
        self.live = []

    def peer(self, axis, d):
        to = list(self.where)
        to[axis] = (to[axis] + d) % 4
        return device(*to)

    def copy(self, src, dst, sem, to):
        made = pltpu.make_async_remote_copy(
            src_ref=src, dst_ref=dst, send_sem=self.send.at[sem], recv_sem=self.recv.at[sem],
            device_id=to, device_id_type=MESH,
        )
        made.start()
        self.live.append(made)

    def wait(self):
        for made in self.live:
            made.wait()
        self.live = []

    def other(self):
        x, y, z, core = self.where
        return device(x, y, z, 1 - core)

    def mine(self):
        return pl.multiple_of(self.where[3] * self.half, 128)

    def add(self, dst, dst_at, parts, rows):
        step = 256 if rows % 256 == 0 else rows

        @pl.loop(0, rows // step)
        def _(n):
            total = None
            for ref, lead, at in parts:
                where = pl.ds(pl.multiple_of(at + n * step, 16), step)
                v = (ref[where, :] if lead is None else ref[lead, where, :]).astype(F32)
                total = v if total is None else total + v
            dst[pl.ds(pl.multiple_of(dst_at + n * step, 16), step), :] = total.astype(BF16)

    def stage(self, n):
        if n == 0:
            theirs = pl.multiple_of((1 - self.where[3]) * self.half, 128)
            self.copy(self.src.at[pl.ds(theirs, self.half)], self.r0, 0, self.other())
        if n == 1:
            self.wait()
            self.add(self.a, 0, [(self.src, None, self.mine()), (self.r0, None, 0)], self.half)
            for k, (at, rows, axes) in enumerate(self.sets):
                me = self.where[axes[0]]
                for d in range(1, 4):
                    piece = pl.multiple_of(at + (me + d) % 4 * (rows // 4), 16)
                    self.copy(
                        self.a.at[pl.ds(piece, rows // 4)], self.r1.at[d - 1, pl.ds(at // 4, rows // 4)],
                        1 + k * 3 + d - 1, self.peer(axes[0], d),
                    )
        if n == 2:
            self.wait()
            for k, (at, rows, axes) in enumerate(self.sets):
                own = at + self.where[axes[0]] * (rows // 4)
                self.add(
                    self.b, at // 4, [(self.a, None, own)] + [(self.r1, d, at // 4) for d in range(3)], rows // 4
                )
                me = self.where[axes[1]]
                for d in range(1, 4):
                    piece = pl.multiple_of(at // 4 + (me + d) % 4 * (rows // 16), 16)
                    self.copy(
                        self.b.at[pl.ds(piece, rows // 16)], self.r2.at[d - 1, pl.ds(at // 16, rows // 16)],
                        10 + k * 3 + d - 1, self.peer(axes[1], d),
                    )
        if n == 3:
            self.wait()
            for k, (at, rows, axes) in enumerate(self.sets):
                own = at // 4 + self.where[axes[1]] * (rows // 16)
                me = self.where[axes[2]]
                small = pl.ds(at // 16, rows // 16)
                total = self.b[pl.ds(pl.multiple_of(own, 16), rows // 16), :].astype(F32)
                for d in range(3):
                    total = total + self.r2[d, small, :].astype(F32)
                self.c4[me, small, :] = total.astype(BF16)
                for d in range(1, 4):
                    self.copy(
                        self.c4.at[me, small], self.c4.at[me, small],
                        19 + k * 3 + d - 1, self.peer(axes[2], d),
                    )
        if n == 4:
            self.wait()
            for k, (at, rows, axes) in enumerate(self.sets):
                small = pl.ds(at // 16, rows // 16)
                total = self.c4[0, small, :].astype(F32)
                for d in range(1, 4):
                    total = total + self.c4[d, small, :].astype(F32)
                here = self.mine() + at + self.where[axes[0]] * (rows // 4) + self.where[axes[1]] * (rows // 16)
                spot = pl.ds(pl.multiple_of(here, 16), rows // 16)
                self.out[spot, :] = total.astype(BF16)
                for d in range(1, 4):
                    self.copy(self.out.at[spot], self.out.at[spot], 28 + k * 3 + d - 1, self.peer(axes[1], d))
        if n == 5:
            self.wait()
            for k, (at, rows, axes) in enumerate(self.sets):
                here = self.mine() + at + self.where[axes[0]] * (rows // 4)
                spot = pl.ds(pl.multiple_of(here, 16), rows // 4)
                for d in range(1, 4):
                    self.copy(self.out.at[spot], self.out.at[spot], 37 + k * 3 + d - 1, self.peer(axes[0], d))
        if n == 6:
            self.wait()
            spot = pl.ds(self.mine(), self.half)
            self.copy(self.out.at[spot], self.out.at[spot], 46, self.other())
        if n == 7:
            self.wait()


STAGES = 8
BIG, LITTLE = (6, 5, 5), (1,)


def job_scratch(rows):
    half = rows // 2
    return [
        pltpu.VMEM((half, 128), BF16),
        pltpu.VMEM((half, 128), BF16),
        pltpu.VMEM((3, half // 4, 128), BF16),
        pltpu.VMEM((half // 4, 128), BF16),
        pltpu.VMEM((3, half // 16, 128), BF16),
        pltpu.VMEM((4, half // 16, 128), BF16),
        pltpu.SemaphoreType.DMA((47,)),
        pltpu.SemaphoreType.DMA((47,)),
    ]


def all_peers(where):
    x, y, z, core = where
    to = [device(x, y, z, 1 - core)]
    for axis in range(3):
        for d in range(1, 4):
            at = list(where)
            at[axis] = (at[axis] + d) % 4
            to.append(device(*at))
    return to


def kernel(
    tok_ref, cot_ref, reg_ref, gain1, gain2, wqkv1, wqkv2, wo1, wo2, tab1, tab2, rel_ref,
    mixed_ref, gt_ref, o2, o1, os,
    quad, packed, highs, lows, step1, step2, bias, p1, pt1, c1, a1, p2, pt2, c2,
    dc, dct, dq, dkvt, pen, ds1, ds2, y, z, dz, dy, grads1, grads2, small, g_gain1, g_gain2, sums,
    send_on, recv_on, send_back, recv_back, *job_mem,
):
    where = place()
    barrier = pltpu.get_barrier_semaphore()
    peers = all_peers(where) + [near(by, m[2], m[3]) for by in (-1, 1) for m in MOVES]
    for dev in peers:
        pl.semaphore_signal(barrier, inc=1, device_id=dev, device_id_type=MESH)
    jobs = []
    for n, (units, src, out) in enumerate(((BIG, grads2, o2), (BIG, grads1, o1), (LITTLE, small, os))):
        held = job_mem[n * 8 : n * 8 + 8]
        jobs.append(Job(units, (src, out) + held[:6], held[6:], where))
    sum2, sum1, sum_small = (job.stage for job in jobs)

    pack_tables(tab1, tab2, packed, step1, step2)
    index_in_quads(rel_ref, highs, lows)
    gather_bias(packed, highs, lows, bias, 0, WT // 8)

    into_quads(tok_ref, quad)
    x = quad[...]
    xh, _ = norm(x)
    project((xh * gain1[...]).astype(BF16), wqkv1, p1, pt1)
    over_heads(p1, pt1, forward=(bias, step1, True, None, c1, a1))
    put_quads((x + dot(c1[...], wo1[...])).astype(BF16), y)

    pl.semaphore_wait(barrier, len(peers))
    on = shift(-1, y, z, send_on, recv_on)
    into_quads(cot_ref, quad)
    ef = quad[...]
    e = ef.astype(BF16)
    context_grad(e, wo2, dc, dct)
    split = reg_ref[0, 0, 0] != reg_ref[0, 11, 0]
    lower_row = lax.broadcasted_iota(I32, (WT, WT), 0) >= 144
    lower_col = lax.broadcasted_iota(I32, (WT, WT), 1) >= 144
    pen[...] = jnp.where((lower_row != lower_col) & split, -1e30, 0.0)
    clear_pad(ds1)
    clear_pad(ds2)
    for copy in on:
        copy.wait()

    x = get_quads(z)
    xh, rstd = norm(x)
    h = (xh * gain2[...]).astype(BF16)
    project(h, wqkv2, p2, pt2)
    over_heads(p2, pt2, (bias, step2, False, pen, c2, None), (dc, dct, None, ds2, dq, dkvt))
    put_quads(input_grad(xh, rstd, gain2[...], ef, dq, dkvt, wqkv2, g_gain2).astype(BF16), dz)
    back = shift(1, dz, dy, send_back, recv_back)
    weight_grads(h, c2, e, dq, dkvt, grads2)
    sum2(0)
    quad[...] = x + dot(c2[...], wo2[...])
    out_of_quads(quad, mixed_ref)

    into_quads(tok_ref, quad)
    xh, rstd = norm(quad[...])
    h = (xh * gain1[...]).astype(BF16)
    for copy in back:
        copy.wait()
    ef = get_quads(dy)
    e = ef.astype(BF16)
    context_grad(e, wo1, dc, dct)
    sum2(1)
    over_heads(p1, pt1, None, (dc, dct, a1, ds1, dq, dkvt), (0, 2))
    sum2(2)
    over_heads(p1, pt1, None, (dc, dct, a1, ds1, dq, dkvt), (2, 4))
    sum2(3)
    weight_grads(h, c1, e, dq, dkvt, grads1)
    sum1(0)
    sum2(4)
    quad[...] = input_grad(xh, rstd, gain1[...], ef, dq, dkvt, wqkv1, g_gain1)
    out_of_quads(quad, gt_ref)
    sum1(1)
    sum2(5)

    sums[...] = jnp.zeros_like(sums)
    for part in range(3):
        table_grads((ds1, ds2), highs, lows, sums, part * 12, part * 12 + 12)
        sum1(2 + part)
        if part < 2:
            sum2(6 + part)
    small[:224, :] = sums[:, :128].astype(BF16)
    small[224:448, :] = sums[:, 128:].astype(BF16)
    gains = [g[:, n * 128 : (n + 1) * 128] for g in (g_gain1, g_gain2) for n in range(4)]
    gains.append(jnp.zeros((SROWS - 456, 128), F32))
    small[448:, :] = jnp.concatenate(gains, 0).astype(BF16)
    sum_small(0)
    sum1(5)
    sum_small(1)
    sum_small(2)
    sum1(6)
    for stage in range(3, 8):
        sum_small(stage)
    sum1(7)


def widen_kernel(s2, s1, small, gq1, gq2, gp1, gp2, gg1, gg2, gt1, gt2):
    for src, gq, gp in ((s1, gq1, gp1), (s2, gq2, gp2)):
        for n in range(12):
            gq[:, n * 128 : (n + 1) * 128] = src[n * D : (n + 1) * D, :].astype(F32)
        for n in range(4):
            gp[:, n * 128 : (n + 1) * 128] = src[(12 + n) * D : (13 + n) * D, :].astype(F32)
    tail = small[448:464, :].astype(F32)
    for b, (gg, gt) in enumerate(((gg1, gt1), (gg2, gt2))):
        for n in range(4):
            gg[:, n * 128 : (n + 1) * 128] = tail[b * 4 + n : b * 4 + n + 1]
        for k in range(2 * HIGHS):
            at = (b * HIGHS + k // 2) * 16 + (k % 2) * 224
            width = min(128, NB - k * 128)
            if width > 0:
                gt[:, k * 128 : k * 128 + width] = small[at : at + 16, :width].astype(F32)


def on_device(
    tokens, cotangent, gain_first, gain_second, qkv_first, qkv_second, proj_first, proj_second,
    table_first, table_second, rel_index, regions,
):
    def arr(shape, dtype=BF16):
        return jax.ShapeDtypeStruct(shape, dtype)

    def mem(*shape, dtype=BF16):
        return pltpu.VMEM(shape, dtype)

    grid = arr((2, 12, 12, D))
    big, little = arr((GROWS, 128)), arr((SROWS, 128))
    three = pltpu.SemaphoreType.DMA((3,))
    mixed, grad_tokens, s2, s1, ss = pl.pallas_call(
        kernel,
        out_shape=[grid, grid, big, big, little],
        in_specs=[VM, VM, SM] + [VM] * 9,
        out_specs=[VM] * 5,
        scratch_shapes=[
            mem(WT, D, dtype=F32), mem(HEADS, CHUNKS * 128, dtype=I32),
            mem(WT, PADW, dtype=I32), mem(WT, PADW, dtype=I32), mem(HEADS, 128, dtype=F32), mem(HEADS, 128, dtype=F32),
            mem(HEADS, WT, PADW, dtype=I32),
            mem(WT, 3 * D), mem(3 * D, WT), mem(WT, D), mem(HEADS, WT, WT),
            mem(WT, 3 * D), mem(3 * D, WT), mem(WT, D),
            mem(WT, D), mem(D, WT), mem(WT, D), mem(2 * D, WT), mem(WT, WT, dtype=F32),
            mem(WT, HEADS, PADW, dtype=F32), mem(WT, HEADS, PADW, dtype=F32),
        ]
        + [mem(4, QPAD, D)] * 4
        + [
            mem(GROWS, 128), mem(GROWS, 128), mem(SROWS, 128),
            mem(1, D, dtype=F32), mem(1, D, dtype=F32), mem(224, 256, dtype=F32),
            three, three, three, three,
        ]
        + job_scratch(GROWS) + job_scratch(GROWS) + job_scratch(SROWS),
        compiler_params=pltpu.CompilerParams(vmem_limit_bytes=62 << 20, collective_id=3, has_side_effects=True),
        name="window_pair",
    )(
        tokens, cotangent, regions, gain_first.reshape(1, D), gain_second.reshape(1, D), qkv_first, qkv_second,
        proj_first, proj_second, table_first, table_second, rel_index,
    )
    gq1, gq2, gp1, gp2, gg1, gg2, gt1, gt2 = pl.pallas_call(
        widen_kernel,
        out_shape=[
            arr((D, 3 * D), F32), arr((D, 3 * D), F32), arr((D, D), F32), arr((D, D), F32),
            arr((1, D), F32), arr((1, D), F32), arr((HEADS, NB), F32), arr((HEADS, NB), F32),
        ],
        in_specs=[VM] * 3, out_specs=[VM] * 8,
        compiler_params=PARAMS,
        name="widen_grads",
    )(s2, s1, ss)
    return mixed, grad_tokens, gg1.reshape(D), gg2.reshape(D), gq1, gq2, gp1, gp2, gt1, gt2


def solution(mesh):
    grid = P(None, "lat", "lon", None)
    return jax.shard_map(
        on_device,
        mesh=mesh,
        in_specs=(grid, grid) + (P(),) * 9 + (P(None, "lat", "lon"),),
        out_specs=(grid, grid) + (P(),) * 8,
        check_vma=False,
    )
```

```python
import jax
import jax.numpy as jnp
from jax import lax
from jax.experimental import pallas as pl
from jax.experimental.pallas import tpu as pltpu
from jax.sharding import PartitionSpec as P

F32, BF16, I32 = jnp.float32, jnp.bfloat16, jnp.int32
MESH = pl.DeviceIdType.MESH
D, HEADS, DEPTH, WT, NB = 512, 16, 32, 288, 1587
QUAD, QPAD = 72, 80
PADW, CHUNKS, HIGHS = 384, 13, 7
EPS = 1e-05
LOG2E = 1.4426950408889634
SCALE = DEPTH**-0.5
GROWS, SROWS = 8192, 512
VM = pl.BlockSpec(memory_space=pltpu.VMEM)
SM = pl.BlockSpec(memory_space=pltpu.SMEM)
PARAMS = pltpu.CompilerParams(vmem_limit_bytes=60 << 20)


def quad_row(row, col_half):
    return row // 6 * 144 + col_half * 72 + row % 6 * 12


def dot(a, b):
    return jnp.dot(a, b, preferred_element_type=F32)


def dot_nt(a, b):
    return lax.dot_general(a, b, (((1,), (1,)), ((), ())), preferred_element_type=F32)


def dot_tn(a, b):
    return lax.dot_general(a, b, (((0,), (0,)), ((), ())), preferred_element_type=F32)


def into_quads(src, dst):
    for r in range(12):
        v = src[r].astype(F32).reshape(24, D)
        for ch in range(2):
            dst[pl.ds(quad_row(r, ch), 12), :] = v[ch * 12 : ch * 12 + 12]


def out_of_quads(src, dst):
    for r in range(12):
        both = [src[pl.ds(quad_row(r, ch), 12), :] for ch in range(2)]
        dst[r] = jnp.concatenate(both, 0).reshape(12, 2, D).astype(BF16)


def put_quads(value, dst):
    for q in range(4):
        dst[q, :QUAD, :] = value[q * QUAD : (q + 1) * QUAD]
        dst[q, QUAD:, :] = jnp.zeros((QPAD - QUAD, D), dst.dtype)


def get_quads(src):
    return jnp.concatenate([src[q, :QUAD, :].astype(F32) for q in range(4)], 0)


def norm(x):
    xc = x - jnp.mean(x, -1, keepdims=True)
    rstd = lax.rsqrt(jnp.mean(xc * xc, -1, keepdims=True) + EPS)
    return xc * rstd, rstd


def project(h, w_ref, p, pt):
    for n in range(3):
        cols = slice(n * D, n * D + D)
        v = dot(h, w_ref[:, cols])
        p[:, cols] = v.astype(BF16)
        pt[cols, :] = v.T.astype(BF16)


def index_in_quads(rel_ref, highs, lows):
    at = lax.broadcasted_iota(I32, (WT, WT), 0)
    half = (at >= 144).astype(I32)
    rest = at - 144 * half
    col = (rest >= 72).astype(I32)
    rest = rest - 72 * col
    row = sum((rest >= 12 * k).astype(I32) for k in range(1, 6))
    rest = rest - 12 * row
    natural = (rest & 1) * 144 + (half * 6 + row) * 12 + col * 6 + (rest >> 1)
    perm = (natural == lax.broadcasted_iota(I32, (WT, WT), 1)).astype(F32).astype(BF16)
    rel = rel_ref[...]
    high = (rel >> 8).astype(F32).astype(BF16)
    low = (rel & 255).astype(F32).astype(BF16)

    def moved(part):
        return dot_nt(dot(perm, part).astype(BF16), perm)

    high, low = moved(high), moved(low)
    highs[:, PADW - 128 :] = jnp.zeros((WT, 128), I32)
    lows[:, PADW - 128 :] = jnp.zeros((WT, 128), I32)
    highs[:, :WT] = high.astype(I32)
    lows[:, :WT] = low.astype(I32)


def pack_tables(first_ref, second_ref, packed, step_first, step_second):
    parts = []
    for ref, step_ref in ((first_ref, step_first), (second_ref, step_second)):
        t = ref[...]
        least = jnp.min(t, -1, keepdims=True)
        span = jnp.maximum(jnp.max(t, -1, keepdims=True) - least, 1e-20)
        parts.append(jnp.clip(jnp.floor((t - least) * (65535.0 / span) + 0.5), 0.0, 65535.0).astype(I32))
        step_ref[...] = jnp.broadcast_to(span * (LOG2E / 65535.0), (HEADS, 128))
    packed[:, (CHUNKS - 1) * 128 :] = jnp.zeros((HEADS, 128), I32)
    packed[:, :NB] = (parts[0] << 16) | parts[1]


def gather_bias(packed, highs, lows, bias, start, count):
    @pl.loop(start, start + count)
    def _(r):
        rows = pl.ds(pl.multiple_of(r * 8, 8), 8)
        for ct in range(3):
            lanes = pl.ds(ct * 128, 128)
            high, low = highs[rows, lanes], lows[rows, lanes]
            chunk = high * 2 + (low >> 7)
            lane = low & 127
            masks = [chunk == c for c in range(CHUNKS)]
            for h in range(HEADS):
                acc = None
                for c in range(CHUNKS):
                    row = jnp.broadcast_to(packed[h : h + 1, c * 128 : (c + 1) * 128], (8, 128))
                    found = jnp.take_along_axis(row, lane, axis=1)
                    acc = found if acc is None else jnp.where(masks[c], found, acc)
                bias[h, rows, lanes] = acc


def softmax_head(q, kt, packed, step, high, pen):
    s = dot(q, kt) * (SCALE * LOG2E)
    steps = lax.shift_right_logical(packed, 16) if high else packed & 0xFFFF
    s = s + steps.astype(F32) * step
    if pen is not None:
        s = s + pen
    e = jnp.exp2(s - jnp.max(s, -1, keepdims=True))
    return e * (1.0 / jnp.sum(e, -1, keepdims=True))


def over_heads(p, pt, forward=None, backward=None, groups=(0, 4)):
    lanes = lax.broadcasted_iota(I32, (WT, 128), 1) // DEPTH

    @pl.loop(*groups)
    def _(g):
        g0 = pl.multiple_of(g * 128, 128)
        qg = p[:, pl.ds(g0, 128)]
        kg = p[:, pl.ds(D + g0, 128)]
        vg = p[:, pl.ds(2 * D + g0, 128)]
        ktg = pt[pl.ds(D + g0, 128), :]
        vtg = pt[pl.ds(2 * D + g0, 128), :]
        zero = jnp.zeros_like(qg)
        c_acc = q_acc = None
        if backward is not None:
            dc, dct, a_in, ds_out, dq, dkvt = backward
            dcg = dc[:, pl.ds(g0, 128)]
        for hh in range(4):
            h = g * 4 + hh
            mine = lanes == hh
            if forward is not None:
                bias, steps, high, pen, c, a_out = forward
                a32 = softmax_head(
                    jnp.where(mine, qg, zero),
                    ktg,
                    bias[h, :, :WT],
                    steps[pl.ds(h, 1), 0:1],
                    high,
                    None if pen is None else pen[...],
                )
                a = a32.astype(BF16)
                ch = dot(a, vg)
                c_acc = ch if c_acc is None else jnp.where(mine, ch, c_acc)
                if a_out is not None:
                    a_out[h] = a
            else:
                a = a_in[h]
                a32 = a.astype(F32)
            if backward is not None:
                r0 = pl.multiple_of(g0 + hh * DEPTH, DEPTH)
                da = dot(jnp.where(mine, dcg, zero), vtg)
                ds = a32 * (da - jnp.sum(a32 * da, -1, keepdims=True))
                ds_out[:, h, :WT] = ds
                dsb = ds.astype(BF16)
                dqh = dot(dsb, kg)
                q_acc = dqh if q_acc is None else jnp.where(mine, dqh, q_acc)
                dkvt[pl.ds(r0, DEPTH), :] = (dot(pt[pl.ds(r0, DEPTH), :], dsb) * SCALE).astype(BF16)
                dkvt[pl.ds(D + r0, DEPTH), :] = dot(dct[pl.ds(r0, DEPTH), :], a).astype(BF16)
        if forward is not None:
            c[:, pl.ds(g0, 128)] = c_acc.astype(BF16)
        if backward is not None:
            dq[:, pl.ds(g0, 128)] = (q_acc * SCALE).astype(BF16)


def table_grads(blocks, highs, lows, out, first, start, stop):
    low_of = lax.broadcasted_iota(I32, (256, PADW), 0).astype(F32).astype(BF16)
    one, nil = jnp.ones((256, PADW), BF16), jnp.zeros((256, PADW), BF16)

    @pl.loop(first + start, first + stop)
    def _(r):
        rows = pl.ds(pl.multiple_of(r * 8, 8), 8)
        high8 = highs[rows, :].astype(F32).astype(BF16)
        low8 = lows[rows, :].astype(F32).astype(BF16)
        for part in range(2):
            left, right = [], []
            for i in range(part * 4, part * 4 + 4):
                high = jnp.broadcast_to(high8[i : i + 1], (HEADS, PADW))
                low = jnp.broadcast_to(low8[i : i + 1], (256, PADW))
                picked = []
                for block, theirs in blocks:
                    ds = (block[r * 8 + i] + theirs[(r - first) * 8 + i]).astype(BF16)
                    picked += [jnp.where(high == jnp.array(k, BF16), ds, jnp.zeros_like(ds)) for k in range(HIGHS)]
                left.append(jnp.concatenate(picked, 0))
                right.append(jnp.where(low == low_of, one, nil))
            out[...] += dot_nt(jnp.concatenate(left, 1), jnp.concatenate(right, 1))


def put_columns(value, dst, first):
    for n in range(value.shape[1] // 128):
        at = (first + n) * D
        dst[at : at + D, :] = value[:, n * 128 : (n + 1) * 128].astype(BF16)


def qkv_grads(h, dq, dkvt, grads):
    put_columns(dot_tn(h, dq[...]), grads, 0)
    put_columns(dot_nt(h.T, dkvt[...]), grads, 4)


def input_grad(xh, rstd, gain, ef, dq, dkvt, wqkv, g_gain):
    dh = dot_nt(dq[...], wqkv[:, :D]) + dot(wqkv[:, D:], dkvt[...]).T
    dh = dh.astype(BF16).astype(F32)
    g_gain[...] = jnp.sum(dh * xh, 0, keepdims=True)
    dxh = dh * gain
    return rstd * (dxh - jnp.mean(dxh, -1, keepdims=True) - xh * jnp.mean(dxh * xh, -1, keepdims=True)) + ef


def clear_pad(ds):
    ds[:, :, PADW - 128 :] = jnp.zeros((WT, HEADS, 128), F32)


def context_grad(e, wo, dc, dct):
    v = dot_nt(e, wo[...])
    dc[...] = v.astype(BF16)
    dct[...] = v.T.astype(BF16)


def place():
    lon, lat = lax.axis_index("lon"), lax.axis_index("lat")
    x, z, y = lon // 8, (lon // 2) % 4, (lon % 2) * 2 + lat // 2
    return x, y, z, lat % 2


def device(x, y, z, core):
    return {"lon": x * 8 + z * 2 + y // 2, "lat": (y % 2) * 2 + core}


def near(step, along_lon, along_lat):
    return {
        "lon": (lax.axis_index("lon") + step * along_lon + 32) % 32,
        "lat": (lax.axis_index("lat") + step * along_lat + 4) % 4,
    }


MOVES = ((2, 1, 1, 0), (1, 2, 0, 1), (0, 3, 1, 1))


def shift(by, src, dst, send, recv):
    copies = []
    for n, (here, there, along_lon, along_lat) in enumerate(MOVES):
        a, b = (here, there) if by < 0 else (there, here)
        copies.append(
            pltpu.make_async_remote_copy(
                src_ref=src.at[a], dst_ref=dst.at[b], send_sem=send.at[n], recv_sem=recv.at[n],
                device_id=near(by, along_lon, along_lat), device_id_type=MESH,
            )
        )
        copies[-1].start()
    a, b = (3, 0) if by < 0 else (0, 3)
    dst[b] = src[a]
    return copies


class Job:
    def __init__(self, units, refs, sems, where):
        self.src, self.out, self.r0, self.a, self.r1, self.b, self.r2, self.c4 = refs
        self.send, self.recv = sems
        self.half = self.src.shape[0] // 2
        self.where = where
        self.sets = []
        at = 0
        for n, count in enumerate(units):
            self.sets.append((at, count * 256, (n % 3, (n + 1) % 3, (n + 2) % 3)))
            at += count * 256
        self.live = []

    def peer(self, axis, d):
        to = list(self.where)
        to[axis] = (to[axis] + d) % 4
        return device(*to)

    def copy(self, src, dst, sem, to):
        made = pltpu.make_async_remote_copy(
            src_ref=src, dst_ref=dst, send_sem=self.send.at[sem], recv_sem=self.recv.at[sem],
            device_id=to, device_id_type=MESH,
        )
        made.start()
        self.live.append(made)

    def wait(self):
        for made in self.live:
            made.wait()
        self.live = []

    def other(self):
        x, y, z, core = self.where
        return device(x, y, z, 1 - core)

    def mine(self):
        return pl.multiple_of(self.where[3] * self.half, 128)

    def add(self, dst, dst_at, parts, rows):
        step = 256 if rows % 256 == 0 else rows

        @pl.loop(0, rows // step)
        def _(n):
            total = None
            for ref, lead, at in parts:
                where = pl.ds(pl.multiple_of(at + n * step, 16), step)
                v = (ref[where, :] if lead is None else ref[lead, where, :]).astype(F32)
                total = v if total is None else total + v
            dst[pl.ds(pl.multiple_of(dst_at + n * step, 16), step), :] = total.astype(BF16)

    def stage(self, n):
        if n == 0:
            theirs = pl.multiple_of((1 - self.where[3]) * self.half, 128)
            self.copy(self.src.at[pl.ds(theirs, self.half)], self.r0, 0, self.other())
        if n == 1:
            self.wait()
            self.add(self.a, 0, [(self.src, None, self.mine()), (self.r0, None, 0)], self.half)
            for k, (at, rows, axes) in enumerate(self.sets):
                me = self.where[axes[0]]
                for d in range(1, 4):
                    piece = pl.multiple_of(at + (me + d) % 4 * (rows // 4), 16)
                    self.copy(
                        self.a.at[pl.ds(piece, rows // 4)], self.r1.at[d - 1, pl.ds(at // 4, rows // 4)],
                        1 + k * 3 + d - 1, self.peer(axes[0], d),
                    )
        if n == 2:
            self.wait()
            for k, (at, rows, axes) in enumerate(self.sets):
                own = at + self.where[axes[0]] * (rows // 4)
                self.add(
                    self.b, at // 4, [(self.a, None, own)] + [(self.r1, d, at // 4) for d in range(3)], rows // 4
                )
                me = self.where[axes[1]]
                for d in range(1, 4):
                    piece = pl.multiple_of(at // 4 + (me + d) % 4 * (rows // 16), 16)
                    self.copy(
                        self.b.at[pl.ds(piece, rows // 16)], self.r2.at[d - 1, pl.ds(at // 16, rows // 16)],
                        10 + k * 3 + d - 1, self.peer(axes[1], d),
                    )
        if n == 3:
            self.wait()
            for k, (at, rows, axes) in enumerate(self.sets):
                own = at // 4 + self.where[axes[1]] * (rows // 16)
                me = self.where[axes[2]]
                small = pl.ds(at // 16, rows // 16)
                total = self.b[pl.ds(pl.multiple_of(own, 16), rows // 16), :].astype(F32)
                for d in range(3):
                    total = total + self.r2[d, small, :].astype(F32)
                self.c4[me, small, :] = total.astype(BF16)
                for d in range(1, 4):
                    self.copy(
                        self.c4.at[me, small], self.c4.at[me, small],
                        19 + k * 3 + d - 1, self.peer(axes[2], d),
                    )
        if n == 4:
            self.wait()
            for k, (at, rows, axes) in enumerate(self.sets):
                small = pl.ds(at // 16, rows // 16)
                total = self.c4[0, small, :].astype(F32)
                for d in range(1, 4):
                    total = total + self.c4[d, small, :].astype(F32)
                here = self.mine() + at + self.where[axes[0]] * (rows // 4) + self.where[axes[1]] * (rows // 16)
                spot = pl.ds(pl.multiple_of(here, 16), rows // 16)
                self.out[spot, :] = total.astype(BF16)
                for d in range(1, 4):
                    self.copy(self.out.at[spot], self.out.at[spot], 28 + k * 3 + d - 1, self.peer(axes[1], d))
        if n == 5:
            self.wait()
            for k, (at, rows, axes) in enumerate(self.sets):
                here = self.mine() + at + self.where[axes[0]] * (rows // 4)
                spot = pl.ds(pl.multiple_of(here, 16), rows // 4)
                for d in range(1, 4):
                    self.copy(self.out.at[spot], self.out.at[spot], 37 + k * 3 + d - 1, self.peer(axes[0], d))
        if n == 6:
            self.wait()
            spot = pl.ds(self.mine(), self.half)
            self.copy(self.out.at[spot], self.out.at[spot], 46, self.other())
        if n == 7:
            self.wait()


class SmallJob(Job):
    def __init__(self, refs, sems, where):
        self.src, self.out, self.r0, self.a, self.r1, self.c4 = refs
        self.send, self.recv = sems
        self.half = self.src.shape[0] // 2
        self.where = where
        self.live = []

    def plane(self):
        x, y, z, core = self.where
        me = x * 4 + z
        for d in range(1, 16):
            to = (me + d) % 16
            yield d, me, to, device(to // 4, y, to % 4, core)

    def stage(self, n):
        x, y, z, core = self.where
        me = x * 4 + z
        if n == 0:
            Job.stage(self, 0)
        if n == 1:
            self.wait()
            total = self.src[pl.ds(self.mine(), self.half), :].astype(F32) + self.r0[...].astype(F32)
            self.a[...] = total.astype(BF16)
            self.r1[me] = self.a[pl.ds(pl.multiple_of(me * 16, 16), 16), :]
            for d, me, to, dev in self.plane():
                self.copy(self.a.at[pl.ds(pl.multiple_of(to * 16, 16), 16)], self.r1.at[me], d, dev)
        if n == 2:
            self.wait()
            total = self.r1[0].astype(F32)
            for k in range(1, 16):
                total = total + self.r1[k].astype(F32)
            self.c4[y] = total.astype(BF16)
            for d in range(1, 4):
                self.copy(self.c4.at[y], self.c4.at[y], 15 + d, device(x, (y + d) % 4, z, core))
        if n == 3:
            self.wait()
            total = self.c4[0].astype(F32)
            for k in range(1, 4):
                total = total + self.c4[k].astype(F32)
            spot = pl.ds(pl.multiple_of(self.mine() + me * 16, 16), 16)
            self.out[spot, :] = total.astype(BF16)
            for d, me, to, dev in self.plane():
                self.copy(self.out.at[spot], self.out.at[spot], 18 + d, dev)
        if n == 4:
            Job.stage(self, 6)
        if n == 5:
            self.wait()


UNITS = {8192: (6, 5, 5), 6144: (4, 4, 4), 2048: (2, 1, 1)}


def small_scratch():
    half = SROWS // 2
    return [
        pltpu.VMEM((half, 128), BF16),
        pltpu.VMEM((half, 128), BF16),
        pltpu.VMEM((16, 16, 128), BF16),
        pltpu.VMEM((4, 16, 128), BF16),
        pltpu.SemaphoreType.DMA((47,)),
        pltpu.SemaphoreType.DMA((47,)),
    ]


def job_scratch(rows):
    half = rows // 2
    return [
        pltpu.VMEM((half, 128), BF16),
        pltpu.VMEM((half, 128), BF16),
        pltpu.VMEM((3, half // 4, 128), BF16),
        pltpu.VMEM((half // 4, 128), BF16),
        pltpu.VMEM((3, half // 16, 128), BF16),
        pltpu.VMEM((4, half // 16, 128), BF16),
        pltpu.SemaphoreType.DMA((47,)),
        pltpu.SemaphoreType.DMA((47,)),
    ]


def all_peers(where):
    x, y, z, core = where
    to = [device(x, y, z, 1 - core)]
    for axis in range(3):
        for d in range(1, 4):
            at = list(where)
            at[axis] = (at[axis] + d) % 4
            to.append(device(*at))
    for dx in range(1, 4):
        for dz in range(1, 4):
            to.append(device((x + dx) % 4, y, (z + dz) % 4, core))
    return to


def kernel(
    tok_ref, cot_ref, reg_ref, gain1, gain2, wqkv1, wqkv2, wo1, wo2, tab1, tab2, rel_ref,
    mixed_ref, gt_ref, o2, oq, oo, os,
    quad, packed, highs, lows, step1, step2, bias, p1, pt1, c1, a1, p2, pt2, c2,
    dc, dct, dq, dkvt, pen, ds1, ds2, their_ds1, their_ds2, y, z, dz, dy,
    small, g_gain1, g_gain2, sums,
    send_on, recv_on, send_back, recv_back, pair_send, pair_recv, *job_mem,
):
    where = place()
    core = where[3]
    barrier = pltpu.get_barrier_semaphore()
    peers = all_peers(where) + [near(by, m[2], m[3]) for by in (-1, 1) for m in MOVES]
    for dev in peers:
        pl.semaphore_signal(barrier, inc=1, device_id=dev, device_id_type=MESH)
    jobs = []
    for n, ref in enumerate((o2, oq, oo)):
        held = job_mem[n * 8 : n * 8 + 8]
        jobs.append(Job(UNITS[ref.shape[0]], (ref, ref) + held[:6], held[6:], where))
    sum2, sum_q, sum_o = (job.stage for job in jobs)
    held = job_mem[24:]
    sum_s = SmallJob((small, os) + held[:4], held[4:], where).stage

    def to_pair(n, src, dst):
        copy = pltpu.make_async_remote_copy(
            src_ref=src, dst_ref=dst, send_sem=pair_send.at[n], recv_sem=pair_recv.at[n],
            device_id=device(*where[:3], 1 - core), device_id_type=MESH,
        )
        copy.start()
        return copy

    mine = pl.multiple_of(core * 144, 16)
    theirs = pl.multiple_of((1 - core) * 144, 16)
    first = core * 18

    pack_tables(tab1, tab2, packed, step1, step2)
    index_in_quads(rel_ref, highs, lows)
    pl.semaphore_wait(barrier, len(peers))
    sent = []
    for part in range(3):
        gather_bias(packed, highs, lows, bias, first + part * 6, 6)
        rows = pl.ds(pl.multiple_of(mine + part * 48, 16), 48)
        sent.append(to_pair(part, bias.at[:, rows], bias.at[:, rows]))

    into_quads(tok_ref, quad)
    x = quad[...]
    xh, _ = norm(x)
    project((xh * gain1[...]).astype(BF16), wqkv1, p1, pt1)
    for copy in sent:
        copy.wait()
    over_heads(p1, pt1, forward=(bias, step1, True, None, c1, a1))
    put_quads((x + dot(c1[...], wo1[...])).astype(BF16), y)

    on = shift(-1, y, z, send_on, recv_on)
    into_quads(cot_ref, quad)
    ef = quad[...]
    e = ef.astype(BF16)
    context_grad(e, wo2, dc, dct)
    split = reg_ref[0, 0, 0] != reg_ref[11, 0, 0]
    lower_row = lax.broadcasted_iota(I32, (WT, WT), 0) >= 144
    lower_col = lax.broadcasted_iota(I32, (WT, WT), 1) >= 144
    pen[...] = jnp.where((lower_row != lower_col) & split, -1e30, 0.0)
    clear_pad(ds1)
    clear_pad(ds2)
    sums[...] = jnp.zeros_like(sums)
    for copy in on:
        copy.wait()

    x = get_quads(z)
    xh, rstd = norm(x)
    h = (xh * gain2[...]).astype(BF16)
    project(h, wqkv2, p2, pt2)
    over_heads(p2, pt2, (bias, step2, False, pen, c2, None), (dc, dct, None, ds2, dq, dkvt))
    put_quads(input_grad(xh, rstd, gain2[...], ef, dq, dkvt, wqkv2, g_gain2).astype(BF16), dz)
    back = shift(1, dz, dy, send_back, recv_back)
    ds_sent = [to_pair(3, ds2.at[pl.ds(theirs, 144)], their_ds2)]
    qkv_grads(h, dq, dkvt, o2)
    put_columns(dot_tn(c2[...], e), o2, 12)
    sum2(0)
    quad[...] = x + dot(c2[...], wo2[...])
    out_of_quads(quad, mixed_ref)

    into_quads(tok_ref, quad)
    xh, rstd = norm(quad[...])
    h = (xh * gain1[...]).astype(BF16)
    for copy in back:
        copy.wait()
    ef = get_quads(dy)
    e = ef.astype(BF16)
    put_columns(dot_tn(c1[...], e), oo, 0)
    sum2(1)
    sum_o(0)
    context_grad(e, wo1, dc, dct)
    sum_o(1)
    over_heads(p1, pt1, None, (dc, dct, a1, ds1, dq, dkvt), (0, 2))
    sum2(2)
    sum_o(2)
    over_heads(p1, pt1, None, (dc, dct, a1, ds1, dq, dkvt), (2, 4))
    ds_sent.append(to_pair(4, ds1.at[pl.ds(theirs, 144)], their_ds1))
    sum2(3)
    sum_o(3)
    qkv_grads(h, dq, dkvt, oq)
    sum_q(0)
    sum2(4)
    sum_o(4)
    quad[...] = input_grad(xh, rstd, gain1[...], ef, dq, dkvt, wqkv1, g_gain1)
    sum_q(1)
    sum2(5)
    out_of_quads(quad, gt_ref)
    sum_o(5)
    for copy in ds_sent:
        copy.wait()

    blocks = ((ds1, their_ds1), (ds2, their_ds2))
    for part in range(3):
        table_grads(blocks, highs, lows, sums, first, part * 6, part * 6 + 6)
        sum_q(2 + part)
        if part > 0:
            sum2(5 + part)
            sum_o(5 + part)
    small[:224, :] = sums[:, :128].astype(BF16)
    small[224:448, :] = sums[:, 128:].astype(BF16)
    gains = [g[:, n * 128 : (n + 1) * 128] for g in (g_gain1, g_gain2) for n in range(4)]
    gains.append(jnp.zeros((SROWS - 456, 128), F32))
    small[448:, :] = jnp.concatenate(gains, 0).astype(BF16)
    sum_s(0)
    sum_s(1)
    sum_q(5)
    sum_s(2)
    sum_s(3)
    sum_q(6)
    sum_s(4)
    sum_s(5)
    sum_q(7)


def widen_kernel(s2, sq, so, small, gq1, gq2, gp1, gp2, gg1, gg2, gt1, gt2):
    for src, at, dst in ((sq, 0, gq1), (so, 0, gp1), (s2, 0, gq2), (s2, 12, gp2)):
        for n in range(dst.shape[1] // 128):
            dst[:, n * 128 : (n + 1) * 128] = src[at + n].astype(F32)

    @pl.when(pl.program_id(0) == 0)
    def _():
        tail = small[448:464, :].astype(F32)
        for b, (gg, gt) in enumerate(((gg1, gt1), (gg2, gt2))):
            for n in range(4):
                gg[:, n * 128 : (n + 1) * 128] = tail[b * 4 + n : b * 4 + n + 1]
            for k in range(CHUNKS):
                at = (b * HIGHS + k // 2) * 16 + (k % 2) * 224
                width = min(128, NB - k * 128)
                gt[:, k * 128 : k * 128 + width] = small[at : at + 16, :width].astype(F32)


def on_device(
    tokens, cotangent, gain_first, gain_second, qkv_first, qkv_second, proj_first, proj_second,
    table_first, table_second, rel_index, regions,
):
    def arr(shape, dtype=BF16):
        return jax.ShapeDtypeStruct(shape, dtype)

    def mem(*shape, dtype=BF16):
        return pltpu.VMEM(shape, dtype)

    grid = arr((12, 12, 2, D))
    rows = (8192, 6144, 2048)
    three = pltpu.SemaphoreType.DMA((3,))
    five = pltpu.SemaphoreType.DMA((5,))
    mixed, grad_tokens, s2, sq, so, small = pl.pallas_call(
        kernel,
        out_shape=[grid, grid] + [arr((n, 128)) for n in rows] + [arr((SROWS, 128))],
        in_specs=[VM, VM, SM] + [VM] * 9,
        out_specs=[VM] * 6,
        scratch_shapes=[
            mem(WT, D, dtype=F32), mem(HEADS, CHUNKS * 128, dtype=I32),
            mem(WT, PADW, dtype=I32), mem(WT, PADW, dtype=I32), mem(HEADS, 128, dtype=F32), mem(HEADS, 128, dtype=F32),
            mem(HEADS, WT, PADW, dtype=I32),
            mem(WT, 3 * D), mem(3 * D, WT), mem(WT, D), mem(HEADS, WT, WT),
            mem(WT, 3 * D), mem(3 * D, WT), mem(WT, D),
            mem(WT, D), mem(D, WT), mem(WT, D), mem(2 * D, WT), mem(WT, WT, dtype=F32),
            mem(WT, HEADS, PADW, dtype=F32), mem(WT, HEADS, PADW, dtype=F32),
            mem(144, HEADS, PADW, dtype=F32), mem(144, HEADS, PADW, dtype=F32),
        ]
        + [mem(4, QPAD, D)] * 4
        + [mem(SROWS, 128), mem(1, D, dtype=F32), mem(1, D, dtype=F32), mem(224, 256, dtype=F32)]
        + [three] * 4 + [five] * 2
        + [ref for n in rows for ref in job_scratch(n)] + small_scratch(),
        compiler_params=pltpu.CompilerParams(vmem_limit_bytes=62 << 20, collective_id=3, has_side_effects=True),
        name="window_pair",
    )(
        tokens.transpose(1, 2, 0, 3), cotangent.transpose(1, 2, 0, 3), regions.transpose(1, 0, 2),
        gain_first.reshape(1, D), gain_second.reshape(1, D), qkv_first, qkv_second,
        proj_first, proj_second, table_first, table_second, rel_index,
    )

    def part(*shape):
        return pl.BlockSpec(shape, lambda i: (0, i, 0) if len(shape) == 3 else (i, 0))

    def whole(*shape):
        return pl.BlockSpec(shape, lambda i: (0, 0))

    gq1, gq2, gp1, gp2, gg1, gg2, gt1, gt2 = pl.pallas_call(
        widen_kernel,
        out_shape=[
            arr((D, 3 * D), F32), arr((D, 3 * D), F32), arr((D, D), F32), arr((D, D), F32),
            arr((1, D), F32), arr((1, D), F32), arr((HEADS, NB), F32), arr((HEADS, NB), F32),
        ],
        grid=(4,),
        in_specs=[part(16, 128, 128), part(12, 128, 128), part(4, 128, 128), whole(SROWS, 128)],
        out_specs=[
            part(128, 3 * D), part(128, 3 * D), part(128, D), part(128, D),
            whole(1, D), whole(1, D), whole(HEADS, NB), whole(HEADS, NB),
        ],
        compiler_params=PARAMS,
        name="widen_grads",
    )(s2.reshape(16, D, 128), sq.reshape(12, D, 128), so.reshape(4, D, 128), small)
    mixed, grad_tokens = mixed.transpose(2, 0, 1, 3), grad_tokens.transpose(2, 0, 1, 3)
    return mixed, grad_tokens, gg1.reshape(D), gg2.reshape(D), gq1, gq2, gp1, gp2, gt1, gt2


def solution(mesh):
    grid = P(None, "lat", "lon", None)
    return jax.shard_map(
        on_device,
        mesh=mesh,
        in_specs=(grid, grid) + (P(),) * 9 + (P(None, "lat", "lon"),),
        out_specs=(grid, grid) + (P(),) * 8,
        check_vma=False,
    )
```

```python
import jax
import jax.numpy as jnp
from jax import lax
from jax.experimental import pallas as pl
from jax.experimental.pallas import tpu as pltpu
from jax.sharding import PartitionSpec as P

F32, BF16, I32 = jnp.float32, jnp.bfloat16, jnp.int32
MESH = pl.DeviceIdType.MESH
D, HEADS, DEPTH, WT, NB = 512, 16, 32, 288, 1587
QUAD, QPAD = 72, 80
PADW, CHUNKS, HIGHS = 384, 13, 7
EPS = 1e-05
LOG2E = 1.4426950408889634
SCALE = DEPTH**-0.5
GROWS, SROWS = 8192, 512
VM = pl.BlockSpec(memory_space=pltpu.VMEM)
SM = pl.BlockSpec(memory_space=pltpu.SMEM)
PARAMS = pltpu.CompilerParams(vmem_limit_bytes=60 << 20)


def quad_row(row, col_half):
    return row // 6 * 144 + col_half * 72 + row % 6 * 12


def dot(a, b):
    return jnp.dot(a, b, preferred_element_type=F32)


def dot_nt(a, b):
    return lax.dot_general(a, b, (((1,), (1,)), ((), ())), preferred_element_type=F32)


def dot_tn(a, b):
    return lax.dot_general(a, b, (((0,), (0,)), ((), ())), preferred_element_type=F32)


def into_quads(src, dst):
    for r in range(12):
        v = src[r].astype(F32).reshape(24, D)
        for ch in range(2):
            dst[pl.ds(quad_row(r, ch), 12), :] = v[ch * 12 : ch * 12 + 12]


def out_of_quads(src, dst):
    for r in range(12):
        both = [src[pl.ds(quad_row(r, ch), 12), :] for ch in range(2)]
        dst[r] = jnp.concatenate(both, 0).reshape(12, 2, D).astype(BF16)


def put_quads(value, dst):
    for q in range(4):
        dst[q, :QUAD, :] = value[q * QUAD : (q + 1) * QUAD]
        dst[q, QUAD:, :] = jnp.zeros((QPAD - QUAD, D), dst.dtype)


def get_quads(src):
    return jnp.concatenate([src[q, :QUAD, :].astype(F32) for q in range(4)], 0)


def norm(x):
    xc = x - jnp.mean(x, -1, keepdims=True)
    rstd = lax.rsqrt(jnp.mean(xc * xc, -1, keepdims=True) + EPS)
    return xc * rstd, rstd


def project(h, w_ref, p, pt):
    for n in range(3):
        cols = slice(n * D, n * D + D)
        v = dot(h, w_ref[:, cols])
        p[:, cols] = v.astype(BF16)
        pt[cols, :] = v.T.astype(BF16)


def index_in_quads(rel_ref, highs, lows):
    at = lax.broadcasted_iota(I32, (WT, WT), 0)
    half = (at >= 144).astype(I32)
    rest = at - 144 * half
    col = (rest >= 72).astype(I32)
    rest = rest - 72 * col
    row = sum((rest >= 12 * k).astype(I32) for k in range(1, 6))
    rest = rest - 12 * row
    natural = (rest & 1) * 144 + (half * 6 + row) * 12 + col * 6 + (rest >> 1)
    perm = (natural == lax.broadcasted_iota(I32, (WT, WT), 1)).astype(F32).astype(BF16)
    rel = rel_ref[...]
    high = (rel >> 8).astype(F32).astype(BF16)
    low = (rel & 255).astype(F32).astype(BF16)

    def moved(part):
        return dot_nt(dot(perm, part).astype(BF16), perm)

    high, low = moved(high), moved(low)
    highs[:, PADW - 128 :] = jnp.zeros((WT, 128), I32)
    lows[:, PADW - 128 :] = jnp.zeros((WT, 128), I32)
    highs[:, :WT] = high.astype(I32)
    lows[:, :WT] = low.astype(I32)


def pack_tables(first_ref, second_ref, packed, step_first, step_second):
    parts = []
    for ref, step_ref in ((first_ref, step_first), (second_ref, step_second)):
        t = ref[...]
        least = jnp.min(t, -1, keepdims=True)
        span = jnp.maximum(jnp.max(t, -1, keepdims=True) - least, 1e-20)
        parts.append(jnp.clip(jnp.floor((t - least) * (65535.0 / span) + 0.5), 0.0, 65535.0).astype(I32))
        step_ref[...] = jnp.broadcast_to(span * (LOG2E / 65535.0), (HEADS, 128))
    packed[:, (CHUNKS - 1) * 128 :] = jnp.zeros((HEADS, 128), I32)
    packed[:, :NB] = (parts[0] << 16) | parts[1]


def gather_bias(packed, highs, lows, bias, start, count):
    @pl.loop(start, start + count)
    def _(r):
        rows = pl.ds(pl.multiple_of(r * 8, 8), 8)
        for ct in range(3):
            lanes = pl.ds(ct * 128, 128)
            high, low = highs[rows, lanes], lows[rows, lanes]
            chunk = high * 2 + (low >> 7)
            lane = low & 127
            masks = [chunk == c for c in range(CHUNKS)]
            for h in range(HEADS):
                acc = None
                for c in range(CHUNKS):
                    row = jnp.broadcast_to(packed[h : h + 1, c * 128 : (c + 1) * 128], (8, 128))
                    found = jnp.take_along_axis(row, lane, axis=1)
                    acc = found if acc is None else jnp.where(masks[c], found, acc)
                bias[h, rows, lanes] = acc


def over_heads(p, pt, forward=None, backward=None, groups=(0, 4), wide=2):
    lanes = lax.broadcasted_iota(I32, (WT, 128), 1) // DEPTH

    @pl.loop(*groups)
    def _(g):
        g0 = pl.multiple_of(g * 128, 128)
        qg = p[:, pl.ds(g0, 128)]
        kg = p[:, pl.ds(D + g0, 128)]
        vg = p[:, pl.ds(2 * D + g0, 128)]
        ktg = pt[pl.ds(D + g0, 128), :]
        vtg = pt[pl.ds(2 * D + g0, 128), :]
        zero = jnp.zeros_like(qg)
        c_acc = q_acc = None
        if backward is not None:
            dc, dct, a_in, ds_out, dq, dkvt = backward
            dcg = dc[:, pl.ds(g0, 128)]
        for start in range(0, 4, wide):
            some = range(start, start + wide)
            heads = [g * 4 + hh for hh in some]
            spans = [pl.ds(pl.multiple_of(g0 + hh * DEPTH, DEPTH), DEPTH) for hh in some]
            if forward is not None:
                bias, steps, high, pen, c, a_out = forward
                s = [dot(jnp.where(lanes == hh, qg, zero), ktg) for hh in some]
            if backward is not None:
                da = [dot(jnp.where(lanes == hh, dcg, zero), vtg) for hh in some]
            if forward is not None:
                for k, h in enumerate(heads):
                    packed = bias[h, :, :WT]
                    entry = lax.shift_right_logical(packed, 16) if high else packed & 0xFFFF
                    s[k] = s[k] * (SCALE * LOG2E) + entry.astype(F32) * steps[pl.ds(h, 1), 0:1]
                    if pen is not None:
                        s[k] = s[k] + pen[...]
                most = [jnp.max(v, -1, keepdims=True) for v in s]
                expo = [jnp.exp2(v - m) for v, m in zip(s, most)]
                total = [1.0 / jnp.sum(v, -1, keepdims=True) for v in expo]
                a32 = [v * r for v, r in zip(expo, total)]
                a = [v.astype(BF16) for v in a32]
            else:
                a = [a_in[h] for h in heads]
                a32 = [v.astype(F32) for v in a]
            if backward is not None:
                mean = [jnp.sum(v * w, -1, keepdims=True) for v, w in zip(a32, da)]
                ds = [v * (w - m) for v, w, m in zip(a32, da, mean)]
                dsb = [v.astype(BF16) for v in ds]
            if forward is not None:
                ctx = [dot(v, vg) for v in a]
            if backward is not None:
                dqh = [dot(v, kg) for v in dsb]
                dk = [dot(pt[span, :], v) * SCALE for span, v in zip(spans, dsb)]
                dv = [dot(dct[span, :], v) for span, v in zip(spans, a)]
            for k, hh in enumerate(some):
                own = lanes == hh
                if forward is not None:
                    c_acc = ctx[k] if c_acc is None else jnp.where(own, ctx[k], c_acc)
                    if a_out is not None:
                        a_out[heads[k]] = a[k]
                if backward is not None:
                    q_acc = dqh[k] if q_acc is None else jnp.where(own, dqh[k], q_acc)
                    ds_out[:, heads[k], :WT] = ds[k]
                    at = pl.multiple_of(g0 + hh * DEPTH, DEPTH)
                    dkvt[pl.ds(at, DEPTH), :] = dk[k].astype(BF16)
                    dkvt[pl.ds(D + at, DEPTH), :] = dv[k].astype(BF16)
        if forward is not None:
            c[:, pl.ds(g0, 128)] = c_acc.astype(BF16)
        if backward is not None:
            dq[:, pl.ds(g0, 128)] = (q_acc * SCALE).astype(BF16)


def table_grads(blocks, highs, lows, out, first, start, stop):
    low_of = lax.broadcasted_iota(I32, (256, PADW), 0).astype(F32).astype(BF16)
    one, nil = jnp.ones((256, PADW), BF16), jnp.zeros((256, PADW), BF16)

    @pl.loop(first + start, first + stop)
    def _(r):
        rows = pl.ds(pl.multiple_of(r * 8, 8), 8)
        high8 = highs[rows, :].astype(F32).astype(BF16)
        low8 = lows[rows, :].astype(F32).astype(BF16)
        for part in range(2):
            left, right = [], []
            for i in range(part * 4, part * 4 + 4):
                high = jnp.broadcast_to(high8[i : i + 1], (HEADS, PADW))
                low = jnp.broadcast_to(low8[i : i + 1], (256, PADW))
                picked = []
                for block, theirs in blocks:
                    ds = (block[r * 8 + i] + theirs[(r - first) * 8 + i]).astype(BF16)
                    picked += [jnp.where(high == jnp.array(k, BF16), ds, jnp.zeros_like(ds)) for k in range(HIGHS)]
                left.append(jnp.concatenate(picked, 0))
                right.append(jnp.where(low == low_of, one, nil))
            out[...] += dot_nt(jnp.concatenate(left, 1), jnp.concatenate(right, 1))


def put_columns(value, dst, first):
    for n in range(value.shape[1] // 128):
        at = (first + n) * D
        dst[at : at + D, :] = value[:, n * 128 : (n + 1) * 128].astype(BF16)


def qkv_grads(h, ht, dq, dkvt, grads, first, last):
    cols = slice(first * 128, last * 128)
    put_columns(dot_tn(h, dq[:, cols]), grads, 0)
    put_columns(dot_nt(ht, dkvt[cols, :]), grads, last - first)
    put_columns(dot_nt(ht, dkvt[D + first * 128 : D + last * 128, :]), grads, 2 * (last - first))


def input_grad(xh, rstd, gain, ef, dq, dkvt, wqkv, g_gain):
    dh = dot_nt(dq[...], wqkv[:, :D]) + dot(wqkv[:, D:], dkvt[...]).T
    dh = dh.astype(BF16).astype(F32)
    g_gain[...] = jnp.sum(dh * xh, 0, keepdims=True)
    dxh = dh * gain
    return rstd * (dxh - jnp.mean(dxh, -1, keepdims=True) - xh * jnp.mean(dxh * xh, -1, keepdims=True)) + ef


def clear_pad(ds):
    ds[:, :, PADW - 128 :] = jnp.zeros((WT, HEADS, 128), F32)


def context_grad(e, wo, dc, dct):
    v = dot_nt(e, wo[...])
    dc[...] = v.astype(BF16)
    dct[...] = v.T.astype(BF16)


def place():
    lon, lat = lax.axis_index("lon"), lax.axis_index("lat")
    x, z, y = lon // 8, (lon // 2) % 4, (lon % 2) * 2 + lat // 2
    return x, y, z, lat % 2


def device(x, y, z, core):
    return {"lon": x * 8 + z * 2 + y // 2, "lat": (y % 2) * 2 + core}


def near(step, along_lon, along_lat):
    return {
        "lon": (lax.axis_index("lon") + step * along_lon + 32) % 32,
        "lat": (lax.axis_index("lat") + step * along_lat + 4) % 4,
    }


MOVES = ((2, 1, 1, 0), (1, 2, 0, 1), (0, 3, 1, 1))


def shift(by, src, dst, send, recv):
    copies = []
    for n, (here, there, along_lon, along_lat) in enumerate(MOVES):
        a, b = (here, there) if by < 0 else (there, here)
        copies.append(
            pltpu.make_async_remote_copy(
                src_ref=src.at[a], dst_ref=dst.at[b], send_sem=send.at[n], recv_sem=recv.at[n],
                device_id=near(by, along_lon, along_lat), device_id_type=MESH,
            )
        )
        copies[-1].start()
    a, b = (3, 0) if by < 0 else (0, 3)
    dst[b] = src[a]
    return copies


class Job:
    def __init__(self, units, refs, sems, where):
        self.src, self.out, self.r0, self.r1, self.b, self.r2, self.c4 = refs
        self.a = self.r0
        self.send, self.recv = sems
        self.half = self.src.shape[0] // 2
        self.where = where
        self.sets = []
        at = 0
        for n, count in enumerate(units):
            self.sets.append((at, count * 256, (n % 3, (n + 1) % 3, (n + 2) % 3)))
            at += count * 256
        self.live = []

    def peer(self, axis, d):
        to = list(self.where)
        to[axis] = (to[axis] + d) % 4
        return device(*to)

    def copy(self, src, dst, sem, to):
        made = pltpu.make_async_remote_copy(
            src_ref=src, dst_ref=dst, send_sem=self.send.at[sem], recv_sem=self.recv.at[sem],
            device_id=to, device_id_type=MESH,
        )
        made.start()
        self.live.append(made)

    def wait(self):
        for made in self.live:
            made.wait()
        self.live = []

    def other(self):
        x, y, z, core = self.where
        return device(x, y, z, 1 - core)

    def mine(self):
        return pl.multiple_of(self.where[3] * self.half, 128)

    def add(self, dst, dst_at, parts, rows):
        step = 256 if rows % 256 == 0 else rows

        @pl.loop(0, rows // step)
        def _(n):
            total = None
            for ref, lead, at in parts:
                where = pl.ds(pl.multiple_of(at + n * step, 16), step)
                v = (ref[where, :] if lead is None else ref[lead, where, :]).astype(F32)
                total = v if total is None else total + v
            dst[pl.ds(pl.multiple_of(dst_at + n * step, 16), step), :] = total.astype(BF16)

    def stage(self, n):
        if n == 0:
            theirs = pl.multiple_of((1 - self.where[3]) * self.half, 128)
            self.copy(self.src.at[pl.ds(theirs, self.half)], self.r0, 0, self.other())
        if n == 1:
            self.wait()
            self.add(self.a, 0, [(self.src, None, self.mine()), (self.r0, None, 0)], self.half)
            for k, (at, rows, axes) in enumerate(self.sets):
                me = self.where[axes[0]]
                for d in range(1, 4):
                    piece = pl.multiple_of(at + (me + d) % 4 * (rows // 4), 16)
                    self.copy(
                        self.a.at[pl.ds(piece, rows // 4)], self.r1.at[d - 1, pl.ds(at // 4, rows // 4)],
                        1 + k * 3 + d - 1, self.peer(axes[0], d),
                    )
        if n == 2:
            self.wait()
            for k, (at, rows, axes) in enumerate(self.sets):
                own = at + self.where[axes[0]] * (rows // 4)
                self.add(
                    self.b, at // 4, [(self.a, None, own)] + [(self.r1, d, at // 4) for d in range(3)], rows // 4
                )
                me = self.where[axes[1]]
                for d in range(1, 4):
                    piece = pl.multiple_of(at // 4 + (me + d) % 4 * (rows // 16), 16)
                    self.copy(
                        self.b.at[pl.ds(piece, rows // 16)], self.r2.at[d - 1, pl.ds(at // 16, rows // 16)],
                        10 + k * 3 + d - 1, self.peer(axes[1], d),
                    )
        if n == 3:
            self.wait()
            for k, (at, rows, axes) in enumerate(self.sets):
                own = at // 4 + self.where[axes[1]] * (rows // 16)
                me = self.where[axes[2]]
                small = pl.ds(at // 16, rows // 16)
                total = self.b[pl.ds(pl.multiple_of(own, 16), rows // 16), :].astype(F32)
                for d in range(3):
                    total = total + self.r2[d, small, :].astype(F32)
                self.c4[me, small, :] = total.astype(BF16)
                for d in range(1, 4):
                    self.copy(
                        self.c4.at[me, small], self.c4.at[me, small],
                        19 + k * 3 + d - 1, self.peer(axes[2], d),
                    )
        if n == 4:
            self.wait()
            for k, (at, rows, axes) in enumerate(self.sets):
                small = pl.ds(at // 16, rows // 16)
                total = self.c4[0, small, :].astype(F32)
                for d in range(1, 4):
                    total = total + self.c4[d, small, :].astype(F32)
                here = self.mine() + at + self.where[axes[0]] * (rows // 4) + self.where[axes[1]] * (rows // 16)
                spot = pl.ds(pl.multiple_of(here, 16), rows // 16)
                self.out[spot, :] = total.astype(BF16)
                for d in range(1, 4):
                    self.copy(self.out.at[spot], self.out.at[spot], 28 + k * 3 + d - 1, self.peer(axes[1], d))
        if n == 5:
            self.wait()
            for k, (at, rows, axes) in enumerate(self.sets):
                here = self.mine() + at + self.where[axes[0]] * (rows // 4)
                spot = pl.ds(pl.multiple_of(here, 16), rows // 4)
                for d in range(1, 4):
                    self.copy(self.out.at[spot], self.out.at[spot], 37 + k * 3 + d - 1, self.peer(axes[0], d))
        if n == 6:
            self.wait()
            spot = pl.ds(self.mine(), self.half)
            self.copy(self.out.at[spot], self.out.at[spot], 46, self.other())
        if n == 7:
            self.wait()


class SmallJob(Job):
    def __init__(self, refs, sems, where):
        self.src, self.out, self.r0, self.a, self.r1, self.c4 = refs
        self.send, self.recv = sems
        self.half = self.src.shape[0] // 2
        self.where = where
        self.live = []

    def plane(self):
        x, y, z, core = self.where
        me = x * 4 + z
        for d in range(1, 16):
            to = (me + d) % 16
            yield d, me, to, device(to // 4, y, to % 4, core)

    def stage(self, n):
        x, y, z, core = self.where
        me = x * 4 + z
        if n == 0:
            Job.stage(self, 0)
        if n == 1:
            self.wait()
            total = self.src[pl.ds(self.mine(), self.half), :].astype(F32) + self.r0[...].astype(F32)
            self.a[...] = total.astype(BF16)
            self.r1[me] = self.a[pl.ds(pl.multiple_of(me * 16, 16), 16), :]
            for d, me, to, dev in self.plane():
                self.copy(self.a.at[pl.ds(pl.multiple_of(to * 16, 16), 16)], self.r1.at[me], d, dev)
        if n == 2:
            self.wait()
            total = self.r1[0].astype(F32)
            for k in range(1, 16):
                total = total + self.r1[k].astype(F32)
            self.c4[y] = total.astype(BF16)
            for d in range(1, 4):
                self.copy(self.c4.at[y], self.c4.at[y], 15 + d, device(x, (y + d) % 4, z, core))
        if n == 3:
            self.wait()
            total = self.c4[0].astype(F32)
            for k in range(1, 4):
                total = total + self.c4[k].astype(F32)
            spot = pl.ds(pl.multiple_of(self.mine() + me * 16, 16), 16)
            self.out[spot, :] = total.astype(BF16)
            for d, me, to, dev in self.plane():
                self.copy(self.out.at[spot], self.out.at[spot], 18 + d, dev)
        if n == 4:
            Job.stage(self, 6)
        if n == 5:
            self.wait()


UNITS = {8192: (6, 5, 5), 3072: (2, 2, 2), 2048: (2, 1, 1)}


def small_scratch():
    half = SROWS // 2
    return [
        pltpu.VMEM((half, 128), BF16),
        pltpu.VMEM((half, 128), BF16),
        pltpu.VMEM((16, 16, 128), BF16),
        pltpu.VMEM((4, 16, 128), BF16),
        pltpu.SemaphoreType.DMA((47,)),
        pltpu.SemaphoreType.DMA((47,)),
    ]


def job_scratch(rows):
    half = rows // 2
    return [
        pltpu.VMEM((half, 128), BF16),
        pltpu.VMEM((3, half // 4, 128), BF16),
        pltpu.VMEM((half // 4, 128), BF16),
        pltpu.VMEM((3, half // 16, 128), BF16),
        pltpu.VMEM((4, half // 16, 128), BF16),
        pltpu.SemaphoreType.DMA((47,)),
        pltpu.SemaphoreType.DMA((47,)),
    ]


def all_peers(where):
    x, y, z, core = where
    to = [device(x, y, z, 1 - core)]
    for axis in range(3):
        for d in range(1, 4):
            at = list(where)
            at[axis] = (at[axis] + d) % 4
            to.append(device(*at))
    for dx in range(1, 4):
        for dz in range(1, 4):
            to.append(device((x + dx) % 4, y, (z + dz) % 4, core))
    return to


def kernel(
    tok_ref, cot_hbm, reg_ref, gain1, gain2, wqkv1_hbm, wqkv2_hbm, wo1_hbm, wo2_hbm, tab1, tab2, rel_ref,
    mixed_ref, gt_ref, out2, out_a, out_b, out_o, os,
    cot_ref, wqkv1, wqkv2, wo1, wo2, g2, ga, gb, go, in_sems, out_sems,
    quad, packed, highs, lows, step1, step2, bias, p1, pt1, c1, a1, p2, pt2, c2,
    dc, dct, dq, dkvt, pen, ds1, ds2, their_ds1, their_ds2, y, z, dz, dy,
    small, g_gain1, g_gain2, sums,
    send_on, recv_on, send_back, recv_back, pair_send, pair_recv, *job_mem,
):
    where = place()
    core = where[3]
    barrier = pltpu.get_barrier_semaphore()
    peers = all_peers(where) + [near(by, m[2], m[3]) for by in (-1, 1) for m in MOVES]
    for dev in peers:
        pl.semaphore_signal(barrier, inc=1, device_id=dev, device_id_type=MESH)
    brought = []
    for n, (src, dst) in enumerate(
        ((wqkv1_hbm, wqkv1), (wo1_hbm, wo1), (cot_hbm, cot_ref), (wo2_hbm, wo2), (wqkv2_hbm, wqkv2))
    ):
        brought.append(pltpu.make_async_copy(src, dst, in_sems.at[n]))
        brought[-1].start()
    jobs = []
    for n, ref in enumerate((g2, ga, gb, go)):
        held = job_mem[n * 7 : n * 7 + 7]
        jobs.append(Job(UNITS[ref.shape[0]], (ref, ref) + held[:5], held[5:], where))
    sum2, sum_a, sum_b, sum_o = (job.stage for job in jobs)
    held = job_mem[28:]
    sum_s = SmallJob((small, os) + held[:4], held[4:], where).stage

    def to_pair(n, src, dst):
        copy = pltpu.make_async_remote_copy(
            src_ref=src, dst_ref=dst, send_sem=pair_send.at[n], recv_sem=pair_recv.at[n],
            device_id=device(*where[:3], 1 - core), device_id_type=MESH,
        )
        copy.start()
        return copy

    written = []

    def write(n, src, dst):
        written.append(pltpu.make_async_copy(src, dst, out_sems.at[n]))
        written[-1].start()

    mine = pl.multiple_of(core * 144, 16)
    theirs = pl.multiple_of((1 - core) * 144, 16)
    first = core * 18

    pack_tables(tab1, tab2, packed, step1, step2)
    index_in_quads(rel_ref, highs, lows)
    pl.semaphore_wait(barrier, len(peers))
    sent = []
    for part in range(3):
        gather_bias(packed, highs, lows, bias, first + part * 6, 6)
        rows = pl.ds(pl.multiple_of(mine + part * 48, 16), 48)
        sent.append(to_pair(part, bias.at[:, rows], bias.at[:, rows]))

    for copy in brought[:2]:
        copy.wait()
    into_quads(tok_ref, quad)
    x = quad[...]
    xh, _ = norm(x)
    project((xh * gain1[...]).astype(BF16), wqkv1, p1, pt1)
    for copy in sent:
        copy.wait()
    over_heads(p1, pt1, forward=(bias, step1, True, None, c1, a1))
    put_quads((x + dot(c1[...], wo1[...])).astype(BF16), y)

    on = shift(-1, y, z, send_on, recv_on)
    for copy in brought[2:]:
        copy.wait()
    into_quads(cot_ref, quad)
    ef = quad[...]
    e = ef.astype(BF16)
    context_grad(e, wo2, dc, dct)
    split = reg_ref[0, 0, 0] != reg_ref[11, 0, 0]
    lower_row = lax.broadcasted_iota(I32, (WT, WT), 0) >= 144
    lower_col = lax.broadcasted_iota(I32, (WT, WT), 1) >= 144
    pen[...] = jnp.where((lower_row != lower_col) & split, -1e30, 0.0)
    clear_pad(ds1)
    clear_pad(ds2)
    sums[...] = jnp.zeros_like(sums)
    for copy in on:
        copy.wait()

    x = get_quads(z)
    xh, rstd = norm(x)
    h = (xh * gain2[...]).astype(BF16)
    project(h, wqkv2, p2, pt2)
    over_heads(p2, pt2, (bias, step2, False, pen, c2, None), (dc, dct, None, ds2, dq, dkvt))
    put_quads(input_grad(xh, rstd, gain2[...], ef, dq, dkvt, wqkv2, g_gain2).astype(BF16), dz)
    back = shift(1, dz, dy, send_back, recv_back)
    ds_sent = [to_pair(3, ds2.at[pl.ds(theirs, 144)], their_ds2)]
    qkv_grads(h, h.T, dq, dkvt, g2, 0, 4)
    put_columns(dot_tn(c2[...], e), g2, 12)
    sum2(0)
    quad[...] = x + dot(c2[...], wo2[...])
    out_of_quads(quad, mixed_ref)

    into_quads(tok_ref, quad)
    xh, rstd = norm(quad[...])
    h = (xh * gain1[...]).astype(BF16)
    for copy in back:
        copy.wait()
    ef = get_quads(dy)
    e = ef.astype(BF16)
    put_columns(dot_tn(c1[...], e), go, 0)
    sum2(1)
    sum_o(0)
    ht = h.T
    context_grad(e, wo1, dc, dct)
    sum_o(1)
    over_heads(p1, pt1, None, (dc, dct, a1, ds1, dq, dkvt), (0, 2))
    ds_sent.append(to_pair(4, ds1.at[pl.ds(theirs, 144), pl.ds(0, 8)], their_ds1.at[:, pl.ds(0, 8)]))
    qkv_grads(h, ht, dq, dkvt, ga, 0, 2)
    sum_a(0)
    sum2(2)
    over_heads(p1, pt1, None, (dc, dct, a1, ds1, dq, dkvt), (2, 4))
    ds_sent.append(to_pair(5, ds1.at[pl.ds(theirs, 144), pl.ds(8, 8)], their_ds1.at[:, pl.ds(8, 8)]))
    sum_a(1)
    qkv_grads(h, ht, dq, dkvt, gb, 2, 4)
    sum_b(0)
    sum_o(2)
    quad[...] = input_grad(xh, rstd, gain1[...], ef, dq, dkvt, wqkv1, g_gain1)
    sum_b(1)
    sum2(3)
    for copy in ds_sent:
        copy.wait()

    blocks = ((ds1, their_ds1), (ds2, their_ds2))
    between = (
        ((sum_a, 2), (sum_o, 3), (sum2, 4)),
        ((sum_b, 2), (sum_a, 3), (sum2, 5)),
        ((sum_b, 3), (sum_o, 4), (sum_a, 4)),
        ((sum_b, 4), (sum_o, 5), (sum_a, 5)),
        ((sum_b, 5), (sum2, 6), (sum_o, 6)),
        ((sum_a, 6), (sum2, 7), (sum_o, 7)),
    )
    for part, steps in enumerate(between):
        table_grads(blocks, highs, lows, sums, first, part * 3, part * 3 + 3)
        for step, n in steps:
            step(n)
    small[:224, :] = sums[:, :128].astype(BF16)
    small[224:448, :] = sums[:, 128:].astype(BF16)
    gains = [g[:, n * 128 : (n + 1) * 128] for g in (g_gain1, g_gain2) for n in range(4)]
    gains.append(jnp.zeros((SROWS - 456, 128), F32))
    small[448:, :] = jnp.concatenate(gains, 0).astype(BF16)
    sum_s(0)
    write(0, g2, out2)
    write(1, go, out_o)
    sum_s(1)
    out_of_quads(quad, gt_ref)
    sum_s(2)
    sum_b(6)
    sum_a(7)
    write(2, ga, out_a)
    sum_s(3)
    sum_b(7)
    write(3, gb, out_b)
    sum_s(4)
    sum_s(5)
    for copy in written:
        copy.wait()


def widen_kernel(s2, sa, sb, so, small, gq1, gq2, gp1, gp2, gg1, gg2, gt1, gt2):
    for k in range(3):
        for n in range(4):
            src = sa if n < 2 else sb
            gq1[:, (k * 4 + n) * 128 : (k * 4 + n + 1) * 128] = src[k * 2 + n % 2].astype(F32)
    for src, at, dst in ((so, 0, gp1), (s2, 0, gq2), (s2, 12, gp2)):
        for n in range(dst.shape[1] // 128):
            dst[:, n * 128 : (n + 1) * 128] = src[at + n].astype(F32)

    @pl.when(pl.program_id(0) == 0)
    def _():
        tail = small[448:464, :].astype(F32)
        for b, (gg, gt) in enumerate(((gg1, gt1), (gg2, gt2))):
            for n in range(4):
                gg[:, n * 128 : (n + 1) * 128] = tail[b * 4 + n : b * 4 + n + 1]
            for k in range(CHUNKS):
                at = (b * HIGHS + k // 2) * 16 + (k % 2) * 224
                width = min(128, NB - k * 128)
                gt[:, k * 128 : k * 128 + width] = small[at : at + 16, :width].astype(F32)


def on_device(
    tokens, cotangent, gain_first, gain_second, qkv_first, qkv_second, proj_first, proj_second,
    table_first, table_second, rel_index, regions,
):
    def arr(shape, dtype=BF16):
        return jax.ShapeDtypeStruct(shape, dtype)

    def mem(*shape, dtype=BF16):
        return pltpu.VMEM(shape, dtype)

    grid = arr((12, 12, 2, D))
    rows = (8192, 3072, 3072, 2048)
    hbm = pl.BlockSpec(memory_space=pl.ANY)
    weights = [mem(D, 3 * D), mem(D, 3 * D), mem(D, D), mem(D, D)]
    three = pltpu.SemaphoreType.DMA((3,))
    six = pltpu.SemaphoreType.DMA((6,))
    mixed, grad_tokens, s2, sa, sb, so, small = pl.pallas_call(
        kernel,
        out_shape=[grid, grid] + [arr((n, 128)) for n in rows] + [arr((SROWS, 128))],
        in_specs=[VM, hbm, SM, VM, VM] + [hbm] * 4 + [VM] * 3,
        out_specs=[VM, VM] + [hbm] * 4 + [VM],
        scratch_shapes=[mem(12, 12, 2, D)] + weights + [mem(n, 128) for n in rows] + [six, six]
        + [
            mem(WT, D, dtype=F32), mem(HEADS, CHUNKS * 128, dtype=I32),
            mem(WT, PADW, dtype=I32), mem(WT, PADW, dtype=I32), mem(HEADS, 128, dtype=F32), mem(HEADS, 128, dtype=F32),
            mem(HEADS, WT, PADW, dtype=I32),
            mem(WT, 3 * D), mem(3 * D, WT), mem(WT, D), mem(HEADS, WT, WT),
            mem(WT, 3 * D), mem(3 * D, WT), mem(WT, D),
            mem(WT, D), mem(D, WT), mem(WT, D), mem(2 * D, WT), mem(WT, WT, dtype=F32),
            mem(WT, HEADS, PADW, dtype=F32), mem(WT, HEADS, PADW, dtype=F32),
            mem(144, HEADS, PADW, dtype=F32), mem(144, HEADS, PADW, dtype=F32),
        ]
        + [mem(4, QPAD, D)] * 4
        + [mem(SROWS, 128), mem(1, D, dtype=F32), mem(1, D, dtype=F32), mem(224, 256, dtype=F32)]
        + [three] * 4 + [six] * 2
        + [ref for n in rows for ref in job_scratch(n)] + small_scratch(),
        compiler_params=pltpu.CompilerParams(vmem_limit_bytes=62 << 20, collective_id=3, has_side_effects=True),
        name="window_pair",
    )(
        tokens.transpose(1, 2, 0, 3), cotangent.transpose(1, 2, 0, 3), regions.transpose(1, 0, 2),
        gain_first.reshape(1, D), gain_second.reshape(1, D), qkv_first, qkv_second,
        proj_first, proj_second, table_first, table_second, rel_index,
    )

    def part(*shape):
        return pl.BlockSpec(shape, lambda i: (0, i, 0) if len(shape) == 3 else (i, 0))

    def whole(*shape):
        return pl.BlockSpec(shape, lambda i: (0, 0))

    gq1, gq2, gp1, gp2, gg1, gg2, gt1, gt2 = pl.pallas_call(
        widen_kernel,
        out_shape=[
            arr((D, 3 * D), F32), arr((D, 3 * D), F32), arr((D, D), F32), arr((D, D), F32),
            arr((1, D), F32), arr((1, D), F32), arr((HEADS, NB), F32), arr((HEADS, NB), F32),
        ],
        grid=(8,),
        in_specs=[part(16, 64, 128), part(6, 64, 128), part(6, 64, 128), part(4, 64, 128), whole(SROWS, 128)],
        out_specs=[
            part(64, 3 * D), part(64, 3 * D), part(64, D), part(64, D),
            whole(1, D), whole(1, D), whole(HEADS, NB), whole(HEADS, NB),
        ],
        compiler_params=PARAMS,
        name="widen_grads",
    )(s2.reshape(16, D, 128), sa.reshape(6, D, 128), sb.reshape(6, D, 128), so.reshape(4, D, 128), small)
    mixed, grad_tokens = mixed.transpose(2, 0, 1, 3), grad_tokens.transpose(2, 0, 1, 3)
    return mixed, grad_tokens, gg1.reshape(D), gg2.reshape(D), gq1, gq2, gp1, gp2, gt1, gt2


def solution(mesh):
    grid = P(None, "lat", "lon", None)
    return jax.shard_map(
        on_device,
        mesh=mesh,
        in_specs=(grid, grid) + (P(),) * 9 + (P(None, "lat", "lon"),),
        out_specs=(grid, grid) + (P(),) * 8,
        check_vma=False,
    )
```

```python
import jax
import jax.numpy as jnp
from jax import lax
from jax.experimental import pallas as pl
from jax.experimental.pallas import tpu as pltpu
from jax.sharding import PartitionSpec as P

F32, BF16, I32 = jnp.float32, jnp.bfloat16, jnp.int32
MESH = pl.DeviceIdType.MESH
D, HEADS, DEPTH, WT, NB = 512, 16, 32, 288, 1587
QUAD, QPAD = 72, 80
PADW, CHUNKS, HIGHS = 384, 13, 7
EPS = 1e-05
LOG2E = 1.4426950408889634
SCALE = DEPTH**-0.5
GROWS, SROWS = 8192, 512
VM = pl.BlockSpec(memory_space=pltpu.VMEM)
SM = pl.BlockSpec(memory_space=pltpu.SMEM)
PARAMS = pltpu.CompilerParams(vmem_limit_bytes=60 << 20)


def quad_row(row, col_half):
    return row // 6 * 144 + col_half * 72 + row % 6 * 12


def dot(a, b):
    return jnp.dot(a, b, preferred_element_type=F32)


def dot_nt(a, b):
    return lax.dot_general(a, b, (((1,), (1,)), ((), ())), preferred_element_type=F32)


def dot_tn(a, b):
    return lax.dot_general(a, b, (((0,), (0,)), ((), ())), preferred_element_type=F32)


def into_quads(src, dst):
    for r in range(12):
        v = src[r].astype(F32).reshape(24, D)
        for ch in range(2):
            dst[pl.ds(quad_row(r, ch), 12), :] = v[ch * 12 : ch * 12 + 12]


def out_of_quads(src, dst):
    for r in range(12):
        both = [src[pl.ds(quad_row(r, ch), 12), :] for ch in range(2)]
        dst[r] = jnp.concatenate(both, 0).reshape(12, 2, D).astype(BF16)


def put_quads(value, dst):
    for q in range(4):
        dst[q, :QUAD, :] = value[q * QUAD : (q + 1) * QUAD]
        dst[q, QUAD:, :] = jnp.zeros((QPAD - QUAD, D), dst.dtype)


def get_quads(src):
    return jnp.concatenate([src[q, :QUAD, :].astype(F32) for q in range(4)], 0)


def norm(x):
    xc = x - jnp.mean(x, -1, keepdims=True)
    rstd = lax.rsqrt(jnp.mean(xc * xc, -1, keepdims=True) + EPS)
    return xc * rstd, rstd


def project(h, w_ref, p, pt):
    for n in range(3):
        cols = slice(n * D, n * D + D)
        v = dot(h, w_ref[:, cols])
        p[:, cols] = v.astype(BF16)
        pt[cols, :] = v.T.astype(BF16)


def index_in_quads(rel_ref, highs, lows):
    at = lax.broadcasted_iota(I32, (WT, WT), 0)
    half = (at >= 144).astype(I32)
    rest = at - 144 * half
    col = (rest >= 72).astype(I32)
    rest = rest - 72 * col
    row = sum((rest >= 12 * k).astype(I32) for k in range(1, 6))
    rest = rest - 12 * row
    natural = (rest & 1) * 144 + (half * 6 + row) * 12 + col * 6 + (rest >> 1)
    perm = (natural == lax.broadcasted_iota(I32, (WT, WT), 1)).astype(F32).astype(BF16)
    rel = rel_ref[...]
    high = (rel >> 8).astype(F32).astype(BF16)
    low = (rel & 255).astype(F32).astype(BF16)

    def moved(part):
        return dot_nt(dot(perm, part).astype(BF16), perm)

    high, low = moved(high), moved(low)
    highs[:, PADW - 128 :] = jnp.zeros((WT, 128), I32)
    lows[:, PADW - 128 :] = jnp.zeros((WT, 128), I32)
    highs[:, :WT] = high.astype(I32)
    lows[:, :WT] = low.astype(I32)


def pack_tables(first_ref, second_ref, packed, step_first, step_second):
    parts = []
    for ref, step_ref in ((first_ref, step_first), (second_ref, step_second)):
        t = ref[...]
        least = jnp.min(t, -1, keepdims=True)
        span = jnp.maximum(jnp.max(t, -1, keepdims=True) - least, 1e-20)
        parts.append(jnp.clip(jnp.floor((t - least) * (65535.0 / span) + 0.5), 0.0, 65535.0).astype(I32))
        step_ref[...] = jnp.broadcast_to(span * (LOG2E / 65535.0), (HEADS, 128))
    packed[:, (CHUNKS - 1) * 128 :] = jnp.zeros((HEADS, 128), I32)
    packed[:, :NB] = (parts[0] << 16) | parts[1]


def gather_bias(packed, highs, lows, bias, start, count):
    @pl.loop(start, start + count)
    def _(r):
        rows = pl.ds(pl.multiple_of(r * 8, 8), 8)
        for ct in range(3):
            lanes = pl.ds(ct * 128, 128)
            high, low = highs[rows, lanes], lows[rows, lanes]
            chunk = high * 2 + (low >> 7)
            lane = low & 127
            masks = [chunk == c for c in range(CHUNKS)]
            for h in range(HEADS):
                acc = None
                for c in range(CHUNKS):
                    row = jnp.broadcast_to(packed[h : h + 1, c * 128 : (c + 1) * 128], (8, 128))
                    found = jnp.take_along_axis(row, lane, axis=1)
                    acc = found if acc is None else jnp.where(masks[c], found, acc)
                bias[h, rows, lanes] = acc


def over_heads(p, pt, forward=None, backward=None, groups=(0, 4), wide=2):
    lanes = lax.broadcasted_iota(I32, (WT, 128), 1) // DEPTH

    @pl.loop(*groups)
    def _(g):
        g0 = pl.multiple_of(g * 128, 128)
        qg = p[:, pl.ds(g0, 128)]
        kg = p[:, pl.ds(D + g0, 128)]
        vg = p[:, pl.ds(2 * D + g0, 128)]
        ktg = pt[pl.ds(D + g0, 128), :]
        vtg = pt[pl.ds(2 * D + g0, 128), :]
        zero = jnp.zeros_like(qg)
        c_acc = q_acc = None
        if backward is not None:
            dc, dct, a_in, ds_out, dq, dkvt = backward
            dcg = dc[:, pl.ds(g0, 128)]
        for start in range(0, 4, wide):
            some = range(start, start + wide)
            heads = [g * 4 + hh for hh in some]
            spans = [pl.ds(pl.multiple_of(g0 + hh * DEPTH, DEPTH), DEPTH) for hh in some]
            if forward is not None:
                bias, steps, high, pen, c, a_out = forward
                s = [dot(jnp.where(lanes == hh, qg, zero), ktg) for hh in some]
            if backward is not None:
                da = [dot(jnp.where(lanes == hh, dcg, zero), vtg) for hh in some]
            if forward is not None:
                for k, h in enumerate(heads):
                    packed = bias[h, :, :WT]
                    entry = lax.shift_right_logical(packed, 16) if high else packed & 0xFFFF
                    s[k] = s[k] * (SCALE * LOG2E) + entry.astype(F32) * steps[pl.ds(h, 1), 0:1]
                    if pen is not None:
                        s[k] = s[k] + pen[...]
                most = [jnp.max(v, -1, keepdims=True) for v in s]
                expo = [jnp.exp2(v - m) for v, m in zip(s, most)]
                total = [1.0 / jnp.sum(v, -1, keepdims=True) for v in expo]
                a32 = [v * r for v, r in zip(expo, total)]
                a = [v.astype(BF16) for v in a32]
            else:
                a = [a_in[h] for h in heads]
                a32 = [v.astype(F32) for v in a]
            if backward is not None:
                mean = [jnp.sum(v * w, -1, keepdims=True) for v, w in zip(a32, da)]
                ds = [v * (w - m) for v, w, m in zip(a32, da, mean)]
                dsb = [v.astype(BF16) for v in ds]
            if forward is not None:
                ctx = [dot(v, vg) for v in a]
            if backward is not None:
                dqh = [dot(v, kg) for v in dsb]
                dk = [dot(pt[span, :], v) * SCALE for span, v in zip(spans, dsb)]
                dv = [dot(dct[span, :], v) for span, v in zip(spans, a)]
            for k, hh in enumerate(some):
                own = lanes == hh
                if forward is not None:
                    c_acc = ctx[k] if c_acc is None else jnp.where(own, ctx[k], c_acc)
                    if a_out is not None:
                        a_out[heads[k]] = a[k]
                if backward is not None:
                    q_acc = dqh[k] if q_acc is None else jnp.where(own, dqh[k], q_acc)
                    ds_out[:, heads[k], :WT] = ds[k]
                    at = pl.multiple_of(g0 + hh * DEPTH, DEPTH)
                    dkvt[pl.ds(at, DEPTH), :] = dk[k].astype(BF16)
                    dkvt[pl.ds(D + at, DEPTH), :] = dv[k].astype(BF16)
        if forward is not None:
            c[:, pl.ds(g0, 128)] = c_acc.astype(BF16)
        if backward is not None:
            dq[:, pl.ds(g0, 128)] = (q_acc * SCALE).astype(BF16)


def table_grads(blocks, highs, lows, out, first, start, stop):
    low_of = lax.broadcasted_iota(I32, (256, PADW), 0).astype(F32).astype(BF16)
    one, nil = jnp.ones((256, PADW), BF16), jnp.zeros((256, PADW), BF16)

    @pl.loop(first + start, first + stop)
    def _(r):
        rows = pl.ds(pl.multiple_of(r * 8, 8), 8)
        high8 = highs[rows, :].astype(F32).astype(BF16)
        low8 = lows[rows, :].astype(F32).astype(BF16)
        for part in range(2):
            left, right = [], []
            for i in range(part * 4, part * 4 + 4):
                high = jnp.broadcast_to(high8[i : i + 1], (HEADS, PADW))
                low = jnp.broadcast_to(low8[i : i + 1], (256, PADW))
                picked = []
                for block, theirs in blocks:
                    ds = (block[r * 8 + i] + theirs[(r - first) * 8 + i].astype(F32)).astype(BF16)
                    picked += [jnp.where(high == jnp.array(k, BF16), ds, jnp.zeros_like(ds)) for k in range(HIGHS)]
                left.append(jnp.concatenate(picked, 0))
                right.append(jnp.where(low == low_of, one, nil))
            out[...] += dot_nt(jnp.concatenate(left, 1), jnp.concatenate(right, 1))


def put_columns(value, dst, first):
    for n in range(value.shape[1] // 128):
        at = (first + n) * D
        dst[at : at + D, :] = value[:, n * 128 : (n + 1) * 128].astype(BF16)


def qkv_grads(h, ht, dq, dkvt, grads, first, last):
    cols = slice(first * 128, last * 128)
    put_columns(dot_tn(h, dq[:, cols]), grads, 0)
    put_columns(dot_nt(ht, dkvt[cols, :]), grads, last - first)
    put_columns(dot_nt(ht, dkvt[D + first * 128 : D + last * 128, :]), grads, 2 * (last - first))


def input_grad(xh, rstd, gain, ef, dq, dkvt, wqkv, g_gain):
    dh = dot_nt(dq[...], wqkv[:, :D]) + dot(wqkv[:, D:], dkvt[...]).T
    dh = dh.astype(BF16).astype(F32)
    g_gain[...] = jnp.sum(dh * xh, 0, keepdims=True)
    dxh = dh * gain
    return rstd * (dxh - jnp.mean(dxh, -1, keepdims=True) - xh * jnp.mean(dxh * xh, -1, keepdims=True)) + ef


def clear_pad(ds):
    ds[:, :, PADW - 128 :] = jnp.zeros((WT, HEADS, 128), F32)


def context_grad(e, wo, dc, dct):
    v = dot_nt(e, wo[...])
    dc[...] = v.astype(BF16)
    dct[...] = v.T.astype(BF16)


def place():
    lon, lat = lax.axis_index("lon"), lax.axis_index("lat")
    x, z, y = lon // 8, (lon // 2) % 4, (lon % 2) * 2 + lat // 2
    return x, y, z, lat % 2


def device(x, y, z, core):
    return {"lon": x * 8 + z * 2 + y // 2, "lat": (y % 2) * 2 + core}


def near(step, along_lon, along_lat):
    return {
        "lon": (lax.axis_index("lon") + step * along_lon + 32) % 32,
        "lat": (lax.axis_index("lat") + step * along_lat + 4) % 4,
    }


MOVES = ((2, 1, 1, 0), (1, 2, 0, 1), (0, 3, 1, 1))


def shift(by, src, dst, send, recv):
    copies = []
    for n, (here, there, along_lon, along_lat) in enumerate(MOVES):
        a, b = (here, there) if by < 0 else (there, here)
        copies.append(
            pltpu.make_async_remote_copy(
                src_ref=src.at[a], dst_ref=dst.at[b], send_sem=send.at[n], recv_sem=recv.at[n],
                device_id=near(by, along_lon, along_lat), device_id_type=MESH,
            )
        )
        copies[-1].start()
    a, b = (3, 0) if by < 0 else (0, 3)
    dst[b] = src[a]
    return copies


class Job:
    def __init__(self, units, refs, sems, where):
        self.src, self.out, self.r0, self.r1, self.b, self.r2, self.c4 = refs
        self.a = self.r0
        self.send, self.recv = sems
        self.half = self.src.shape[0] // 2
        self.where = where
        self.sets = []
        at = 0
        for n, count in enumerate(units):
            self.sets.append((at, count * 256, (n % 3, (n + 1) % 3, (n + 2) % 3)))
            at += count * 256
        self.live = []

    def peer(self, axis, d):
        to = list(self.where)
        to[axis] = (to[axis] + d) % 4
        return device(*to)

    def copy(self, src, dst, sem, to):
        made = pltpu.make_async_remote_copy(
            src_ref=src, dst_ref=dst, send_sem=self.send.at[sem], recv_sem=self.recv.at[sem],
            device_id=to, device_id_type=MESH,
        )
        made.start()
        self.live.append(made)

    def wait(self):
        for made in self.live:
            made.wait()
        self.live = []

    def other(self):
        x, y, z, core = self.where
        return device(x, y, z, 1 - core)

    def mine(self):
        return pl.multiple_of(self.where[3] * self.half, 128)

    def add(self, dst, dst_at, parts, rows):
        step = 256 if rows % 256 == 0 else rows

        @pl.loop(0, rows // step)
        def _(n):
            total = None
            for ref, lead, at in parts:
                where = pl.ds(pl.multiple_of(at + n * step, 16), step)
                v = (ref[where, :] if lead is None else ref[lead, where, :]).astype(F32)
                total = v if total is None else total + v
            dst[pl.ds(pl.multiple_of(dst_at + n * step, 16), step), :] = total.astype(BF16)

    def stage(self, n):
        if n == 0:
            theirs = pl.multiple_of((1 - self.where[3]) * self.half, 128)
            self.copy(self.src.at[pl.ds(theirs, self.half)], self.r0, 0, self.other())
        if n == 1:
            self.wait()
            self.add(self.a, 0, [(self.src, None, self.mine()), (self.r0, None, 0)], self.half)
            for k, (at, rows, axes) in enumerate(self.sets):
                me = self.where[axes[0]]
                for d in range(1, 4):
                    piece = pl.multiple_of(at + (me + d) % 4 * (rows // 4), 16)
                    self.copy(
                        self.a.at[pl.ds(piece, rows // 4)], self.r1.at[d - 1, pl.ds(at // 4, rows // 4)],
                        1 + k * 3 + d - 1, self.peer(axes[0], d),
                    )
        if n == 2:
            self.wait()
            for k, (at, rows, axes) in enumerate(self.sets):
                own = at + self.where[axes[0]] * (rows // 4)
                self.add(
                    self.b, at // 4, [(self.a, None, own)] + [(self.r1, d, at // 4) for d in range(3)], rows // 4
                )
                me = self.where[axes[1]]
                for d in range(1, 4):
                    piece = pl.multiple_of(at // 4 + (me + d) % 4 * (rows // 16), 16)
                    self.copy(
                        self.b.at[pl.ds(piece, rows // 16)], self.r2.at[d - 1, pl.ds(at // 16, rows // 16)],
                        10 + k * 3 + d - 1, self.peer(axes[1], d),
                    )
        if n == 3:
            self.wait()
            for k, (at, rows, axes) in enumerate(self.sets):
                own = at // 4 + self.where[axes[1]] * (rows // 16)
                me = self.where[axes[2]]
                small = pl.ds(at // 16, rows // 16)
                total = self.b[pl.ds(pl.multiple_of(own, 16), rows // 16), :].astype(F32)
                for d in range(3):
                    total = total + self.r2[d, small, :].astype(F32)
                self.c4[me, small, :] = total.astype(BF16)
                for d in range(1, 4):
                    self.copy(
                        self.c4.at[me, small], self.c4.at[me, small],
                        19 + k * 3 + d - 1, self.peer(axes[2], d),
                    )
        if n == 4:
            self.wait()
            for k, (at, rows, axes) in enumerate(self.sets):
                small = pl.ds(at // 16, rows // 16)
                total = self.c4[0, small, :].astype(F32)
                for d in range(1, 4):
                    total = total + self.c4[d, small, :].astype(F32)
                here = self.mine() + at + self.where[axes[0]] * (rows // 4) + self.where[axes[1]] * (rows // 16)
                spot = pl.ds(pl.multiple_of(here, 16), rows // 16)
                self.out[spot, :] = total.astype(BF16)
                for d in range(1, 4):
                    self.copy(self.out.at[spot], self.out.at[spot], 28 + k * 3 + d - 1, self.peer(axes[1], d))
        if n == 5:
            self.wait()
            for k, (at, rows, axes) in enumerate(self.sets):
                here = self.mine() + at + self.where[axes[0]] * (rows // 4)
                spot = pl.ds(pl.multiple_of(here, 16), rows // 4)
                for d in range(1, 4):
                    self.copy(self.out.at[spot], self.out.at[spot], 37 + k * 3 + d - 1, self.peer(axes[0], d))
        if n == 6:
            self.wait()
            spot = pl.ds(self.mine(), self.half)
            self.copy(self.out.at[spot], self.out.at[spot], 46, self.other())
        if n == 7:
            self.wait()


class SmallJob(Job):
    def __init__(self, refs, sems, where):
        self.src, self.out, self.r0, self.a, self.r1, self.c4 = refs
        self.send, self.recv = sems
        self.half = self.src.shape[0] // 2
        self.where = where
        self.live = []

    def plane(self):
        x, y, z, core = self.where
        me = x * 4 + z
        for d in range(1, 16):
            to = (me + d) % 16
            yield d, me, to, device(to // 4, y, to % 4, core)

    def stage(self, n):
        x, y, z, core = self.where
        me = x * 4 + z
        if n == 0:
            Job.stage(self, 0)
        if n == 1:
            self.wait()
            total = self.src[pl.ds(self.mine(), self.half), :].astype(F32) + self.r0[...].astype(F32)
            self.a[...] = total.astype(BF16)
            self.r1[me] = self.a[pl.ds(pl.multiple_of(me * 16, 16), 16), :]
            for d, me, to, dev in self.plane():
                self.copy(self.a.at[pl.ds(pl.multiple_of(to * 16, 16), 16)], self.r1.at[me], d, dev)
        if n == 2:
            self.wait()
            total = self.r1[0].astype(F32)
            for k in range(1, 16):
                total = total + self.r1[k].astype(F32)
            self.c4[y] = total.astype(BF16)
            for d in range(1, 4):
                self.copy(self.c4.at[y], self.c4.at[y], 15 + d, device(x, (y + d) % 4, z, core))
        if n == 3:
            self.wait()
            total = self.c4[0].astype(F32)
            for k in range(1, 4):
                total = total + self.c4[k].astype(F32)
            spot = pl.ds(pl.multiple_of(self.mine() + me * 16, 16), 16)
            self.out[spot, :] = total.astype(BF16)
            for d, me, to, dev in self.plane():
                self.copy(self.out.at[spot], self.out.at[spot], 18 + d, dev)
        if n == 4:
            Job.stage(self, 6)
        if n == 5:
            self.wait()


UNITS = {8192: (6, 5, 5), 3072: (2, 2, 2), 2048: (2, 1, 1)}


def small_scratch():
    half = SROWS // 2
    return [
        pltpu.VMEM((half, 128), BF16),
        pltpu.VMEM((half, 128), BF16),
        pltpu.VMEM((16, 16, 128), BF16),
        pltpu.VMEM((4, 16, 128), BF16),
        pltpu.SemaphoreType.DMA((47,)),
        pltpu.SemaphoreType.DMA((47,)),
    ]


def job_scratch(rows):
    half = rows // 2
    return [
        pltpu.VMEM((half, 128), BF16),
        pltpu.VMEM((3, half // 4, 128), BF16),
        pltpu.VMEM((half // 4, 128), BF16),
        pltpu.VMEM((3, half // 16, 128), BF16),
        pltpu.VMEM((4, half // 16, 128), BF16),
        pltpu.SemaphoreType.DMA((47,)),
        pltpu.SemaphoreType.DMA((47,)),
    ]


def all_peers(where):
    x, y, z, core = where
    to = [device(x, y, z, 1 - core)]
    for axis in range(3):
        for d in range(1, 4):
            at = list(where)
            at[axis] = (at[axis] + d) % 4
            to.append(device(*at))
    for dx in range(1, 4):
        for dz in range(1, 4):
            to.append(device((x + dx) % 4, y, (z + dz) % 4, core))
    return to


def kernel(
    tok_ref, cot_hbm, reg_ref, gain1, gain2, wqkv1_hbm, wqkv2_hbm, wo1_hbm, wo2_hbm, tab1, tab2, rel_ref,
    mixed_ref, gt_ref, out2, out_a, out_b, out_o, os,
    cot_ref, wqkv1, wqkv2, wo1, wo2, g2, ga, gb, go, in_sems, out_sems,
    quad, packed, highs, lows, step1, step2, bias, p1, pt1, c1, a1, p2, pt2, c2,
    dc, dct, dq, dkvt, pen, ds1, ds2, their_ds1, their_ds2, ds1_out, ds2_out, y, z, dz, dy,
    small, g_gain1, g_gain2, sums,
    send_on, recv_on, send_back, recv_back, pair_send, pair_recv, *job_mem,
):
    where = place()
    core = where[3]
    barrier = pltpu.get_barrier_semaphore()
    peers = all_peers(where) + [near(by, m[2], m[3]) for by in (-1, 1) for m in MOVES]
    for dev in peers:
        pl.semaphore_signal(barrier, inc=1, device_id=dev, device_id_type=MESH)
    brought = []
    for n, (src, dst) in enumerate(
        ((wqkv1_hbm, wqkv1), (wo1_hbm, wo1), (cot_hbm, cot_ref), (wo2_hbm, wo2), (wqkv2_hbm, wqkv2))
    ):
        brought.append(pltpu.make_async_copy(src, dst, in_sems.at[n]))
        brought[-1].start()
    jobs = []
    for n, ref in enumerate((g2, ga, gb, go)):
        held = job_mem[n * 7 : n * 7 + 7]
        jobs.append(Job(UNITS[ref.shape[0]], (ref, ref) + held[:5], held[5:], where))
    sum2, sum_a, sum_b, sum_o = (job.stage for job in jobs)
    held = job_mem[28:]
    sum_s = SmallJob((small, os) + held[:4], held[4:], where).stage

    def to_pair(n, src, dst):
        copy = pltpu.make_async_remote_copy(
            src_ref=src, dst_ref=dst, send_sem=pair_send.at[n], recv_sem=pair_recv.at[n],
            device_id=device(*where[:3], 1 - core), device_id_type=MESH,
        )
        copy.start()
        return copy

    written = []

    def write(n, src, dst):
        written.append(pltpu.make_async_copy(src, dst, out_sems.at[n]))
        written[-1].start()

    def ds_to_pair(n, ds, out, dst):
        @pl.loop(0, 18)
        def _(r):
            out[pl.ds(r * 8, 8)] = ds[pl.ds(theirs + r * 8, 8)].astype(BF16)

        return to_pair(n, out, dst)

    mine = pl.multiple_of(core * 144, 16)
    theirs = pl.multiple_of((1 - core) * 144, 16)
    first = core * 18

    pack_tables(tab1, tab2, packed, step1, step2)
    index_in_quads(rel_ref, highs, lows)
    pl.semaphore_wait(barrier, len(peers))
    sent = []
    for part in range(3):
        gather_bias(packed, highs, lows, bias, first + part * 6, 6)
        rows = pl.ds(pl.multiple_of(mine + part * 48, 16), 48)
        sent.append(to_pair(part, bias.at[:, rows], bias.at[:, rows]))

    for copy in brought[:2]:
        copy.wait()
    into_quads(tok_ref, quad)
    x = quad[...]
    xh, _ = norm(x)
    project((xh * gain1[...]).astype(BF16), wqkv1, p1, pt1)
    for copy in sent:
        copy.wait()
    over_heads(p1, pt1, forward=(bias, step1, True, None, c1, a1))
    put_quads((x + dot(c1[...], wo1[...])).astype(BF16), y)

    on = shift(-1, y, z, send_on, recv_on)
    for copy in brought[2:]:
        copy.wait()
    into_quads(cot_ref, quad)
    ef = quad[...]
    e = ef.astype(BF16)
    context_grad(e, wo2, dc, dct)
    split = reg_ref[0, 0, 0] != reg_ref[11, 0, 0]
    lower_row = lax.broadcasted_iota(I32, (WT, WT), 0) >= 144
    lower_col = lax.broadcasted_iota(I32, (WT, WT), 1) >= 144
    pen[...] = jnp.where((lower_row != lower_col) & split, -1e30, 0.0)
    clear_pad(ds1)
    clear_pad(ds2)
    sums[...] = jnp.zeros_like(sums)
    for copy in on:
        copy.wait()

    x = get_quads(z)
    xh, rstd = norm(x)
    h = (xh * gain2[...]).astype(BF16)
    project(h, wqkv2, p2, pt2)
    over_heads(p2, pt2, (bias, step2, False, pen, c2, None), (dc, dct, None, ds2, dq, dkvt))
    put_quads(input_grad(xh, rstd, gain2[...], ef, dq, dkvt, wqkv2, g_gain2).astype(BF16), dz)
    back = shift(1, dz, dy, send_back, recv_back)
    qkv_grads(h, h.T, dq, dkvt, g2, 0, 4)
    put_columns(dot_tn(c2[...], e), g2, 12)
    sum2(0)
    quad[...] = x + dot(c2[...], wo2[...])
    out_of_quads(quad, mixed_ref)
    ds_sent = [ds_to_pair(3, ds2, ds2_out, their_ds2)]

    into_quads(tok_ref, quad)
    xh, rstd = norm(quad[...])
    h = (xh * gain1[...]).astype(BF16)
    ht = h.T
    sum2(1)
    for copy in back:
        copy.wait()
    ef = get_quads(dy)
    e = ef.astype(BF16)
    put_columns(dot_tn(c1[...], e), go, 0)
    sum_o(0)
    context_grad(e, wo1, dc, dct)
    over_heads(p1, pt1, None, (dc, dct, a1, ds1, dq, dkvt), (0, 2))
    sum_o(1)
    qkv_grads(h, ht, dq, dkvt, ga, 0, 2)
    sum_a(0)
    over_heads(p1, pt1, None, (dc, dct, a1, ds1, dq, dkvt), (2, 4))
    ds_sent.append(ds_to_pair(4, ds1, ds1_out, their_ds1))
    sum2(2)
    sum_a(1)
    qkv_grads(h, ht, dq, dkvt, gb, 2, 4)
    sum_b(0)
    quad[...] = input_grad(xh, rstd, gain1[...], ef, dq, dkvt, wqkv1, g_gain1)
    sum_o(2)
    for copy in ds_sent:
        copy.wait()
    sum_b(1)

    blocks = ((ds1, their_ds1), (ds2, their_ds2))
    between = (
        ((sum2, 3), (sum_a, 2)),
        ((sum_o, 3), (sum_b, 2), (sum2, 4)),
        ((sum_a, 3), (sum_b, 3)),
        ((sum2, 5), (sum_o, 4), (sum_a, 4)),
        ((sum_b, 4), (sum_o, 5), (sum_a, 5)),
        ((sum_b, 5),),
    )
    for part, steps in enumerate(between):
        table_grads(blocks, highs, lows, sums, first, part * 3, part * 3 + 3)
        for step, n in steps:
            step(n)
    small[:224, :] = sums[:, :128].astype(BF16)
    small[224:448, :] = sums[:, 128:].astype(BF16)
    gains = [g[:, n * 128 : (n + 1) * 128] for g in (g_gain1, g_gain2) for n in range(4)]
    gains.append(jnp.zeros((SROWS - 456, 128), F32))
    small[448:, :] = jnp.concatenate(gains, 0).astype(BF16)
    sum_s(0)
    sum2(6)
    sum_s(1)
    out_of_quads(quad, gt_ref)
    sum_o(6)
    sum_a(6)
    sum_s(2)
    sum_b(6)
    sum2(7)
    write(0, g2, out2)
    sum_o(7)
    write(1, go, out_o)
    sum_s(3)
    sum_a(7)
    write(2, ga, out_a)
    sum_b(7)
    write(3, gb, out_b)
    sum_s(4)
    sum_s(5)
    for copy in written:
        copy.wait()


def widen_kernel(s2, sa, sb, so, small, gq1, gq2, gp1, gp2, gg1, gg2, gt1, gt2, m2, ma, mb, mo, wide, in_sems, out_sems):
    ins = [pltpu.make_async_copy(so, mo, in_sems.at[0])]
    ins += [pltpu.make_async_copy(s2.at[pl.ds(k * 4, 4)], m2.at[pl.ds(k * 4, 4)], in_sems.at[1 + k]) for k in range(4)]
    ins += [pltpu.make_async_copy(sa, ma, in_sems.at[5]), pltpu.make_async_copy(sb, mb, in_sems.at[6])]
    for copy in ins:
        copy.start()

    def slab(dst, k):
        return dst.at[:, pl.ds(k * D, D)]

    plan = [(mo, 0, gp1, 1)] + [(m2, k * 4, slab(gq2, k), 1) for k in range(3)] + [(m2, 12, gp2, 1)]
    plan += [(None, k, slab(gq1, k), 2 if k == 0 else 0) for k in range(3)]
    outs = []
    waits = iter(ins)
    for n, (src, at, dst, arrivals) in enumerate(plan):
        for _ in range(arrivals):
            next(waits).wait()
        for c in range(4):
            block = src[at + c] if src is not None else (ma if c < 2 else mb)[at * 2 + c % 2]
            wide[n, :, c * 128 : (c + 1) * 128] = block.astype(F32)
        outs.append(pltpu.make_async_copy(wide.at[n], dst, out_sems.at[n]))
        outs[-1].start()
    tail = small[448:464, :].astype(F32)
    for b, (gg, gt) in enumerate(((gg1, gt1), (gg2, gt2))):
        for n in range(4):
            gg[:, n * 128 : (n + 1) * 128] = tail[b * 4 + n : b * 4 + n + 1]
        for k in range(CHUNKS):
            at = (b * HIGHS + k // 2) * 16 + (k % 2) * 224
            width = min(128, NB - k * 128)
            gt[:, k * 128 : k * 128 + width] = small[at : at + 16, :width].astype(F32)
    for copy in outs:
        copy.wait()


def on_device(
    tokens, cotangent, gain_first, gain_second, qkv_first, qkv_second, proj_first, proj_second,
    table_first, table_second, rel_index, regions,
):
    def arr(shape, dtype=BF16):
        return jax.ShapeDtypeStruct(shape, dtype)

    def mem(*shape, dtype=BF16):
        return pltpu.VMEM(shape, dtype)

    grid = arr((12, 12, 2, D))
    rows = (8192, 3072, 3072, 2048)
    hbm = pl.BlockSpec(memory_space=pl.ANY)
    weights = [mem(D, 3 * D), mem(D, 3 * D), mem(D, D), mem(D, D)]
    three = pltpu.SemaphoreType.DMA((3,))
    six = pltpu.SemaphoreType.DMA((6,))
    mixed, grad_tokens, s2, sa, sb, so, small = pl.pallas_call(
        kernel,
        out_shape=[grid, grid] + [arr((n, 128)) for n in rows] + [arr((SROWS, 128))],
        in_specs=[VM, hbm, SM, VM, VM] + [hbm] * 4 + [VM] * 3,
        out_specs=[VM, VM] + [hbm] * 4 + [VM],
        scratch_shapes=[mem(12, 12, 2, D)] + weights + [mem(n, 128) for n in rows] + [six, six]
        + [
            mem(WT, D, dtype=F32), mem(HEADS, CHUNKS * 128, dtype=I32),
            mem(WT, PADW, dtype=I32), mem(WT, PADW, dtype=I32), mem(HEADS, 128, dtype=F32), mem(HEADS, 128, dtype=F32),
            mem(HEADS, WT, PADW, dtype=I32),
            mem(WT, 3 * D), mem(3 * D, WT), mem(WT, D), mem(HEADS, WT, WT),
            mem(WT, 3 * D), mem(3 * D, WT), mem(WT, D),
            mem(WT, D), mem(D, WT), mem(WT, D), mem(2 * D, WT), mem(WT, WT, dtype=F32),
            mem(WT, HEADS, PADW, dtype=F32), mem(WT, HEADS, PADW, dtype=F32),
            mem(144, HEADS, PADW), mem(144, HEADS, PADW), mem(144, HEADS, PADW), mem(144, HEADS, PADW),
        ]
        + [mem(4, QPAD, D)] * 4
        + [mem(SROWS, 128), mem(1, D, dtype=F32), mem(1, D, dtype=F32), mem(224, 256, dtype=F32)]
        + [three] * 4 + [six] * 2
        + [ref for n in rows for ref in job_scratch(n)] + small_scratch(),
        compiler_params=pltpu.CompilerParams(vmem_limit_bytes=62 << 20, collective_id=3, has_side_effects=True),
        name="window_pair",
    )(
        tokens.transpose(1, 2, 0, 3), cotangent.transpose(1, 2, 0, 3), regions.transpose(1, 0, 2),
        gain_first.reshape(1, D), gain_second.reshape(1, D), qkv_first, qkv_second,
        proj_first, proj_second, table_first, table_second, rel_index,
    )

    gq1, gq2, gp1, gp2, gg1, gg2, gt1, gt2 = pl.pallas_call(
        widen_kernel,
        out_shape=[
            arr((D, 3 * D), F32), arr((D, 3 * D), F32), arr((D, D), F32), arr((D, D), F32),
            arr((1, D), F32), arr((1, D), F32), arr((HEADS, NB), F32), arr((HEADS, NB), F32),
        ],
        in_specs=[hbm] * 4 + [VM],
        out_specs=[hbm] * 4 + [VM] * 4,
        scratch_shapes=[
            mem(16, D, 128), mem(6, D, 128), mem(6, D, 128), mem(4, D, 128), mem(8, D, D, dtype=F32),
            pltpu.SemaphoreType.DMA((7,)), pltpu.SemaphoreType.DMA((8,)),
        ],
        compiler_params=PARAMS,
        name="widen_grads",
    )(s2.reshape(16, D, 128), sa.reshape(6, D, 128), sb.reshape(6, D, 128), so.reshape(4, D, 128), small)
    mixed, grad_tokens = mixed.transpose(2, 0, 1, 3), grad_tokens.transpose(2, 0, 1, 3)
    return mixed, grad_tokens, gg1.reshape(D), gg2.reshape(D), gq1, gq2, gp1, gp2, gt1, gt2


def solution(mesh):
    grid = P(None, "lat", "lon", None)
    return jax.shard_map(
        on_device,
        mesh=mesh,
        in_specs=(grid, grid) + (P(),) * 9 + (P(None, "lat", "lon"),),
        out_specs=(grid, grid) + (P(),) * 8,
        check_vma=False,
    )
```

```python
import jax
import jax.numpy as jnp
from jax import lax
from jax.experimental import pallas as pl
from jax.experimental.pallas import tpu as pltpu
from jax.sharding import PartitionSpec as P

F32, BF16, I32 = jnp.float32, jnp.bfloat16, jnp.int32
MESH = pl.DeviceIdType.MESH
D, HEADS, DEPTH, WT, NB = 512, 16, 32, 288, 1587
QUAD, QPAD = 72, 80
PADW, CHUNKS, HIGHS = 384, 13, 7
EPS = 1e-05
LOG2E = 1.4426950408889634
SCALE = DEPTH**-0.5
GROWS, SROWS = 8192, 512
VM = pl.BlockSpec(memory_space=pltpu.VMEM)
SM = pl.BlockSpec(memory_space=pltpu.SMEM)
PARAMS = pltpu.CompilerParams(vmem_limit_bytes=60 << 20)


def quad_row(row, col_half):
    return row // 6 * 144 + col_half * 72 + row % 6 * 12


def dot(a, b):
    return jnp.dot(a, b, preferred_element_type=F32)


def dot_nt(a, b):
    return lax.dot_general(a, b, (((1,), (1,)), ((), ())), preferred_element_type=F32)


def dot_tn(a, b):
    return lax.dot_general(a, b, (((0,), (0,)), ((), ())), preferred_element_type=F32)


def into_quads(src, dst):
    for r in range(12):
        v = src[r].astype(F32).reshape(24, D)
        for ch in range(2):
            dst[pl.ds(quad_row(r, ch), 12), :] = v[ch * 12 : ch * 12 + 12]


def out_of_quads(src, dst):
    for r in range(12):
        both = [src[pl.ds(quad_row(r, ch), 12), :] for ch in range(2)]
        dst[r] = jnp.concatenate(both, 0).reshape(12, 2, D).astype(BF16)


def put_quads(value, dst):
    for q in range(4):
        dst[q, :QUAD, :] = value[q * QUAD : (q + 1) * QUAD]
        dst[q, QUAD:, :] = jnp.zeros((QPAD - QUAD, D), dst.dtype)


def get_quads(src):
    return jnp.concatenate([src[q, :QUAD, :].astype(F32) for q in range(4)], 0)


def norm(x):
    xc = x - jnp.mean(x, -1, keepdims=True)
    rstd = lax.rsqrt(jnp.mean(xc * xc, -1, keepdims=True) + EPS)
    return xc * rstd, rstd


def project(h, w_ref, p, pt):
    for n in range(3):
        cols = slice(n * D, n * D + D)
        v = dot(h, w_ref[:, cols])
        p[:, cols] = v.astype(BF16)
        pt[cols, :] = v.T.astype(BF16)


def index_in_quads(rel_ref, highs, lows):
    at = lax.broadcasted_iota(I32, (WT, WT), 0)
    half = (at >= 144).astype(I32)
    rest = at - 144 * half
    col = (rest >= 72).astype(I32)
    rest = rest - 72 * col
    row = sum((rest >= 12 * k).astype(I32) for k in range(1, 6))
    rest = rest - 12 * row
    natural = (rest & 1) * 144 + (half * 6 + row) * 12 + col * 6 + (rest >> 1)
    perm = (natural == lax.broadcasted_iota(I32, (WT, WT), 1)).astype(F32).astype(BF16)
    rel = rel_ref[...]
    high = (rel >> 8).astype(F32).astype(BF16)
    low = (rel & 255).astype(F32).astype(BF16)

    def moved(part):
        return dot_nt(dot(perm, part).astype(BF16), perm)

    high, low = moved(high), moved(low)
    highs[:, PADW - 128 :] = jnp.zeros((WT, 128), I32)
    lows[:, PADW - 128 :] = jnp.zeros((WT, 128), I32)
    highs[:, :WT] = high.astype(I32)
    lows[:, :WT] = low.astype(I32)


def pack_tables(first_ref, second_ref, packed, step_first, step_second):
    parts = []
    for ref, step_ref in ((first_ref, step_first), (second_ref, step_second)):
        t = ref[...]
        least = jnp.min(t, -1, keepdims=True)
        span = jnp.maximum(jnp.max(t, -1, keepdims=True) - least, 1e-20)
        parts.append(jnp.clip(jnp.floor((t - least) * (65535.0 / span) + 0.5), 0.0, 65535.0).astype(I32))
        step_ref[...] = jnp.broadcast_to(span * (LOG2E / 65535.0), (HEADS, 128))
    packed[:, (CHUNKS - 1) * 128 :] = jnp.zeros((HEADS, 128), I32)
    packed[:, :NB] = (parts[0] << 16) | parts[1]


def gather_bias(packed, highs, lows, bias, start, count):
    @pl.loop(start, start + count)
    def _(r):
        rows = pl.ds(pl.multiple_of(r * 8, 8), 8)
        for ct in range(3):
            lanes = pl.ds(ct * 128, 128)
            high, low = highs[rows, lanes], lows[rows, lanes]
            chunk = high * 2 + (low >> 7)
            lane = low & 127
            masks = [chunk == c for c in range(CHUNKS)]
            for h in range(HEADS):
                acc = None
                for c in range(CHUNKS):
                    row = jnp.broadcast_to(packed[h : h + 1, c * 128 : (c + 1) * 128], (8, 128))
                    found = jnp.take_along_axis(row, lane, axis=1)
                    acc = found if acc is None else jnp.where(masks[c], found, acc)
                bias[h, rows, lanes] = acc


def over_heads(p, pt, forward=None, backward=None, groups=(0, 4), wide=2):
    lanes = lax.broadcasted_iota(I32, (WT, 128), 1) // DEPTH

    @pl.loop(*groups)
    def _(g):
        g0 = pl.multiple_of(g * 128, 128)
        qg = p[:, pl.ds(g0, 128)]
        kg = p[:, pl.ds(D + g0, 128)]
        vg = p[:, pl.ds(2 * D + g0, 128)]
        ktg = pt[pl.ds(D + g0, 128), :]
        vtg = pt[pl.ds(2 * D + g0, 128), :]
        zero = jnp.zeros_like(qg)
        c_acc = q_acc = None
        if backward is not None:
            dc, dct, a_in, ds_out, dq, dkvt = backward
            dcg = dc[:, pl.ds(g0, 128)]
        for start in range(0, 4, wide):
            some = range(start, start + wide)
            heads = [g * 4 + hh for hh in some]
            spans = [pl.ds(pl.multiple_of(g0 + hh * DEPTH, DEPTH), DEPTH) for hh in some]
            if forward is not None:
                bias, steps, high, pen, c, a_out = forward
                s = [dot(jnp.where(lanes == hh, qg, zero), ktg) for hh in some]
            if backward is not None:
                da = [dot(jnp.where(lanes == hh, dcg, zero), vtg) for hh in some]
            if forward is not None:
                for k, h in enumerate(heads):
                    packed = bias[h, :, :WT]
                    entry = lax.shift_right_logical(packed, 16) if high else packed & 0xFFFF
                    s[k] = s[k] * (SCALE * LOG2E) + entry.astype(F32) * steps[pl.ds(h, 1), 0:1]
                    if pen is not None:
                        s[k] = s[k] + pen[...]
                most = [jnp.max(v, -1, keepdims=True) for v in s]
                expo = [jnp.exp2(v - m) for v, m in zip(s, most)]
                total = [1.0 / jnp.sum(v, -1, keepdims=True) for v in expo]
                a32 = [v * r for v, r in zip(expo, total)]
                a = [v.astype(BF16) for v in a32]
            else:
                a = [a_in[h] for h in heads]
                a32 = [v.astype(F32) for v in a]
            if backward is not None:
                mean = [jnp.sum(v * w, -1, keepdims=True) for v, w in zip(a32, da)]
                ds = [v * (w - m) for v, w, m in zip(a32, da, mean)]
                dsb = [v.astype(BF16) for v in ds]
            if forward is not None:
                ctx = [dot(v, vg) for v in a]
            if backward is not None:
                dqh = [dot(v, kg) for v in dsb]
                dk = [dot(pt[span, :], v) * SCALE for span, v in zip(spans, dsb)]
                dv = [dot(dct[span, :], v) for span, v in zip(spans, a)]
            for k, hh in enumerate(some):
                own = lanes == hh
                if forward is not None:
                    c_acc = ctx[k] if c_acc is None else jnp.where(own, ctx[k], c_acc)
                    if a_out is not None:
                        a_out[heads[k]] = a[k]
                if backward is not None:
                    q_acc = dqh[k] if q_acc is None else jnp.where(own, dqh[k], q_acc)
                    ds_out[:, heads[k], :WT] = ds[k]
                    at = pl.multiple_of(g0 + hh * DEPTH, DEPTH)
                    dkvt[pl.ds(at, DEPTH), :] = dk[k].astype(BF16)
                    dkvt[pl.ds(D + at, DEPTH), :] = dv[k].astype(BF16)
        if forward is not None:
            c[:, pl.ds(g0, 128)] = c_acc.astype(BF16)
        if backward is not None:
            dq[:, pl.ds(g0, 128)] = (q_acc * SCALE).astype(BF16)


def table_grads(blocks, highs, lows, out, first, start, stop):
    low_of = lax.broadcasted_iota(I32, (256, PADW), 0).astype(F32).astype(BF16)
    one, nil = jnp.ones((256, PADW), BF16), jnp.zeros((256, PADW), BF16)

    @pl.loop(first + start, first + stop)
    def _(r):
        rows = pl.ds(pl.multiple_of(r * 8, 8), 8)
        high8 = highs[rows, :].astype(F32).astype(BF16)
        low8 = lows[rows, :].astype(F32).astype(BF16)
        for part in range(2):
            left, right = [], []
            for i in range(part * 4, part * 4 + 4):
                high = jnp.broadcast_to(high8[i : i + 1], (HEADS, PADW))
                low = jnp.broadcast_to(low8[i : i + 1], (256, PADW))
                picked = []
                for block, theirs in blocks:
                    ds = (block[r * 8 + i] + theirs[(r - first) * 8 + i].astype(F32)).astype(BF16)
                    picked += [jnp.where(high == jnp.array(k, BF16), ds, jnp.zeros_like(ds)) for k in range(HIGHS)]
                left.append(jnp.concatenate(picked, 0))
                right.append(jnp.where(low == low_of, one, nil))
            out[...] += dot_nt(jnp.concatenate(left, 1), jnp.concatenate(right, 1))


def put_columns(value, dst, first):
    for n in range(value.shape[1] // 128):
        at = (first + n) * D
        dst[at : at + D, :] = value[:, n * 128 : (n + 1) * 128].astype(BF16)


def qkv_grads(h, ht, dq, dkvt, grads, first, last):
    cols = slice(first * 128, last * 128)
    put_columns(dot_tn(h, dq[:, cols]), grads, 0)
    put_columns(dot_nt(ht, dkvt[cols, :]), grads, last - first)
    put_columns(dot_nt(ht, dkvt[D + first * 128 : D + last * 128, :]), grads, 2 * (last - first))


def input_grad(xh, rstd, gain, ef, dq, dkvt, wqkv, g_gain):
    dh = dot_nt(dq[...], wqkv[:, :D]) + dot(wqkv[:, D:], dkvt[...]).T
    dh = dh.astype(BF16).astype(F32)
    g_gain[...] = jnp.sum(dh * xh, 0, keepdims=True)
    dxh = dh * gain
    return rstd * (dxh - jnp.mean(dxh, -1, keepdims=True) - xh * jnp.mean(dxh * xh, -1, keepdims=True)) + ef


def clear_pad(ds):
    ds[:, :, PADW - 128 :] = jnp.zeros((WT, HEADS, 128), F32)


def context_grad(e, wo, dc, dct):
    v = dot_nt(e, wo[...])
    dc[...] = v.astype(BF16)
    dct[...] = v.T.astype(BF16)


def place():
    lon, lat = lax.axis_index("lon"), lax.axis_index("lat")
    x, z, y = lon // 8, (lon // 2) % 4, (lon % 2) * 2 + lat // 2
    return x, y, z, lat % 2


def device(x, y, z, core):
    return {"lon": x * 8 + z * 2 + y // 2, "lat": (y % 2) * 2 + core}


def near(step, along_lon, along_lat):
    return {
        "lon": (lax.axis_index("lon") + step * along_lon + 32) % 32,
        "lat": (lax.axis_index("lat") + step * along_lat + 4) % 4,
    }


MOVES = ((2, 1, 1, 0), (1, 2, 0, 1), (0, 3, 1, 1))


def shift(by, src, dst, send, recv):
    copies = []
    for n, (here, there, along_lon, along_lat) in enumerate(MOVES):
        a, b = (here, there) if by < 0 else (there, here)
        copies.append(
            pltpu.make_async_remote_copy(
                src_ref=src.at[a], dst_ref=dst.at[b], send_sem=send.at[n], recv_sem=recv.at[n],
                device_id=near(by, along_lon, along_lat), device_id_type=MESH,
            )
        )
        copies[-1].start()
    a, b = (3, 0) if by < 0 else (0, 3)
    dst[b] = src[a]
    return copies


class Job:
    def __init__(self, units, refs, sems, where):
        self.src, self.out, self.r0, self.r1, self.b, self.r2, self.c4 = refs
        self.a = self.r0
        self.send, self.recv = sems
        self.half = self.src.shape[0] // 2
        self.where = where
        self.sets = []
        at = 0
        for n, count in enumerate(units):
            self.sets.append((at, count * 256, (n % 3, (n + 1) % 3, (n + 2) % 3)))
            at += count * 256
        self.live = []

    def peer(self, axis, d):
        to = list(self.where)
        to[axis] = (to[axis] + d) % 4
        return device(*to)

    def copy(self, src, dst, sem, to):
        made = pltpu.make_async_remote_copy(
            src_ref=src, dst_ref=dst, send_sem=self.send.at[sem], recv_sem=self.recv.at[sem],
            device_id=to, device_id_type=MESH,
        )
        made.start()
        self.live.append(made)

    def wait(self):
        for made in self.live:
            made.wait()
        self.live = []

    def other(self):
        x, y, z, core = self.where
        return device(x, y, z, 1 - core)

    def mine(self):
        return pl.multiple_of(self.where[3] * self.half, 128)

    def add(self, dst, dst_at, parts, rows):
        step = 256 if rows % 256 == 0 else rows

        @pl.loop(0, rows // step)
        def _(n):
            total = None
            for ref, lead, at in parts:
                where = pl.ds(pl.multiple_of(at + n * step, 16), step)
                v = (ref[where, :] if lead is None else ref[lead, where, :]).astype(F32)
                total = v if total is None else total + v
            dst[pl.ds(pl.multiple_of(dst_at + n * step, 16), step), :] = total.astype(BF16)

    def stage(self, n):
        if n == 0:
            theirs = pl.multiple_of((1 - self.where[3]) * self.half, 128)
            self.copy(self.src.at[pl.ds(theirs, self.half)], self.r0, 0, self.other())
        if n == 1:
            self.wait()
            self.add(self.a, 0, [(self.src, None, self.mine()), (self.r0, None, 0)], self.half)
            for k, (at, rows, axes) in enumerate(self.sets):
                me = self.where[axes[0]]
                for d in range(1, 4):
                    piece = pl.multiple_of(at + (me + d) % 4 * (rows // 4), 16)
                    self.copy(
                        self.a.at[pl.ds(piece, rows // 4)], self.r1.at[d - 1, pl.ds(at // 4, rows // 4)],
                        1 + k * 3 + d - 1, self.peer(axes[0], d),
                    )
        if n == 2:
            self.wait()
            for k, (at, rows, axes) in enumerate(self.sets):
                own = at + self.where[axes[0]] * (rows // 4)
                self.add(
                    self.b, at // 4, [(self.a, None, own)] + [(self.r1, d, at // 4) for d in range(3)], rows // 4
                )
                me = self.where[axes[1]]
                for d in range(1, 4):
                    piece = pl.multiple_of(at // 4 + (me + d) % 4 * (rows // 16), 16)
                    self.copy(
                        self.b.at[pl.ds(piece, rows // 16)], self.r2.at[d - 1, pl.ds(at // 16, rows // 16)],
                        10 + k * 3 + d - 1, self.peer(axes[1], d),
                    )
        if n == 3:
            self.wait()
            for k, (at, rows, axes) in enumerate(self.sets):
                own = at // 4 + self.where[axes[1]] * (rows // 16)
                me = self.where[axes[2]]
                small = pl.ds(at // 16, rows // 16)
                total = self.b[pl.ds(pl.multiple_of(own, 16), rows // 16), :].astype(F32)
                for d in range(3):
                    total = total + self.r2[d, small, :].astype(F32)
                self.c4[me, small, :] = total.astype(BF16)
                for d in range(1, 4):
                    self.copy(
                        self.c4.at[me, small], self.c4.at[me, small],
                        19 + k * 3 + d - 1, self.peer(axes[2], d),
                    )
        if n == 4:
            self.wait()
            for k, (at, rows, axes) in enumerate(self.sets):
                small = pl.ds(at // 16, rows // 16)
                total = self.c4[0, small, :].astype(F32)
                for d in range(1, 4):
                    total = total + self.c4[d, small, :].astype(F32)
                here = self.mine() + at + self.where[axes[0]] * (rows // 4) + self.where[axes[1]] * (rows // 16)
                spot = pl.ds(pl.multiple_of(here, 16), rows // 16)
                self.out[spot, :] = total.astype(BF16)
                for d in range(1, 4):
                    self.copy(self.out.at[spot], self.out.at[spot], 28 + k * 3 + d - 1, self.peer(axes[1], d))
        if n == 5:
            self.wait()
            for k, (at, rows, axes) in enumerate(self.sets):
                here = self.mine() + at + self.where[axes[0]] * (rows // 4)
                spot = pl.ds(pl.multiple_of(here, 16), rows // 4)
                for d in range(1, 4):
                    self.copy(self.out.at[spot], self.out.at[spot], 37 + k * 3 + d - 1, self.peer(axes[0], d))
        if n == 6:
            self.wait()
            spot = pl.ds(self.mine(), self.half)
            self.copy(self.out.at[spot], self.out.at[spot], 46, self.other())
        if n == 7:
            self.wait()


class SmallJob(Job):
    def __init__(self, refs, sems, where):
        self.src, self.out, self.r0, self.a, self.r1, self.c4 = refs
        self.send, self.recv = sems
        self.half = self.src.shape[0] // 2
        self.where = where
        self.live = []

    def plane(self):
        x, y, z, core = self.where
        me = x * 4 + z
        for d in range(1, 16):
            to = (me + d) % 16
            yield d, me, to, device(to // 4, y, to % 4, core)

    def stage(self, n):
        x, y, z, core = self.where
        me = x * 4 + z
        if n == 0:
            Job.stage(self, 0)
        if n == 1:
            self.wait()
            total = self.src[pl.ds(self.mine(), self.half), :].astype(F32) + self.r0[...].astype(F32)
            self.a[...] = total.astype(BF16)
            self.r1[me] = self.a[pl.ds(pl.multiple_of(me * 16, 16), 16), :]
            for d, me, to, dev in self.plane():
                self.copy(self.a.at[pl.ds(pl.multiple_of(to * 16, 16), 16)], self.r1.at[me], d, dev)
        if n == 2:
            self.wait()
            total = self.r1[0].astype(F32)
            for k in range(1, 16):
                total = total + self.r1[k].astype(F32)
            self.c4[y] = total.astype(BF16)
            for d in range(1, 4):
                self.copy(self.c4.at[y], self.c4.at[y], 15 + d, device(x, (y + d) % 4, z, core))
        if n == 3:
            self.wait()
            total = self.c4[0].astype(F32)
            for k in range(1, 4):
                total = total + self.c4[k].astype(F32)
            spot = pl.ds(pl.multiple_of(self.mine() + me * 16, 16), 16)
            self.out[spot, :] = total.astype(BF16)
            for d, me, to, dev in self.plane():
                self.copy(self.out.at[spot], self.out.at[spot], 18 + d, dev)
        if n == 4:
            Job.stage(self, 6)
        if n == 5:
            self.wait()


UNITS = {8192: (6, 5, 5), 3072: (2, 2, 2), 2048: (2, 1, 1)}


def small_scratch():
    half = SROWS // 2
    return [
        pltpu.VMEM((half, 128), BF16),
        pltpu.VMEM((half, 128), BF16),
        pltpu.VMEM((16, 16, 128), BF16),
        pltpu.VMEM((4, 16, 128), BF16),
        pltpu.SemaphoreType.DMA((47,)),
        pltpu.SemaphoreType.DMA((47,)),
    ]


def job_scratch(rows):
    half = rows // 2
    return [
        pltpu.VMEM((half, 128), BF16),
        pltpu.VMEM((3, half // 4, 128), BF16),
        pltpu.VMEM((half // 4, 128), BF16),
        pltpu.VMEM((3, half // 16, 128), BF16),
        pltpu.VMEM((4, half // 16, 128), BF16),
        pltpu.SemaphoreType.DMA((47,)),
        pltpu.SemaphoreType.DMA((47,)),
    ]


def all_peers(where):
    x, y, z, core = where
    to = [device(x, y, z, 1 - core)]
    for axis in range(3):
        for d in range(1, 4):
            at = list(where)
            at[axis] = (at[axis] + d) % 4
            to.append(device(*at))
    for dx in range(1, 4):
        for dz in range(1, 4):
            to.append(device((x + dx) % 4, y, (z + dz) % 4, core))
    return to


def kernel(
    tok_ref, cot_hbm, reg_ref, gain1, gain2, wqkv1_hbm, wqkv2_hbm, wo1_hbm, wo2_hbm, tab1, tab2, rel_ref,
    mixed_ref, gt_ref, out2, out_a, out_b, out_o, os,
    cot_ref, wqkv1, wqkv2, wo1, wo2, g2, ga, gb, go, in_sems, out_sems,
    quad, packed, highs, lows, step1, step2, bias, p1, pt1, c1, a1, p2, pt2, c2,
    dc, dct, dq, dkvt, pen, ds1, ds2, their_ds1, their_ds2, ds1_out, ds2_out, y, z, dz, dy,
    small, g_gain1, g_gain2, sums,
    send_on, recv_on, send_back, recv_back, pair_send, pair_recv, *job_mem,
):
    where = place()
    core = where[3]
    barrier = pltpu.get_barrier_semaphore()
    peers = all_peers(where) + [near(by, m[2], m[3]) for by in (-1, 1) for m in MOVES]
    for dev in peers:
        pl.semaphore_signal(barrier, inc=1, device_id=dev, device_id_type=MESH)
    brought = []
    for n, (src, dst) in enumerate(
        ((wqkv1_hbm, wqkv1), (wo1_hbm, wo1), (cot_hbm, cot_ref), (wo2_hbm, wo2), (wqkv2_hbm, wqkv2))
    ):
        brought.append(pltpu.make_async_copy(src, dst, in_sems.at[n]))
        brought[-1].start()
    jobs = []
    for n, ref in enumerate((g2, ga, gb, go)):
        held = job_mem[n * 7 : n * 7 + 7]
        jobs.append(Job(UNITS[ref.shape[0]], (ref, ref) + held[:5], held[5:], where))
    sum2, sum_a, sum_b, sum_o = (job.stage for job in jobs)
    held = job_mem[28:]
    sum_s = SmallJob((small, os) + held[:4], held[4:], where).stage

    def to_pair(n, src, dst):
        copy = pltpu.make_async_remote_copy(
            src_ref=src, dst_ref=dst, send_sem=pair_send.at[n], recv_sem=pair_recv.at[n],
            device_id=device(*where[:3], 1 - core), device_id_type=MESH,
        )
        copy.start()
        return copy

    written = []

    def write(n, src, dst):
        written.append(pltpu.make_async_copy(src, dst, out_sems.at[n]))
        written[-1].start()

    def ds_to_pair(n, ds, out, dst):
        @pl.loop(0, 18)
        def _(r):
            out[pl.ds(r * 8, 8)] = ds[pl.ds(theirs + r * 8, 8)].astype(BF16)

        return to_pair(n, out, dst)

    mine = pl.multiple_of(core * 144, 16)
    theirs = pl.multiple_of((1 - core) * 144, 16)
    first = core * 18

    pack_tables(tab1, tab2, packed, step1, step2)
    index_in_quads(rel_ref, highs, lows)
    pl.semaphore_wait(barrier, len(peers))
    sent = []
    for part in range(3):
        gather_bias(packed, highs, lows, bias, first + part * 6, 6)
        rows = pl.ds(pl.multiple_of(mine + part * 48, 16), 48)
        sent.append(to_pair(part, bias.at[:, rows], bias.at[:, rows]))

    for copy in brought[:2]:
        copy.wait()
    into_quads(tok_ref, quad)
    x = quad[...]
    xh, _ = norm(x)
    project((xh * gain1[...]).astype(BF16), wqkv1, p1, pt1)
    for copy in sent:
        copy.wait()
    over_heads(p1, pt1, forward=(bias, step1, True, None, c1, a1), wide=4)
    put_quads((x + dot(c1[...], wo1[...])).astype(BF16), y)

    on = shift(-1, y, z, send_on, recv_on)
    for copy in brought[2:]:
        copy.wait()
    into_quads(cot_ref, quad)
    ef = quad[...]
    e = ef.astype(BF16)
    context_grad(e, wo2, dc, dct)
    split = reg_ref[0, 0, 0] != reg_ref[11, 0, 0]
    lower_row = lax.broadcasted_iota(I32, (WT, WT), 0) >= 144
    lower_col = lax.broadcasted_iota(I32, (WT, WT), 1) >= 144
    pen[...] = jnp.where((lower_row != lower_col) & split, -1e30, 0.0)
    clear_pad(ds1)
    clear_pad(ds2)
    sums[...] = jnp.zeros_like(sums)
    for copy in on:
        copy.wait()

    x = get_quads(z)
    xh, rstd = norm(x)
    h = (xh * gain2[...]).astype(BF16)
    project(h, wqkv2, p2, pt2)
    over_heads(p2, pt2, (bias, step2, False, pen, c2, None), (dc, dct, None, ds2, dq, dkvt))
    put_quads(input_grad(xh, rstd, gain2[...], ef, dq, dkvt, wqkv2, g_gain2).astype(BF16), dz)
    back = shift(1, dz, dy, send_back, recv_back)
    qkv_grads(h, h.T, dq, dkvt, g2, 0, 4)
    put_columns(dot_tn(c2[...], e), g2, 12)
    sum2(0)
    quad[...] = x + dot(c2[...], wo2[...])
    out_of_quads(quad, mixed_ref)
    ds_sent = [ds_to_pair(3, ds2, ds2_out, their_ds2)]

    into_quads(tok_ref, quad)
    xh, rstd = norm(quad[...])
    h = (xh * gain1[...]).astype(BF16)
    ht = h.T
    sum2(1)
    for copy in back:
        copy.wait()
    ef = get_quads(dy)
    e = ef.astype(BF16)
    put_columns(dot_tn(c1[...], e), go, 0)
    sum_o(0)
    context_grad(e, wo1, dc, dct)
    over_heads(p1, pt1, None, (dc, dct, a1, ds1, dq, dkvt), (0, 2), 4)
    sum_o(1)
    qkv_grads(h, ht, dq, dkvt, ga, 0, 2)
    sum_a(0)
    over_heads(p1, pt1, None, (dc, dct, a1, ds1, dq, dkvt), (2, 4), 4)
    ds_sent.append(ds_to_pair(4, ds1, ds1_out, their_ds1))
    sum2(2)
    sum_a(1)
    qkv_grads(h, ht, dq, dkvt, gb, 2, 4)
    sum_b(0)
    quad[...] = input_grad(xh, rstd, gain1[...], ef, dq, dkvt, wqkv1, g_gain1)
    sum_o(2)
    for copy in ds_sent:
        copy.wait()
    sum_b(1)

    blocks = ((ds1, their_ds1), (ds2, their_ds2))
    between = (
        ((sum2, 3), (sum_a, 2)),
        ((sum_o, 3), (sum_b, 2), (sum2, 4)),
        ((sum_a, 3), (sum_b, 3)),
        ((sum2, 5), (sum_o, 4), (sum_a, 4)),
        ((sum_b, 4), (sum_o, 5), (sum_a, 5)),
        ((sum_b, 5),),
    )
    for part, steps in enumerate(between):
        table_grads(blocks, highs, lows, sums, first, part * 3, part * 3 + 3)
        for step, n in steps:
            step(n)
    small[:224, :] = sums[:, :128].astype(BF16)
    small[224:448, :] = sums[:, 128:].astype(BF16)
    gains = [g[:, n * 128 : (n + 1) * 128] for g in (g_gain1, g_gain2) for n in range(4)]
    gains.append(jnp.zeros((SROWS - 456, 128), F32))
    small[448:, :] = jnp.concatenate(gains, 0).astype(BF16)
    sum_s(0)
    sum2(6)
    sum_s(1)
    out_of_quads(quad, gt_ref)
    sum_o(6)
    sum_a(6)
    sum_s(2)
    sum_b(6)
    sum2(7)
    write(0, g2, out2)
    sum_o(7)
    write(1, go, out_o)
    sum_s(3)
    sum_a(7)
    write(2, ga, out_a)
    sum_b(7)
    write(3, gb, out_b)
    sum_s(4)
    sum_s(5)
    for copy in written:
        copy.wait()


def widen_kernel(s2, sa, sb, so, small, gq1, gq2, gp1, gp2, gg1, gg2, gt1, gt2, m2, ma, mb, mo, wide, in_sems, out_sems):
    ins = [pltpu.make_async_copy(so, mo, in_sems.at[0])]
    ins += [pltpu.make_async_copy(s2.at[pl.ds(k * 4, 4)], m2.at[pl.ds(k * 4, 4)], in_sems.at[1 + k]) for k in range(4)]
    ins += [pltpu.make_async_copy(sa, ma, in_sems.at[5]), pltpu.make_async_copy(sb, mb, in_sems.at[6])]
    for copy in ins:
        copy.start()

    def slab(dst, k):
        return dst.at[:, pl.ds(k * D, D)]

    plan = [(mo, 0, gp1, 1)] + [(m2, k * 4, slab(gq2, k), 1) for k in range(3)] + [(m2, 12, gp2, 1)]
    plan += [(None, k, slab(gq1, k), 2 if k == 0 else 0) for k in range(3)]
    outs = []
    waits = iter(ins)
    for n, (src, at, dst, arrivals) in enumerate(plan):
        for _ in range(arrivals):
            next(waits).wait()
        for c in range(4):
            block = src[at + c] if src is not None else (ma if c < 2 else mb)[at * 2 + c % 2]
            wide[n, :, c * 128 : (c + 1) * 128] = block.astype(F32)
        outs.append(pltpu.make_async_copy(wide.at[n], dst, out_sems.at[n]))
        outs[-1].start()
    tail = small[448:464, :].astype(F32)
    for b, (gg, gt) in enumerate(((gg1, gt1), (gg2, gt2))):
        for n in range(4):
            gg[:, n * 128 : (n + 1) * 128] = tail[b * 4 + n : b * 4 + n + 1]
        for k in range(CHUNKS):
            at = (b * HIGHS + k // 2) * 16 + (k % 2) * 224
            width = min(128, NB - k * 128)
            gt[:, k * 128 : k * 128 + width] = small[at : at + 16, :width].astype(F32)
    for copy in outs:
        copy.wait()


def on_device(
    tokens, cotangent, gain_first, gain_second, qkv_first, qkv_second, proj_first, proj_second,
    table_first, table_second, rel_index, regions,
):
    def arr(shape, dtype=BF16):
        return jax.ShapeDtypeStruct(shape, dtype)

    def mem(*shape, dtype=BF16):
        return pltpu.VMEM(shape, dtype)

    grid = arr((12, 12, 2, D))
    rows = (8192, 3072, 3072, 2048)
    hbm = pl.BlockSpec(memory_space=pl.ANY)
    weights = [mem(D, 3 * D), mem(D, 3 * D), mem(D, D), mem(D, D)]
    three = pltpu.SemaphoreType.DMA((3,))
    six = pltpu.SemaphoreType.DMA((6,))
    mixed, grad_tokens, s2, sa, sb, so, small = pl.pallas_call(
        kernel,
        out_shape=[grid, grid] + [arr((n, 128)) for n in rows] + [arr((SROWS, 128))],
        in_specs=[VM, hbm, SM, VM, VM] + [hbm] * 4 + [VM] * 3,
        out_specs=[VM, VM] + [hbm] * 4 + [VM],
        scratch_shapes=[mem(12, 12, 2, D)] + weights + [mem(n, 128) for n in rows] + [six, six]
        + [
            mem(WT, D, dtype=F32), mem(HEADS, CHUNKS * 128, dtype=I32),
            mem(WT, PADW, dtype=I32), mem(WT, PADW, dtype=I32), mem(HEADS, 128, dtype=F32), mem(HEADS, 128, dtype=F32),
            mem(HEADS, WT, PADW, dtype=I32),
            mem(WT, 3 * D), mem(3 * D, WT), mem(WT, D), mem(HEADS, WT, WT),
            mem(WT, 3 * D), mem(3 * D, WT), mem(WT, D),
            mem(WT, D), mem(D, WT), mem(WT, D), mem(2 * D, WT), mem(WT, WT, dtype=F32),
            mem(WT, HEADS, PADW, dtype=F32), mem(WT, HEADS, PADW, dtype=F32),
            mem(144, HEADS, PADW), mem(144, HEADS, PADW), mem(144, HEADS, PADW), mem(144, HEADS, PADW),
        ]
        + [mem(4, QPAD, D)] * 4
        + [mem(SROWS, 128), mem(1, D, dtype=F32), mem(1, D, dtype=F32), mem(224, 256, dtype=F32)]
        + [three] * 4 + [six] * 2
        + [ref for n in rows for ref in job_scratch(n)] + small_scratch(),
        compiler_params=pltpu.CompilerParams(vmem_limit_bytes=62 << 20, collective_id=3, has_side_effects=True),
        name="window_pair",
    )(
        tokens.transpose(1, 2, 0, 3), cotangent.transpose(1, 2, 0, 3), regions.transpose(1, 0, 2),
        gain_first.reshape(1, D), gain_second.reshape(1, D), qkv_first, qkv_second,
        proj_first, proj_second, table_first, table_second, rel_index,
    )

    gq1, gq2, gp1, gp2, gg1, gg2, gt1, gt2 = pl.pallas_call(
        widen_kernel,
        out_shape=[
            arr((D, 3 * D), F32), arr((D, 3 * D), F32), arr((D, D), F32), arr((D, D), F32),
            arr((1, D), F32), arr((1, D), F32), arr((HEADS, NB), F32), arr((HEADS, NB), F32),
        ],
        in_specs=[hbm] * 4 + [VM],
        out_specs=[hbm] * 4 + [VM] * 4,
        scratch_shapes=[
            mem(16, D, 128), mem(6, D, 128), mem(6, D, 128), mem(4, D, 128), mem(8, D, D, dtype=F32),
            pltpu.SemaphoreType.DMA((7,)), pltpu.SemaphoreType.DMA((8,)),
        ],
        compiler_params=PARAMS,
        name="widen_grads",
    )(s2.reshape(16, D, 128), sa.reshape(6, D, 128), sb.reshape(6, D, 128), so.reshape(4, D, 128), small)
    mixed, grad_tokens = mixed.transpose(2, 0, 1, 3), grad_tokens.transpose(2, 0, 1, 3)
    return mixed, grad_tokens, gg1.reshape(D), gg2.reshape(D), gq1, gq2, gp1, gp2, gt1, gt2


def solution(mesh):
    grid = P(None, "lat", "lon", None)
    return jax.shard_map(
        on_device,
        mesh=mesh,
        in_specs=(grid, grid) + (P(),) * 9 + (P(None, "lat", "lon"),),
        out_specs=(grid, grid) + (P(),) * 8,
        check_vma=False,
    )
```
